128 devices in a mesh: dp: 16 (over y, z), tensor: 8 (over x, core).
Axes of the slice: x: 4, y: 4, z: 4, core: 2. Of those that a mesh axis runs over, the one named last changes fastest.
Arguments:
- tokens: bfloat16 [80, 128, 3200], P('dp', 'tensor'), may hold values from -6 to 6
- norm_gain: float32 [3200], replicated, may hold values from 0.25 to 1.75
- fc1: bfloat16 [3200, 6400], P(None, 'tensor'), may hold values from -0.109375 to 0.109375
- fc2t: bfloat16 [3200, 6400], P(None, 'tensor'), may hold values from -0.078125 to 0.078125
- block_slot: int32 [80], replicated, may hold values from -1 to 31, as said below
- out_grad: bfloat16 [32, 128, 3200], P('dp', 'tensor'), may hold values from -6 to 6
Outputs:
- mixed: bfloat16 [32, 128, 3200], P('dp', 'tensor')
- tokens_grad: bfloat16 [80, 128, 3200], P('dp', 'tensor')
- fc1_grad: float32 [3200, 6400], P('dp', 'tensor')
- fc2t_grad: float32 [3200, 6400], P('dp', 'tensor')
- gain_grad: float32 [3200], replicated
The draws below stay inside these ranges and needn't reach their ends.
Inputs may be any that keep to these rules, and one draw needn't show every extreme that they name: Home block b belongs to dp index b // 5 and balanced block s to dp index s // 2. block_slot is -1 for an empty home block; every balanced block is named by exactly one home block. Home block j of dp index r, when live, names a balanced block of dp index (r + j) mod the number of dp indices. Dp index 0 has all 5 of its home blocks live, and home block 1 of the last dp index is live.
All inputs are finite; a program needn't handle non-finite values.
Results may differ from the reference program's by a relative error of at most 0.0055.
Values may be sent and summed in bfloat16 or wider, within the bound.
A program may use at most 192 MiB of HBM per device.

```python
import jax
import jax.numpy as jnp
from jax import lax

D = 3200
FF = 6400
BLOCK = 128
BAL_BLK = 2
HOME_BLK = 5
SLOTS = 32
HOMES = 80


def draw_block_slot(key, part):
    key = jax.random.fold_in(key, 7)
    rank_count = HOMES // HOME_BLK
    place_keys = jax.random.split(key, rank_count)
    shuffles = jax.vmap(lambda single: jax.random.permutation(single, HOME_BLK))(place_keys).astype(jnp.int32)
    rank_ids = jnp.arange(rank_count, dtype=jnp.int32)
    offsets = jnp.arange(HOME_BLK, dtype=jnp.int32)
    forced = (offsets[None, :] - rank_ids[:, None]) % rank_count == 0
    forced = forced | (rank_ids[:, None] == 0) & (offsets[None, :] == 1)
    priority = jnp.where(forced, shuffles - HOME_BLK, shuffles)
    ahead = jnp.sum((priority[:, None, :] < priority[:, :, None]).astype(jnp.int32), axis=2)
    chosen = ahead < BAL_BLK
    receiver = (rank_ids[:, None] + offsets[None, :]) % rank_count
    live = chosen[receiver, offsets[None, :]]
    place = ahead[receiver, offsets[None, :]]
    return jnp.where(live, receiver * BAL_BLK + place, -1).reshape(-1).astype(jnp.int32)


def block_levels(stream_key, dims, pieces, smallest, top_value):
    def one(position, parts):
        draws = jax.random.uniform(jax.random.fold_in(jax.random.fold_in(stream_key, 6), position), (parts,), jnp.float32, smallest / len(pieces), top_value / len(pieces))
        return jnp.repeat(jnp.exp(draws), dims[position] // parts).reshape((-1,) + (1,) * (len(dims) - position - 1))

    loudness = one(*pieces[0])
    for cut in pieces[1:]:
        loudness = loudness * one(*cut)
    return loudness


def noise(own_key, dims, deviation, bound, shards=(), kind=jnp.bfloat16):
    drawn = jax.random.normal(own_key, dims, jnp.float32) * deviation
    if len(shards) > 0:
        drawn = block_levels(own_key, dims, shards, -0.22, 0.18) * drawn
    return jnp.clip(drawn, min=-bound, max=bound).astype(kind)


def setup_inputs(seed: int = 0) -> dict:
    splits = jax.random.split(jax.random.key(seed), 7)
    return {
        "tokens": noise(splits[0], (HOMES, BLOCK, D), 1.0, 6.0, ((0, 16), (1, 8))),
        "norm_gain": jnp.clip(1.0 + 0.15 * jax.random.normal(splits[1], (D,), jnp.float32), 0.25, 1.75),
        "fc1": noise(splits[2], (D, FF), D ** -0.5, 0.109375, ((1, 8),)),
        "fc2t": noise(splits[3], (D, FF), FF ** -0.5, 0.078125, ((1, 8),)),
        "block_slot": draw_block_slot(jax.random.fold_in(splits[6], 71), 0),
        "out_grad": noise(splits[5], (SLOTS, BLOCK, D), 1.0, 6.0, ((0, 16), (1, 8))),
    }


ROW_DIMS = (((1,), (1,)), ((), ()))
COL_DIMS = (((0,), (0,)), ((), ()))

def gelu_slope(value):
    normal_cdf = 0.5 * (1.0 + jax.scipy.special.erf(value * 0.7071067811865476))
    return normal_cdf + value * jnp.exp(-0.5 * value * value) * 0.3989422804014327

def reference(tokens, norm_gain, fc1, fc2t, block_slot, out_grad):
    live_block = block_slot >= 0
    target = jnp.where(live_block, block_slot, SLOTS).astype(jnp.int32)
    row_input = jnp.zeros((SLOTS, BLOCK, D), jnp.bfloat16).at[target].set(tokens, mode='drop')
    rows_flat = row_input.reshape(SLOTS * BLOCK, D).astype(jnp.float32)
    inverse_rms = lax.rsqrt(lax.optimization_barrier(jnp.mean(rows_flat * rows_flat, axis=-1, keepdims=True)) + 1e-06)
    unit_rows = rows_flat * inverse_rms
    normed = (unit_rows * norm_gain).astype(jnp.bfloat16)
    pre_act = jnp.dot(normed, fc1, preferred_element_type=jnp.float32)
    hidden = jax.nn.gelu(pre_act, approximate=False).astype(jnp.bfloat16)
    branch = lax.dot_general(hidden, fc2t, ROW_DIMS, preferred_element_type=jnp.float32)
    mixed = (rows_flat + branch).astype(jnp.bfloat16).reshape(SLOTS, BLOCK, D)
    grad_flat = out_grad.reshape(SLOTS * BLOCK, D)
    hidden_grad = jnp.dot(grad_flat, fc2t, preferred_element_type=jnp.float32)
    pre_grad = (hidden_grad * gelu_slope(pre_act)).astype(jnp.bfloat16)
    fc2t_grad = lax.dot_general(grad_flat, hidden, COL_DIMS, preferred_element_type=jnp.float32)
    fc1_grad = lax.dot_general(normed, pre_grad, COL_DIMS, preferred_element_type=jnp.float32)
    normed_grad = lax.dot_general(pre_grad, fc1, ROW_DIMS, preferred_element_type=jnp.float32)
    gain_grad = lax.optimization_barrier(jnp.sum(normed_grad * unit_rows, axis=0))
    scaled = normed_grad * norm_gain
    input_grad = grad_flat.astype(jnp.float32) + inverse_rms * (scaled - unit_rows * lax.optimization_barrier(jnp.mean(scaled * unit_rows, axis=-1, keepdims=True)))
    input_grad = input_grad.astype(jnp.bfloat16).reshape(SLOTS, BLOCK, D)
    source = jnp.where(live_block, block_slot, 0).astype(jnp.int32)
    tokens_grad = jnp.where(live_block[:, None, None], input_grad[source], jnp.zeros((), jnp.bfloat16)).astype(jnp.bfloat16)
    return (mixed, tokens_grad, fc1_grad, fc2t_grad, gain_grad)
```

```python
import functools

import jax
import jax.numpy as jnp
from jax import lax
from jax.experimental import pallas as pl
from jax.experimental.pallas import tpu as pltpu
from jax.sharding import PartitionSpec as P

MESH = pl.DeviceIdType.MESH
ROW_DIMS = (((1,), (1,)), ((), ()))
RING = 4
F32 = jnp.float32
BF16 = jnp.bfloat16


def round_up(value, unit):
    return (value + unit - 1) // unit * unit


def chunk_of(width, limit):
    tiles = width // 128
    best = 1
    for count in range(1, tiles + 1):
        if tiles % count == 0 and count * 128 <= limit:
            best = count
    return best * 128


class Sizes:
    def __init__(self, tokens, fc1, out_grad):
        self.homes, self.block_rows, self.width = tokens
        self.units = fc1[1]
        self.slots = out_grad[0]
        self.own = self.slots * self.block_rows
        self.rows = 2 * RING * self.own
        self.owned = self.width // (RING * RING)
        self.owned_pad = round_up(self.owned, 16)
        self.window = round_up(self.owned + 127, 128)
        self.last_tile = (self.width - self.window) // 128
        self.chunk = chunk_of(self.width, 640)


def kernel(
    sz,
    copies,
    slot_ref,
    gain_ref,
    tokens_ref,
    fc1_hbm,
    fc2_hbm,
    grad_hbm,
    mixed_ref,
    tgrad_ref,
    fc1_grad_ref,
    fc2_grad_ref,
    gain_grad_ref,
    fc1_ref,
    fc2_ref,
    arrived,
    row_in,
    inv_ref,
    grad_all,
    norm_all,
    grad_t,
    norm_t,
    grad_tg,
    norm_tg,
    hid_g,
    pre_g,
    pre_act,
    hid_grad,
    row_sum,
    sib_out,
    sib_in,
    rs_out,
    rs_in,
    wg_sum,
    wg_out,
    wg_in,
    back_out,
    input_grad,
    gain_sib,
    gain_x,
    gain_y,
    gain_z,
    local_sems,
    send_sems,
    recv_sems,
):
    dp = lax.axis_index("dp")
    t = lax.axis_index("tensor")
    y, z = dp // RING, dp % RING
    x, c = t // 2, t % 2
    ranks = RING * RING
    own, width, units = sz.own, sz.width, sz.units
    half = own // 2

    def on_dp(k):
        return ((dp + k + ranks) % ranks, t)

    def on_x(k):
        return (dp, ((x + k + RING) % RING) * 2 + c)

    def on_y(k):
        return (((y + k + RING) % RING) * RING + z, t)

    def on_z(k):
        return (y * RING + (z + k + RING) % RING, t)

    sibling = (dp, t + 1 - 2 * c)

    started = []

    def send(src, dst, device):
        index = len(started)
        made = pltpu.make_async_remote_copy(
            src_ref=src,
            dst_ref=dst,
            send_sem=send_sems.at[index],
            recv_sem=recv_sems.at[index],
            device_id=device,
            device_id_type=MESH,
        )
        made.start()
        started.append(made)
        return made

    def at(base, k):
        return (base + k + RING) % RING

    my_rows = pl.ds(pl.multiple_of(t * own, own), own)
    load_grad = pltpu.make_async_copy(grad_hbm, grad_all.at[my_rows], local_sems.at[0])
    load_fc2 = pltpu.make_async_copy(fc2_hbm, fc2_ref, local_sems.at[1])
    load_fc1 = pltpu.make_async_copy(fc1_hbm, fc1_ref, local_sems.at[2])
    load_grad.start()
    load_fc2.start()
    load_fc1.start()

    partners = [on_dp(k) for k in range(1, sz.homes)]
    partners += [on_dp(-k) for k in range(1, sz.homes)]
    partners += [on_y(k) for k in (1, -1, 2)]
    partners += [on_z(k) for k in (1, -1, 2)]
    partners += [on_x(k) for k in (1, -1, 2)]
    partners += [sibling]
    barrier = pltpu.get_barrier_semaphore()
    for device in partners:
        pl.semaphore_signal(barrier, inc=1, device_id=device, device_id_type=MESH)
    pl.semaphore_wait(barrier, len(partners))

    routed = [
        send(tokens_ref.at[j], arrived.at[j - 1], on_dp(j)) for j in range(1, sz.homes)
    ]

    class RowGather:
        def __init__(self, buf):
            self.buf = buf

        def part(self, k, core, lo, count):
            place = (at(x, k) * 2 + core) * own + lo
            return self.buf.at[pl.ds(pl.multiple_of(place, 16), count)]

        def start(self):
            mine = self.part(0, c, 0, own)
            self.right = send(mine, mine, on_x(1))
            self.left = send(mine, mine, on_x(-1))
            self.shared = [send(mine, mine, sibling)]

        def forward(self):
            self.right.wait_recv()
            low = self.part(-1, c, 0, half)
            self.right2 = send(low, low, on_x(1))
            whole = self.part(-1, c, 0, own)
            self.shared.append(send(whole, whole, sibling))
            self.left.wait_recv()
            high = self.part(1, c, half, own - half)
            self.left2 = send(high, high, on_x(-1))
            whole = self.part(1, c, 0, own)
            self.shared.append(send(whole, whole, sibling))

        def finish(self):
            self.right2.wait_recv()
            low = self.part(2, c, 0, half)
            self.shared.append(send(low, low, sibling))
            self.left2.wait_recv()
            high = self.part(2, c, half, own - half)
            self.shared.append(send(high, high, sibling))
            for made in self.shared:
                made.wait_recv()

    class RingGather:
        def __init__(self, buf, me, on_axis):
            self.buf, self.me, self.on_axis = buf, me, on_axis
            self.mid = buf.shape[1] // 2

        def start(self):
            mine = self.buf.at[self.me]
            self.right = send(mine, mine, self.on_axis(1))
            self.left = send(mine, mine, self.on_axis(-1))

        def forward(self):
            self.right.wait_recv()
            low = self.buf.at[at(self.me, -1), pl.ds(0, self.mid)]
            self.right2 = send(low, low, self.on_axis(1))
            self.left.wait_recv()
            high = self.buf.at[at(self.me, 1), pl.ds(self.mid, self.mid)]
            self.left2 = send(high, high, self.on_axis(-1))

        def finish(self):
            self.right2.wait_recv()
            self.left2.wait_recv()

    def transpose_slices(src, dst, dp_of):
        @pl.loop(0, ranks)
        def _(k):
            owner = dp_of(k)
            first = owner * sz.owned
            tile = jnp.minimum(first // 128, sz.last_tile)
            shift = first - tile * 128
            shape = (sz.owned_pad, sz.window)
            rows = lax.broadcasted_iota(jnp.int32, shape, 0)
            cols = lax.broadcasted_iota(jnp.int32, shape, 1)
            pick = jnp.where(cols == rows + shift, 1.0, 0.0).astype(BF16)
            part = src[:, pl.ds(pl.multiple_of(tile * 128, 128), sz.window)]
            dst[k] = lax.dot_general(
                pick, part, ROW_DIMS, preferred_element_type=F32
            ).astype(BF16)

    class SliceExchange:
        def __init__(self, src, dst, me, on_axis, sem):
            self.src, self.dst, self.me, self.on_axis = src, dst, me, on_axis
            self.sem = sem

        def start(self):
            pair = RING // 2
            self.direct = []
            for k in (1, -1, 2):
                piece = self.src.at[pl.ds(at(self.me, k) * RING + pair * c, pair)]
                place = self.dst.at[self.me, pl.ds(pair * c, pair)]
                self.direct.append(send(piece, place, self.on_axis(k)))
            self.local = pltpu.make_async_copy(
                self.src.at[pl.ds(self.me * RING, RING)], self.dst.at[self.me], self.sem
            )
            self.local.start()

        def share(self):
            pair = RING // 2
            self.shared = []
            for k, made in zip((1, -1, 2), self.direct):
                made.wait_recv()
                place = self.dst.at[at(self.me, -k), pl.ds(pair * c, pair)]
                self.shared.append(send(place, place, sibling))

        def finish(self):
            for made in self.shared:
                made.wait_recv()
            self.local.wait()

    class RingReduce:
        def __init__(self, part, out, into, me, on_axis, mid):
            self.part, self.out, self.into = part, out, into
            self.me, self.on_axis, self.mid = me, on_axis, mid
            self.count = part.shape[1]

        def start(self):
            lo, hi = pl.ds(0, self.mid), pl.ds(self.mid, self.count - self.mid)
            far, right, left = at(self.me, 2), at(self.me, 1), at(self.me, -1)
            out, into = self.out, self.into
            out[0, lo] = self.part[far, lo].astype(BF16)
            self.far_right = send(out.at[0, lo], into.at[0, lo], self.on_axis(1))
            out[0, hi] = self.part[far, hi].astype(BF16)
            self.far_left = send(out.at[0, hi], into.at[0, hi], self.on_axis(-1))
            out[1, hi] = self.part[right, hi].astype(BF16)
            self.near_right = send(out.at[1, hi], into.at[1, hi], self.on_axis(1))
            out[2, lo] = self.part[left, lo].astype(BF16)
            self.near_left = send(out.at[2, lo], into.at[2, lo], self.on_axis(-1))

        def forward(self):
            lo, hi = pl.ds(0, self.mid), pl.ds(self.mid, self.count - self.mid)
            right, left = at(self.me, 1), at(self.me, -1)
            out, into = self.out, self.into
            self.far_right.wait_recv()
            out[1, lo] = (self.part[right, lo] + into[0, lo].astype(F32)).astype(BF16)
            self.sum_right = send(out.at[1, lo], into.at[1, lo], self.on_axis(1))
            self.far_left.wait_recv()
            out[2, hi] = (self.part[left, hi] + into[0, hi].astype(F32)).astype(BF16)
            self.sum_left = send(out.at[2, hi], into.at[2, hi], self.on_axis(-1))

        def finish(self):
            self.near_right.wait_recv()
            self.near_left.wait_recv()
            self.sum_right.wait_recv()
            self.sum_left.wait_recv()

        def total(self):
            return (
                self.part[self.me]
                + self.into[1].astype(F32)
                + self.into[2].astype(F32)
            )

    class RowReduce:
        def __init__(self, index):
            self.index = index

        def multiply(self, lhs, weight):
            index = self.index

            @pl.loop(0, width // sz.chunk)
            def _(n):
                cols = pl.ds(pl.multiple_of(n * sz.chunk, sz.chunk), sz.chunk)
                full = lax.dot_general(
                    lhs[...], weight[cols, :], ROW_DIMS, preferred_element_type=F32
                )
                for k in range(RING):
                    even = full[2 * k * own : (2 * k + 1) * own]
                    odd = full[(2 * k + 1) * own : (2 * k + 2) * own]
                    row_sum[index, k, :, cols] = jnp.where(c == 0, even, odd)
                    sib_out[index, k, :, cols] = jnp.where(c == 0, odd, even).astype(BF16)

            self.copy = send(sib_out.at[index], sib_in.at[index], sibling)

        def start(self):
            index = self.index
            self.copy.wait_recv()
            row_sum[index] = row_sum[index] + sib_in[index].astype(F32)
            self.ring = RingReduce(
                row_sum.at[index], rs_out.at[index], rs_in.at[index], x, on_x, half
            )
            self.ring.start()

    def multiply_grad(index, lhs, rhs):
        @pl.loop(0, RING)
        def _(k):
            total = jnp.dot(lhs[0, k], rhs[0], preferred_element_type=F32)
            for g in range(1, RING):
                total += jnp.dot(lhs[g, k], rhs[g], preferred_element_type=F32)
            wg_sum[index, k] = total

    grad_rows = RowGather(grad_all)
    norm_rows = RowGather(norm_all)
    load_grad.wait()
    grad_rows.start()

    def pick(s, j):
        home = (dp - j + ranks) % ranks
        named = slot_ref[home * sz.homes + j]
        return jnp.where(named == dp * sz.slots + s, 1.0, 0.0).astype(F32)

    grad_rows.forward()
    for made in routed:
        made.wait_recv()
    for s in range(sz.slots):
        total = pick(s, 0) * tokens_ref[0].astype(F32)
        for j in range(1, sz.homes):
            total += pick(s, j) * arrived[j - 1].astype(F32)
        row_in[s * sz.block_rows : (s + 1) * sz.block_rows, :] = total
    rows_f = row_in[...]
    inv = lax.rsqrt(jnp.mean(rows_f * rows_f, axis=-1, keepdims=True) + 1e-06)
    inv_ref[...] = jnp.broadcast_to(inv, inv_ref.shape)
    norm_all[my_rows, :] = (rows_f * inv * gain_ref[...]).astype(BF16)
    norm_rows.start()

    grad_rows.finish()
    load_fc2.wait()

    def multiply_in(lhs, weight, out):
        @pl.loop(0, width // sz.chunk)
        def _(n):
            cols = pl.ds(pl.multiple_of(n * sz.chunk, sz.chunk), sz.chunk)
            part = jnp.dot(lhs[:, cols], weight[cols, :], preferred_element_type=F32)

            @pl.when(n == 0)
            def _():
                out[...] = part

            @pl.when(n > 0)
            def _():
                out[...] += part

    multiply_in(grad_all, fc2_ref, hid_grad)
    norm_rows.forward()
    transpose_slices(grad_all, grad_t, lambda k: k)
    grad_slices = SliceExchange(grad_t, grad_tg, y, on_y, local_sems.at[3])
    grad_slices.start()
    norm_rows.finish()

    load_fc1.wait()
    multiply_in(norm_all, fc1_ref, pre_act)

    @pl.loop(0, sz.rows // 16)
    def _(n):
        rows = pl.ds(pl.multiple_of(n * 16, 16), 16)
        value = pre_act[rows, :]
        cdf = 0.5 * (1.0 + lax.erf(value * 0.7071067811865476))
        slope = cdf + value * jnp.exp(-0.5 * value * value) * 0.3989422804014327
        hid_g[y, rows, :] = (value * cdf).astype(BF16)
        pre_g[z, rows, :] = (hid_grad[rows, :] * slope).astype(BF16)

    hid_ring = RingGather(hid_g, y, on_y)
    pre_ring = RingGather(pre_g, z, on_z)
    hid_ring.start()
    pre_ring.start()
    transpose_slices(norm_all, norm_t, lambda k: (k % RING) * RING + k // RING)
    norm_slices = SliceExchange(norm_t, norm_tg, z, on_z, local_sems.at[4])
    norm_slices.start()
    grad_slices.share()

    branch = RowReduce(0)
    branch.multiply(hid_g.at[y], fc2_ref)
    back = RowReduce(1)
    back.multiply(pre_g.at[z], fc1_ref)
    branch.start()
    hid_ring.forward()
    pre_ring.forward()
    back.start()
    norm_slices.share()
    branch.ring.forward()
    back.ring.forward()

    branch.ring.finish()
    mixed_ref[...] = (row_in[...] + branch.ring.total()).astype(BF16)

    back.ring.finish()
    normed_grad = back.ring.total()
    unit = row_in[...] * inv_ref[:, :1]
    product = normed_grad * unit
    gain_sib[0] = jnp.sum(product, axis=0, keepdims=True)
    gain_pair = send(gain_sib.at[0], gain_sib.at[1], sibling)
    scaled = normed_grad * gain_ref[...]
    inner = scaled - unit * jnp.mean(scaled * unit, axis=-1, keepdims=True)
    input_grad[...] = (
        grad_all[my_rows, :].astype(F32) + inv_ref[:, :1] * inner
    ).astype(BF16).astype(F32)

    returned = []
    for j in range(sz.homes):
        total = pick(0, j) * input_grad[0 : sz.block_rows, :]
        for s in range(1, sz.slots):
            total += pick(s, j) * input_grad[s * sz.block_rows : (s + 1) * sz.block_rows, :]
        if j == 0:
            tgrad_ref[0] = total.astype(BF16)
        else:
            back_out[j - 1] = total.astype(BF16)
            returned.append(send(back_out.at[j - 1], tgrad_ref.at[j], on_dp(-j)))

    hid_ring.finish()
    grad_slices.finish()
    multiply_grad(0, grad_tg, hid_g)
    mid = round_up(sz.owned_pad // 2, 16)
    fc2_ring = RingReduce(wg_sum.at[0], wg_out.at[0], wg_in.at[0], z, on_z, mid)
    fc2_ring.start()
    pre_ring.finish()
    norm_slices.finish()
    multiply_grad(1, norm_tg, pre_g)
    fc1_ring = RingReduce(wg_sum.at[1], wg_out.at[1], wg_in.at[1], y, on_y, mid)
    fc1_ring.start()

    gain_pair.wait_recv()
    total = gain_sib[0] + gain_sib[1]

    def add_over(buf, me, on_axis, total):
        buf[me] = total
        made = [send(buf.at[me], buf.at[me], on_axis(k)) for k in (1, -1, 2)]
        for one in made:
            one.wait_recv()
        return buf[0] + buf[1] + buf[2] + buf[3]

    total = add_over(gain_x, x, on_x, total)
    fc2_ring.forward()
    total = add_over(gain_y, y, on_y, total)
    fc1_ring.forward()
    total = add_over(gain_z, z, on_z, total)
    gain_grad_ref[...] = total

    fc2_ring.finish()
    fc2_grad_ref[...] = fc2_ring.total()[: sz.owned]
    fc1_ring.finish()
    fc1_grad_ref[...] = fc1_ring.total()[: sz.owned]
    for made in returned:
        made.wait_recv()
    for made in started:
        made.wait_send()
    if len(started) != copies:
        raise ValueError(len(started))


COPIES = 82


def local(tokens, norm_gain, fc1, fc2t, block_slot, out_grad):
    sz = Sizes(tokens.shape, fc1.shape, out_grad.shape)
    width, units = sz.width, sz.units
    vmem = pl.BlockSpec(memory_space=pltpu.VMEM)
    anywhere = pl.BlockSpec(memory_space=pl.ANY)
    slices = (RING, RING, sz.owned_pad, sz.rows)
    mixed, tgrad, fc1_grad, fc2_grad, gain_grad = pl.pallas_call(
        functools.partial(kernel, sz, COPIES),
        out_shape=(
            jax.ShapeDtypeStruct((sz.own, width), BF16),
            jax.ShapeDtypeStruct(tokens.shape, BF16),
            jax.ShapeDtypeStruct((sz.owned, units), F32),
            jax.ShapeDtypeStruct((sz.owned, units), F32),
            jax.ShapeDtypeStruct((1, width), F32),
        ),
        in_specs=[
            pl.BlockSpec(memory_space=pltpu.SMEM),
            vmem,
            vmem,
            anywhere,
            anywhere,
            anywhere,
        ],
        out_specs=(vmem,) * 5,
        scratch_shapes=[
            pltpu.VMEM(fc1.shape, BF16),
            pltpu.VMEM(fc2t.shape, BF16),
            pltpu.VMEM((sz.homes - 1, sz.block_rows, width), BF16),
            pltpu.VMEM((sz.own, width), F32),
            pltpu.VMEM((sz.own, 128), F32),
            pltpu.VMEM((sz.rows, width), BF16),
            pltpu.VMEM((sz.rows, width), BF16),
            pltpu.VMEM((RING * RING, sz.owned_pad, sz.rows), BF16),
            pltpu.VMEM((RING * RING, sz.owned_pad, sz.rows), BF16),
            pltpu.VMEM(slices, BF16),
            pltpu.VMEM(slices, BF16),
            pltpu.VMEM((RING, sz.rows, units), BF16),
            pltpu.VMEM((RING, sz.rows, units), BF16),
            pltpu.VMEM((sz.rows, units), F32),
            pltpu.VMEM((sz.rows, units), F32),
            pltpu.VMEM((2, RING, sz.own, width), F32),
            pltpu.VMEM((2, RING, sz.own, width), BF16),
            pltpu.VMEM((2, RING, sz.own, width), BF16),
            pltpu.VMEM((2, 3, sz.own, width), BF16),
            pltpu.VMEM((2, 3, sz.own, width), BF16),
            pltpu.VMEM((2, RING, sz.owned_pad, units), F32),
            pltpu.VMEM((2, 3, sz.owned_pad, units), BF16),
            pltpu.VMEM((2, 3, sz.owned_pad, units), BF16),
            pltpu.VMEM((sz.homes - 1, sz.block_rows, width), BF16),
            pltpu.VMEM((sz.own, width), F32),
            pltpu.VMEM((2, 1, width), F32),
            pltpu.VMEM((RING, 1, width), F32),
            pltpu.VMEM((RING, 1, width), F32),
            pltpu.VMEM((RING, 1, width), F32),
            pltpu.SemaphoreType.DMA((5,)),
            pltpu.SemaphoreType.DMA((COPIES,)),
            pltpu.SemaphoreType.DMA((COPIES,)),
        ],
        compiler_params=pltpu.CompilerParams(
            collective_id=0, has_side_effects=True, vmem_limit_bytes=60 * 1024 * 1024
        ),
        cost_estimate=pl.CostEstimate(
            flops=12 * sz.rows * width * units,
            bytes_accessed=4 * width * units,
            transcendentals=2 * sz.rows * units,
        ),
        name="mlp_block",
    )(
        block_slot,
        norm_gain.reshape(1, width),
        tokens,
        fc1,
        fc2t,
        out_grad.reshape(sz.own, width),
    )
    return (
        mixed.reshape(out_grad.shape),
        tgrad,
        fc1_grad,
        fc2_grad,
        gain_grad.reshape(width),
    )


def solution(mesh):
    placed = (
        P("dp", "tensor", None),
        P(),
        P(None, "tensor"),
        P(None, "tensor"),
        P(),
        P("dp", "tensor", None),
    )
    return jax.shard_map(
        local,
        mesh=mesh,
        in_specs=placed,
        out_specs=(
            P("dp", "tensor", None),
            P("dp", "tensor", None),
            P("dp", "tensor"),
            P("dp", "tensor"),
            P(),
        ),
        check_vma=False,
    )
```

```python
import functools

import jax
import jax.numpy as jnp
from jax import lax
from jax.experimental import pallas as pl
from jax.experimental.pallas import tpu as pltpu
from jax.sharding import PartitionSpec as P

MESH = pl.DeviceIdType.MESH
ROW_DIMS = (((1,), (1,)), ((), ()))
RING = 4
F32 = jnp.float32
BF16 = jnp.bfloat16


def round_up(value, unit):
    return (value + unit - 1) // unit * unit


def chunk_of(width, limit):
    tiles = width // 128
    best = 1
    for count in range(1, tiles + 1):
        if tiles % count == 0 and count * 128 <= limit:
            best = count
    return best * 128


class Sizes:
    def __init__(self, tokens, fc1, out_grad):
        self.homes, self.block_rows, self.width = tokens
        self.units = fc1[1]
        self.slots = out_grad[0]
        self.own = self.slots * self.block_rows
        self.rows = 2 * RING * self.own
        self.owned = self.width // (RING * RING)
        self.owned_pad = round_up(self.owned, 16)
        self.window = round_up(self.owned + 127, 128)
        self.last_tile = (self.width - self.window) // 128
        self.chunk = chunk_of(self.width, 640)


def kernel(
    sz,
    copies,
    slot_ref,
    gain_ref,
    tokens_ref,
    fc1_hbm,
    fc2_hbm,
    grad_hbm,
    mixed_ref,
    tgrad_ref,
    fc1_grad_ref,
    fc2_grad_ref,
    gain_grad_ref,
    fc1_ref,
    fc2_ref,
    arrived,
    row_in,
    inv_ref,
    grad_all,
    norm_all,
    grad_t,
    norm_t,
    grad_tg,
    norm_tg,
    hid_g,
    pre_g,
    pre_act,
    hid_grad,
    row_sum,
    sib_out,
    sib_in,
    rs_out,
    rs_in,
    wg_sum,
    wg_out,
    wg_in,
    back_out,
    input_grad,
    gain_sib,
    gain_x,
    gain_y,
    gain_z,
    local_sems,
    send_sems,
    recv_sems,
):
    dp = lax.axis_index("dp")
    t = lax.axis_index("tensor")
    y, z = dp // RING, dp % RING
    x, c = t // 2, t % 2
    ranks = RING * RING
    own, width, units = sz.own, sz.width, sz.units
    half = own // 2

    def on_dp(k):
        return ((dp + k + ranks) % ranks, t)

    def on_x(k):
        return (dp, ((x + k + RING) % RING) * 2 + c)

    def on_y(k):
        return (((y + k + RING) % RING) * RING + z, t)

    def on_z(k):
        return (y * RING + (z + k + RING) % RING, t)

    sibling = (dp, t + 1 - 2 * c)

    started = []

    def send(src, dst, device):
        index = len(started)
        made = pltpu.make_async_remote_copy(
            src_ref=src,
            dst_ref=dst,
            send_sem=send_sems.at[index],
            recv_sem=recv_sems.at[index],
            device_id=device,
            device_id_type=MESH,
        )
        made.start()
        started.append(made)
        return made

    def at(base, k):
        return (base + k + RING) % RING

    my_rows = pl.ds(pl.multiple_of(t * own, own), own)
    load_grad = pltpu.make_async_copy(grad_hbm, grad_all.at[my_rows], local_sems.at[0])
    load_fc2 = pltpu.make_async_copy(fc2_hbm, fc2_ref, local_sems.at[1])
    load_fc1 = pltpu.make_async_copy(fc1_hbm, fc1_ref, local_sems.at[2])
    load_grad.start()
    load_fc2.start()
    load_fc1.start()

    partners = [on_dp(k) for k in range(1, sz.homes)]
    partners += [on_dp(-k) for k in range(1, sz.homes)]
    partners += [on_y(k) for k in (1, -1, 2)]
    partners += [on_z(k) for k in (1, -1, 2)]
    partners += [on_x(k) for k in (1, -1, 2)]
    partners += [sibling]
    barrier = pltpu.get_barrier_semaphore()
    for device in partners:
        pl.semaphore_signal(barrier, inc=1, device_id=device, device_id_type=MESH)
    pl.semaphore_wait(barrier, len(partners))

    routed = [
        send(tokens_ref.at[j], arrived.at[j - 1], on_dp(j)) for j in range(1, sz.homes)
    ]

    class RowGather:
        def __init__(self, buf):
            self.buf = buf

        def part(self, k, core, lo, count):
            place = (at(x, k) * 2 + core) * own + lo
            return self.buf.at[pl.ds(pl.multiple_of(place, 16), count)]

        def start(self):
            mine = self.part(0, c, 0, own)
            self.right = send(mine, mine, on_x(1))
            self.left = send(mine, mine, on_x(-1))
            self.shared = [send(mine, mine, sibling)]

        def forward(self):
            self.right.wait_recv()
            low = self.part(-1, c, 0, half)
            self.right2 = send(low, low, on_x(1))
            whole = self.part(-1, c, 0, own)
            self.shared.append(send(whole, whole, sibling))
            self.left.wait_recv()
            high = self.part(1, c, half, own - half)
            self.left2 = send(high, high, on_x(-1))
            whole = self.part(1, c, 0, own)
            self.shared.append(send(whole, whole, sibling))

        def finish(self):
            self.right2.wait_recv()
            low = self.part(2, c, 0, half)
            self.shared.append(send(low, low, sibling))
            self.left2.wait_recv()
            high = self.part(2, c, half, own - half)
            self.shared.append(send(high, high, sibling))
            for made in self.shared:
                made.wait_recv()

    class RingGather:
        def __init__(self, buf, me, on_axis):
            self.buf, self.me, self.on_axis = buf, me, on_axis
            self.mid = buf.shape[1] // 2

        def start(self):
            mine = self.buf.at[self.me]
            self.right = send(mine, mine, self.on_axis(1))
            self.left = send(mine, mine, self.on_axis(-1))

        def forward(self):
            self.right.wait_recv()
            low = self.buf.at[at(self.me, -1), pl.ds(0, self.mid)]
            self.right2 = send(low, low, self.on_axis(1))
            self.left.wait_recv()
            high = self.buf.at[at(self.me, 1), pl.ds(self.mid, self.mid)]
            self.left2 = send(high, high, self.on_axis(-1))

        def finish(self):
            self.right2.wait_recv()
            self.left2.wait_recv()

    def transpose_slices(src, dst, dp_of):
        @pl.loop(0, ranks)
        def _(k):
            owner = dp_of(k)
            first = owner * sz.owned
            tile = jnp.minimum(first // 128, sz.last_tile)
            shift = first - tile * 128
            shape = (sz.owned_pad, sz.window)
            rows = lax.broadcasted_iota(jnp.int32, shape, 0)
            cols = lax.broadcasted_iota(jnp.int32, shape, 1)
            pick = jnp.where(cols == rows + shift, 1.0, 0.0).astype(BF16)
            part = src[:, pl.ds(pl.multiple_of(tile * 128, 128), sz.window)]
            dst[k] = lax.dot_general(
                pick, part, ROW_DIMS, preferred_element_type=F32
            ).astype(BF16)

    class SliceExchange:
        def __init__(self, src, dst, me, on_axis, sem):
            self.src, self.dst, self.me, self.on_axis = src, dst, me, on_axis
            self.sem = sem

        def start(self):
            pair = RING // 2
            self.direct = []
            for k in (1, -1, 2):
                piece = self.src.at[pl.ds(at(self.me, k) * RING + pair * c, pair)]
                place = self.dst.at[self.me, pl.ds(pair * c, pair)]
                self.direct.append(send(piece, place, self.on_axis(k)))
            self.local = pltpu.make_async_copy(
                self.src.at[pl.ds(self.me * RING, RING)], self.dst.at[self.me], self.sem
            )
            self.local.start()

        def share(self):
            pair = RING // 2
            self.shared = []
            for k, made in zip((1, -1, 2), self.direct):
                made.wait_recv()
                place = self.dst.at[at(self.me, -k), pl.ds(pair * c, pair)]
                self.shared.append(send(place, place, sibling))

        def finish(self):
            for made in self.shared:
                made.wait_recv()
            self.local.wait()

    class RingReduce:
        def __init__(self, part, out, into, me, on_axis, mid):
            self.part, self.out, self.into = part, out, into
            self.me, self.on_axis, self.mid = me, on_axis, mid
            self.count = part.shape[1]

        def start(self):
            lo, hi = pl.ds(0, self.mid), pl.ds(self.mid, self.count - self.mid)
            far, right, left = at(self.me, 2), at(self.me, 1), at(self.me, -1)
            out, into = self.out, self.into
            out[0, lo] = self.part[far, lo].astype(BF16)
            self.far_right = send(out.at[0, lo], into.at[0, lo], self.on_axis(1))
            out[0, hi] = self.part[far, hi].astype(BF16)
            self.far_left = send(out.at[0, hi], into.at[0, hi], self.on_axis(-1))
            out[1, hi] = self.part[right, hi].astype(BF16)
            self.near_right = send(out.at[1, hi], into.at[1, hi], self.on_axis(1))
            out[2, lo] = self.part[left, lo].astype(BF16)
            self.near_left = send(out.at[2, lo], into.at[2, lo], self.on_axis(-1))

        def forward(self):
            lo, hi = pl.ds(0, self.mid), pl.ds(self.mid, self.count - self.mid)
            right, left = at(self.me, 1), at(self.me, -1)
            out, into = self.out, self.into
            self.far_right.wait_recv()
            out[1, lo] = (self.part[right, lo] + into[0, lo].astype(F32)).astype(BF16)
            self.sum_right = send(out.at[1, lo], into.at[1, lo], self.on_axis(1))
            self.far_left.wait_recv()
            out[2, hi] = (self.part[left, hi] + into[0, hi].astype(F32)).astype(BF16)
            self.sum_left = send(out.at[2, hi], into.at[2, hi], self.on_axis(-1))

        def finish(self):
            self.near_right.wait_recv()
            self.near_left.wait_recv()
            self.sum_right.wait_recv()
            self.sum_left.wait_recv()

        def total(self):
            return (
                self.part[self.me]
                + self.into[1].astype(F32)
                + self.into[2].astype(F32)
            )

    class RowReduce:
        def __init__(self, index):
            self.index = index

        def multiply(self, lhs, weight):
            index = self.index

            @pl.loop(0, width // sz.chunk)
            def _(n):
                cols = pl.ds(pl.multiple_of(n * sz.chunk, sz.chunk), sz.chunk)
                full = jnp.dot(lhs[...], weight[:, cols], preferred_element_type=F32)
                for k in range(RING):
                    even = full[2 * k * own : (2 * k + 1) * own]
                    odd = full[(2 * k + 1) * own : (2 * k + 2) * own]
                    row_sum[index, k, :, cols] = jnp.where(c == 0, even, odd)
                    sib_out[index, k, :, cols] = jnp.where(c == 0, odd, even).astype(BF16)

            self.copy = send(sib_out.at[index], sib_in.at[index], sibling)

        def start(self):
            index = self.index
            self.copy.wait_recv()
            row_sum[index] = row_sum[index] + sib_in[index].astype(F32)
            self.ring = RingReduce(
                row_sum.at[index], rs_out.at[index], rs_in.at[index], x, on_x, half
            )
            self.ring.start()

    def multiply_grad(index, lhs, rhs):
        @pl.loop(0, RING)
        def _(k):
            total = jnp.dot(lhs[0, k], rhs[0], preferred_element_type=F32)
            for g in range(1, RING):
                total += jnp.dot(lhs[g, k], rhs[g], preferred_element_type=F32)
            wg_sum[index, k] = total

    grad_rows = RowGather(grad_all)
    norm_rows = RowGather(norm_all)
    load_grad.wait()
    grad_rows.start()

    def pick(s, j):
        home = (dp - j + ranks) % ranks
        named = slot_ref[home * sz.homes + j]
        return jnp.where(named == dp * sz.slots + s, 1.0, 0.0).astype(F32)

    grad_rows.forward()
    for made in routed:
        made.wait_recv()
    for s in range(sz.slots):
        total = pick(s, 0) * tokens_ref[0].astype(F32)
        for j in range(1, sz.homes):
            total += pick(s, j) * arrived[j - 1].astype(F32)
        row_in[s * sz.block_rows : (s + 1) * sz.block_rows, :] = total
    rows_f = row_in[...]
    inv = lax.rsqrt(jnp.mean(rows_f * rows_f, axis=-1, keepdims=True) + 1e-06)
    inv_ref[...] = jnp.broadcast_to(inv, inv_ref.shape)
    norm_all[my_rows, :] = (rows_f * inv * gain_ref[...].reshape(1, width)).astype(BF16)
    norm_rows.start()

    grad_rows.finish()
    load_fc2.wait()

    def multiply_in(lhs, weight, out):
        @pl.loop(0, width // sz.chunk)
        def _(n):
            cols = pl.ds(pl.multiple_of(n * sz.chunk, sz.chunk), sz.chunk)
            part = lax.dot_general(
                lhs[:, cols], weight[:, cols], ROW_DIMS, preferred_element_type=F32
            )

            @pl.when(n == 0)
            def _():
                out[...] = part

            @pl.when(n > 0)
            def _():
                out[...] += part

    multiply_in(grad_all, fc2_ref, hid_grad)
    norm_rows.forward()
    transpose_slices(grad_all, grad_t, lambda k: k)
    grad_slices = SliceExchange(grad_t, grad_tg, y, on_y, local_sems.at[3])
    grad_slices.start()
    norm_rows.finish()

    load_fc1.wait()
    multiply_in(norm_all, fc1_ref, pre_act)

    @pl.loop(0, sz.rows // 16)
    def _(n):
        rows = pl.ds(pl.multiple_of(n * 16, 16), 16)
        value = pre_act[rows, :]
        cdf = 0.5 * (1.0 + lax.erf(value * 0.7071067811865476))
        slope = cdf + value * jnp.exp(-0.5 * value * value) * 0.3989422804014327
        hid_g[y, rows, :] = (value * cdf).astype(BF16)
        pre_g[z, rows, :] = (hid_grad[rows, :] * slope).astype(BF16)

    hid_ring = RingGather(hid_g, y, on_y)
    pre_ring = RingGather(pre_g, z, on_z)
    hid_ring.start()
    pre_ring.start()
    transpose_slices(norm_all, norm_t, lambda k: (k % RING) * RING + k // RING)
    norm_slices = SliceExchange(norm_t, norm_tg, z, on_z, local_sems.at[4])
    norm_slices.start()
    grad_slices.share()

    branch = RowReduce(0)
    branch.multiply(hid_g.at[y], fc2_ref)
    back = RowReduce(1)
    back.multiply(pre_g.at[z], fc1_ref)
    branch.start()
    hid_ring.forward()
    pre_ring.forward()
    back.start()
    norm_slices.share()
    branch.ring.forward()
    back.ring.forward()

    branch.ring.finish()
    mixed_ref[...] = (row_in[...] + branch.ring.total()).astype(BF16)

    back.ring.finish()
    normed_grad = back.ring.total()
    unit = row_in[...] * inv_ref[:, :1]
    product = normed_grad * unit
    gain_sib[0] = jnp.sum(product, axis=0, keepdims=True)
    gain_pair = send(gain_sib.at[0], gain_sib.at[1], sibling)
    scaled = normed_grad * gain_ref[...].reshape(1, width)
    inner = scaled - unit * jnp.mean(scaled * unit, axis=-1, keepdims=True)
    input_grad[...] = (
        grad_all[my_rows, :].astype(F32) + inv_ref[:, :1] * inner
    ).astype(BF16).astype(F32)

    returned = []
    for j in range(sz.homes):
        total = pick(0, j) * input_grad[0 : sz.block_rows, :]
        for s in range(1, sz.slots):
            total += pick(s, j) * input_grad[s * sz.block_rows : (s + 1) * sz.block_rows, :]
        if j == 0:
            tgrad_ref[0] = total.astype(BF16)
        else:
            back_out[j - 1] = total.astype(BF16)
            returned.append(send(back_out.at[j - 1], tgrad_ref.at[j], on_dp(-j)))

    hid_ring.finish()
    grad_slices.finish()
    multiply_grad(0, grad_tg, hid_g)
    mid = round_up(sz.owned_pad // 2, 16)
    fc2_ring = RingReduce(wg_sum.at[0], wg_out.at[0], wg_in.at[0], z, on_z, mid)
    fc2_ring.start()
    pre_ring.finish()
    norm_slices.finish()
    multiply_grad(1, norm_tg, pre_g)
    fc1_ring = RingReduce(wg_sum.at[1], wg_out.at[1], wg_in.at[1], y, on_y, mid)
    fc1_ring.start()

    gain_pair.wait_recv()
    total = gain_sib[0] + gain_sib[1]

    def add_over(buf, me, on_axis, total):
        buf[me] = total
        made = [send(buf.at[me], buf.at[me], on_axis(k)) for k in (1, -1, 2)]
        for one in made:
            one.wait_recv()
        return buf[0] + buf[1] + buf[2] + buf[3]

    total = add_over(gain_x, x, on_x, total)
    fc2_ring.forward()
    total = add_over(gain_y, y, on_y, total)
    fc1_ring.forward()
    total = add_over(gain_z, z, on_z, total)
    gain_grad_ref[...] = total.reshape(width)

    fc2_ring.finish()
    fc2_grad_ref[...] = fc2_ring.total()[: sz.owned]
    fc1_ring.finish()
    fc1_grad_ref[...] = fc1_ring.total()[: sz.owned]
    for made in returned:
        made.wait_recv()
    for made in started:
        made.wait_send()
    if len(started) != copies:
        raise ValueError(len(started))


def hand_over_kernel(*refs):
    count = len(refs) // 2
    sems = refs[-1]
    made = [
        pltpu.make_async_copy(refs[i], refs[count + i], sems.at[i]) for i in range(count)
    ]
    for one in made:
        one.start()
    for one in made:
        one.wait()


def hand_over(*arrays):
    anywhere = pl.BlockSpec(memory_space=pl.ANY)
    return pl.pallas_call(
        hand_over_kernel,
        out_shape=tuple(jax.ShapeDtypeStruct(a.shape, a.dtype) for a in arrays),
        in_specs=[anywhere] * len(arrays),
        out_specs=(anywhere,) * len(arrays),
        scratch_shapes=[pltpu.SemaphoreType.DMA((len(arrays),))],
        compiler_params=pltpu.CompilerParams(vmem_limit_bytes=60 * 1024 * 1024),
        name="hand_over",
    )(*arrays)


COPIES = 82


def local(tokens, norm_gain, fc1, fc2t, block_slot, out_grad):
    sz = Sizes(tokens.shape, fc1.shape, out_grad.shape)
    width, units = sz.width, sz.units
    vmem = pl.BlockSpec(memory_space=pltpu.VMEM)
    anywhere = pl.BlockSpec(memory_space=pl.ANY)
    slices = (RING, RING, sz.owned_pad, sz.rows)
    mixed, tgrad, fc1_grad, fc2_grad, gain_grad = pl.pallas_call(
        functools.partial(kernel, sz, COPIES),
        out_shape=(
            jax.ShapeDtypeStruct((sz.own, width), BF16),
            jax.ShapeDtypeStruct(tokens.shape, BF16),
            jax.ShapeDtypeStruct((sz.owned, units), F32),
            jax.ShapeDtypeStruct((sz.owned, units), F32),
            jax.ShapeDtypeStruct((width,), F32),
        ),
        in_specs=[
            pl.BlockSpec(memory_space=pltpu.SMEM),
            vmem,
            vmem,
            anywhere,
            anywhere,
            anywhere,
        ],
        out_specs=(vmem,) * 5,
        scratch_shapes=[
            pltpu.VMEM((units, width), BF16),
            pltpu.VMEM((units, width), BF16),
            pltpu.VMEM((sz.homes - 1, sz.block_rows, width), BF16),
            pltpu.VMEM((sz.own, width), F32),
            pltpu.VMEM((sz.own, 128), F32),
            pltpu.VMEM((sz.rows, width), BF16),
            pltpu.VMEM((sz.rows, width), BF16),
            pltpu.VMEM((RING * RING, sz.owned_pad, sz.rows), BF16),
            pltpu.VMEM((RING * RING, sz.owned_pad, sz.rows), BF16),
            pltpu.VMEM(slices, BF16),
            pltpu.VMEM(slices, BF16),
            pltpu.VMEM((RING, sz.rows, units), BF16),
            pltpu.VMEM((RING, sz.rows, units), BF16),
            pltpu.VMEM((sz.rows, units), F32),
            pltpu.VMEM((sz.rows, units), F32),
            pltpu.VMEM((2, RING, sz.own, width), F32),
            pltpu.VMEM((2, RING, sz.own, width), BF16),
            pltpu.VMEM((2, RING, sz.own, width), BF16),
            pltpu.VMEM((2, 3, sz.own, width), BF16),
            pltpu.VMEM((2, 3, sz.own, width), BF16),
            pltpu.VMEM((2, RING, sz.owned_pad, units), F32),
            pltpu.VMEM((2, 3, sz.owned_pad, units), BF16),
            pltpu.VMEM((2, 3, sz.owned_pad, units), BF16),
            pltpu.VMEM((sz.homes - 1, sz.block_rows, width), BF16),
            pltpu.VMEM((sz.own, width), F32),
            pltpu.VMEM((2, 1, width), F32),
            pltpu.VMEM((RING, 1, width), F32),
            pltpu.VMEM((RING, 1, width), F32),
            pltpu.VMEM((RING, 1, width), F32),
            pltpu.SemaphoreType.DMA((5,)),
            pltpu.SemaphoreType.DMA((COPIES,)),
            pltpu.SemaphoreType.DMA((COPIES,)),
        ],
        compiler_params=pltpu.CompilerParams(
            collective_id=0, has_side_effects=True, vmem_limit_bytes=60 * 1024 * 1024
        ),
        cost_estimate=pl.CostEstimate(
            flops=12 * sz.rows * width * units,
            bytes_accessed=4 * width * units,
            transcendentals=2 * sz.rows * units,
        ),
        name="mlp_block",
    )(
        block_slot,
        norm_gain,
        tokens,
        fc1.T,
        fc2t.T,
        out_grad.reshape(sz.own, width),
    )
    mixed, tgrad, fc1_grad, fc2_grad, gain_grad = hand_over(
        mixed, tgrad, fc1_grad, fc2_grad, gain_grad
    )
    return mixed.reshape(out_grad.shape), tgrad, fc1_grad, fc2_grad, gain_grad


def solution(mesh):
    placed = (
        P("dp", "tensor", None),
        P(),
        P(None, "tensor"),
        P(None, "tensor"),
        P(),
        P("dp", "tensor", None),
    )
    return jax.shard_map(
        local,
        mesh=mesh,
        in_specs=placed,
        out_specs=(
            P("dp", "tensor", None),
            P("dp", "tensor", None),
            P("dp", "tensor"),
            P("dp", "tensor"),
            P(),
        ),
        check_vma=False,
    )
```

```python
import functools

import jax
import jax.numpy as jnp
from jax import lax
from jax.experimental import pallas as pl
from jax.experimental.pallas import tpu as pltpu
from jax.sharding import PartitionSpec as P

MESH = pl.DeviceIdType.MESH
ROW_DIMS = (((1,), (1,)), ((), ()))
RING = 4
RANKS = RING * RING
F32 = jnp.float32
BF16 = jnp.bfloat16

STEP = (0, -1, 1, 2)


def round_up(value, unit):
    return (value + unit - 1) // unit * unit


def chunk_of(width, limit):
    tiles = width // 128
    best = 1
    for count in range(1, tiles + 1):
        if tiles % count == 0 and count * 128 <= limit:
            best = count
    return best * 128


class Sizes:
    def __init__(self, tokens, fc1, out_grad):
        self.homes, self.block_rows, self.width = tokens
        self.units = fc1[1]
        self.slots = out_grad[0]
        self.own = self.slots * self.block_rows
        self.pair = 2 * self.own
        self.rows = RING * self.pair
        self.owned = self.width // RANKS
        self.owned_pad = round_up(self.owned, 16)
        self.group = RING * self.owned
        self.group_step = self.group // 128 * 128
        self.group_pad = round_up(self.group + (RING - 1) * (self.group - self.group_step), 128)
        self.sum_rows = self.group_pad + 8
        self.chunk = chunk_of(self.width, 640)
        first = round_up(self.units // 2, 128) - 128
        self.parts = ((0, first), (first, self.units - first))
        self.part_max = max(count for _, count in self.parts)


def kernel(
    sz,
    copies,
    slot_ref,
    gain_ref,
    tokens_hbm,
    fc1_hbm,
    fc2_hbm,
    grad_hbm,
    mixed_ref,
    tgrad_ref,
    fc1_grad_ref,
    fc2_grad_ref,
    gain_grad_ref,
    fc1_ref,
    fc2_ref,
    arrived,
    row_in,
    inv_ref,
    grad_all,
    norm_all,
    norm_cut,
    grad_sl,
    norm_sl,
    grad_t,
    norm_t,
    hid_g,
    pre_g,
    hid_n,
    pre_n,
    pre_act,
    hid_grad,
    row_sum,
    sib_out,
    sib_in,
    rs_out,
    rs_in,
    wg_sum,
    wg_out,
    wg_in,
    back_out,
    input_grad,
    gain_sib,
    gain_x,
    gain_y,
    gain_z,
    local_sems,
    send_sems,
    recv_sems,
):
    dp = lax.axis_index("dp")
    t = lax.axis_index("tensor")
    y, z = dp // RING, dp % RING
    x, c = t // 2, t % 2
    own, width = sz.own, sz.width
    half = own // 2
    gain = gain_ref[...].reshape(1, width)

    def on_dp(k):
        return ((dp + k + RANKS) % RANKS, t)

    def on_x(k):
        return (dp, ((x + k + RING) % RING) * 2 + c)

    def on_y(k):
        return (((y + k + RING) % RING) * RING + z, t)

    def on_z(k):
        return (y * RING + (z + k + RING) % RING, t)

    sibling = (dp, t + 1 - 2 * c)

    started = []

    def send(src, dst, device):
        index = len(started)
        made = pltpu.make_async_remote_copy(
            src_ref=src,
            dst_ref=dst,
            send_sem=send_sems.at[index],
            recv_sem=recv_sems.at[index],
            device_id=device,
            device_id_type=MESH,
        )
        made.start()
        started.append(made)
        return made

    my_rows = pl.ds(pl.multiple_of(c * own, own), own)
    load_grad = pltpu.make_async_copy(grad_hbm, grad_all.at[my_rows], local_sems.at[0])
    load_token = pltpu.make_async_copy(tokens_hbm.at[0], arrived.at[0], local_sems.at[1])
    load_fc2 = pltpu.make_async_copy(fc2_hbm, fc2_ref, local_sems.at[2])
    load_fc1 = pltpu.make_async_copy(fc1_hbm, fc1_ref, local_sems.at[3])
    load_grad.start()
    load_token.start()
    load_fc2.start()
    load_fc1.start()

    partners = [on_dp(k) for k in range(1, sz.homes)]
    partners += [on_dp(-k) for k in range(1, sz.homes)]
    partners += [on_y(k) for k in (1, -1, 2)]
    partners += [on_z(k) for k in (1, -1, 2)]
    partners += [on_x(k) for k in (1, -1, 2)]
    partners += [sibling]
    barrier = pltpu.get_barrier_semaphore()
    for device in partners:
        pl.semaphore_signal(barrier, inc=1, device_id=device, device_id_type=MESH)
    pl.semaphore_wait(barrier, len(partners))

    class RowGather:
        def __init__(self, view):
            self.view = view

        def part(self, slot, lo, count):
            place = sz.pair * slot + c * own + lo
            return self.view(pl.ds(pl.multiple_of(place, 16), count))

        def start(self):
            mine = self.part(0, 0, own)
            self.right = send(mine, self.part(1, 0, own), on_x(1))
            self.left = send(mine, self.part(2, 0, own), on_x(-1))
            self.shared = [send(mine, mine, sibling)]

        def forward(self):
            self.right.wait_recv()
            self.right2 = send(self.part(1, 0, half), self.part(3, 0, half), on_x(1))
            whole = self.part(1, 0, own)
            self.shared.append(send(whole, whole, sibling))
            self.left.wait_recv()
            rest = own - half
            self.left2 = send(self.part(2, half, rest), self.part(3, half, rest), on_x(-1))
            whole = self.part(2, 0, own)
            self.shared.append(send(whole, whole, sibling))

        def finish(self):
            self.right2.wait_recv()
            low = self.part(3, 0, half)
            self.shared.append(send(low, low, sibling))
            self.left2.wait_recv()
            high = self.part(3, half, own - half)
            self.shared.append(send(high, high, sibling))
            for made in self.shared:
                made.wait_recv()

    class RingGather:
        def __init__(self, buf, lo, count, on_axis):
            self.buf, self.on_axis = buf, on_axis
            self.whole = pl.ds(lo, count)
            self.low = pl.ds(lo, count // 2)
            self.high = pl.ds(lo + count // 2, count // 2)

        def start(self):
            buf, on_axis = self.buf, self.on_axis
            mine = buf.at[0, self.whole]
            self.right = send(mine, buf.at[1, self.whole], on_axis(1))
            self.left = send(mine, buf.at[2, self.whole], on_axis(-1))

        def forward(self):
            buf, on_axis = self.buf, self.on_axis
            self.right.wait_recv()
            self.right2 = send(buf.at[1, self.low], buf.at[3, self.low], on_axis(1))
            self.left.wait_recv()
            self.left2 = send(buf.at[2, self.high], buf.at[3, self.high], on_axis(-1))

        def finish(self):
            self.right2.wait_recv()
            self.left2.wait_recv()

    class RingReduce:
        def __init__(self, part, out, into, on_axis, mid, count):
            self.part, self.out, self.into = part, out, into
            self.on_axis, self.mid, self.count = on_axis, mid, count

        def start(self):
            mid, rest = self.mid, self.count - self.mid
            lo, hi = pl.ds(0, mid), pl.ds(mid, rest)
            part, out, into, on_axis = self.part, self.out, self.into, self.on_axis
            out[0, lo] = part(3, 0, mid).astype(BF16)
            self.far_right = send(out.at[0, lo], into.at[0, lo], on_axis(1))
            out[0, hi] = part(3, mid, rest).astype(BF16)
            self.far_left = send(out.at[0, hi], into.at[0, hi], on_axis(-1))
            out[1, hi] = part(2, mid, rest).astype(BF16)
            self.near_right = send(out.at[1, hi], into.at[1, hi], on_axis(1))
            out[2, lo] = part(1, 0, mid).astype(BF16)
            self.near_left = send(out.at[2, lo], into.at[2, lo], on_axis(-1))

        def forward(self):
            mid, rest = self.mid, self.count - self.mid
            lo, hi = pl.ds(0, mid), pl.ds(mid, rest)
            part, out, into, on_axis = self.part, self.out, self.into, self.on_axis
            self.far_right.wait_recv()
            out[1, lo] = (part(2, 0, mid) + into[0, lo].astype(F32)).astype(BF16)
            self.sum_right = send(out.at[1, lo], into.at[1, lo], on_axis(1))
            self.far_left.wait_recv()
            out[2, hi] = (part(1, mid, rest) + into[0, hi].astype(F32)).astype(BF16)
            self.sum_left = send(out.at[2, hi], into.at[2, hi], on_axis(-1))

        def finish(self):
            self.near_right.wait_recv()
            self.near_left.wait_recv()
            self.sum_right.wait_recv()
            self.sum_left.wait_recv()

        def total(self):
            first = self.part(0, 0, self.count) + self.into[1].astype(F32)
            return first + self.into[2].astype(F32)

    class RowReduce:
        def __init__(self, index):
            self.index = index

        def multiply(self, lhs, weight, also=None):
            index = self.index

            @pl.loop(0, width // sz.chunk)
            def _(n):
                cols = pl.ds(pl.multiple_of(n * sz.chunk, sz.chunk), sz.chunk)
                full = jnp.dot(lhs[...], weight[:, cols], preferred_element_type=F32)
                for k in range(RING):
                    even = full[sz.pair * k : sz.pair * k + own]
                    odd = full[sz.pair * k + own : sz.pair * (k + 1)]
                    row_sum[index, k, :, cols] = jnp.where(c == 0, even, odd)
                    sib_out[index, k, :, cols] = jnp.where(c == 0, odd, even).astype(BF16)
                if also is not None:
                    also(cols, full)

            self.copy = send(sib_out.at[index], sib_in.at[index], sibling)

        def start(self):
            index = self.index
            self.copy.wait_recv()
            row_sum[index] = row_sum[index] + sib_in[index].astype(F32)

            def part(k, lo, count):
                return row_sum[index, k, lo : lo + count]

            self.ring = RingReduce(part, rs_out.at[index], rs_in.at[index], on_x, half, own)
            self.ring.start()

    class WeightGrad:
        def __init__(self, index, p, slices, blocks, on_axis, owner_row, out):
            self.index, self.p, self.out = index, p, out
            self.slices, self.blocks = slices, blocks
            self.lo, self.units = sz.parts[p]
            self.on_axis, self.owner_row = on_axis, owner_row

        def multiply(self):
            index, p, lo, units = self.index, self.p, self.lo, self.units
            step = sz.group_pad // RING

            @pl.loop(0, RING)
            def _(m):
                rows = pl.ds(pl.multiple_of(m * step, step), step)
                total = None
                for k in range(RING):
                    one = lax.dot_general(
                        self.slices[k, rows, :],
                        self.blocks[k, lo : lo + units, :],
                        ROW_DIMS,
                        preferred_element_type=F32,
                    )
                    total = one if total is None else total + one
                wg_sum[index, p, rows, 0:units] = total

            wg_sum[index, p, sz.group_pad : sz.sum_rows, 0:units] = jnp.zeros((8, units), F32)

            def part(k, first, count):
                place = pl.multiple_of(self.owner_row(k) + first, 8)
                return wg_sum[index, p, pl.ds(place, count), 0:units]

            self.ring = RingReduce(
                part,
                wg_out.at[index, p, :, :, pl.ds(0, units)],
                wg_in.at[index, p, :, :, pl.ds(0, units)],
                self.on_axis,
                round_up(sz.owned_pad // 2, 16),
                sz.owned_pad,
            )
            self.ring.start()

        def finish(self):
            self.ring.finish()
            self.out[:, self.lo : self.lo + self.units] = self.ring.total()[: sz.owned]

    grad_rows = RowGather(lambda rows: grad_all.at[rows])
    norm_rows = RowGather(lambda rows: norm_all.at[rows])
    cut_rows = RowGather(lambda rows: norm_sl.at[pl.ds(1, RING - 1), rows])
    routed = [send(tokens_hbm.at[j], arrived.at[j], on_dp(j)) for j in range(1, sz.homes)]
    load_grad.wait()
    grad_rows.start()

    def pick(s, j):
        home = (dp - j + RANKS) % RANKS
        named = slot_ref[home * sz.homes + j]
        return jnp.where(named == dp * sz.slots + s, 1.0, 0.0).astype(F32)

    def group_columns(rows, q):
        cuts = []
        for k in range(RING):
            first = sz.owned * (RING * k + q)
            cuts.append(rows[:, first : first + sz.owned])
        cuts.append(jnp.zeros((rows.shape[0], sz.group_pad - sz.group), rows.dtype))
        return jnp.concatenate(cuts, axis=1)

    load_token.wait()
    for made in routed:
        made.wait_recv()
    for s in range(sz.slots):
        total = pick(s, 0) * arrived[0].astype(F32)
        for j in range(1, sz.homes):
            total += pick(s, j) * arrived[j].astype(F32)
        row_in[s * sz.block_rows : (s + 1) * sz.block_rows, :] = total
    rows_f = row_in[...]
    inv = lax.rsqrt(jnp.mean(rows_f * rows_f, axis=-1, keepdims=True) + 1e-06)
    inv_ref[...] = jnp.broadcast_to(inv, inv_ref.shape)
    norm_own = (rows_f * inv * gain).astype(BF16)
    norm_all[my_rows, :] = norm_own
    norm_rows.start()
    grad_rows.forward()
    for q in range(RING):
        norm_cut[q] = group_columns(norm_own, q)
    cut_sent = []
    for k, slot in ((1, 1), (-1, 2), (2, 3)):
        cut_sent.append(
            send(norm_cut.at[(z + k + RING) % RING], norm_sl.at[slot, my_rows], on_z(k))
        )

    grad_rows.finish()
    side = sz.rows // 2
    side_rows = pl.ds(pl.multiple_of(c * side, side), side)
    slice_sent = []
    for k, slot in ((1, 1), (-1, 2), (2, 3)):
        first = pl.multiple_of(((y + k + RING) % RING) * sz.group_step, 128)
        slice_sent.append(
            send(
                grad_all.at[side_rows, pl.ds(first, sz.group_pad)],
                grad_sl.at[slot, side_rows],
                on_y(k),
            )
        )

    load_fc2.wait()

    def multiply_in(lhs, lo, count, rows, out):
        @pl.loop(0, width // sz.chunk)
        def _(n):
            cols = pl.ds(pl.multiple_of(n * sz.chunk, sz.chunk), sz.chunk)
            part = lax.dot_general(
                lhs[lo : lo + count, cols], rows[:, cols], ROW_DIMS, preferred_element_type=F32
            )

            @pl.when(n == 0)
            def _():
                out[lo : lo + count, :] = part

            @pl.when(n > 0)
            def _():
                out[lo : lo + count, :] += part

    multiply_in(fc2_ref, *sz.parts[0], grad_all, hid_grad)
    norm_rows.forward()
    multiply_in(fc2_ref, *sz.parts[1], grad_all, hid_grad)
    own_first = pl.multiple_of(y * sz.group_step, 128)
    grad_t[0] = grad_all[:, pl.ds(own_first, sz.group_pad)].T
    load_fc1.wait()
    norm_rows.finish()
    for made in cut_sent:
        made.wait_recv()
    cut_rows.start()

    hid_ring, pre_ring = [], []
    for lo, count in sz.parts:
        multiply_in(fc1_ref, lo, count, norm_all, pre_act)

        @pl.loop(0, count // 32)
        def _(n):
            rows = pl.ds(pl.multiple_of(lo + n * 32, 32), 32)
            value = pre_act[rows, :]
            cdf = 0.5 * (1.0 + lax.erf(value * 0.7071067811865476))
            slope = cdf + value * jnp.exp(-0.5 * value * value) * 0.3989422804014327
            hid_g[0, rows, :] = (value * cdf).astype(BF16)
            pre_g[0, rows, :] = (hid_grad[rows, :] * slope).astype(BF16)

        hid_ring.append(RingGather(hid_g, lo, count, on_y))
        pre_ring.append(RingGather(pre_g, lo, count, on_z))
        hid_ring[-1].start()
        pre_ring[-1].start()

    slice_shared = []
    for slot, made in zip((1, 2, 3), slice_sent):
        made.wait_recv()
        place = grad_sl.at[slot, side_rows]
        slice_shared.append(send(place, place, sibling))
    cut_rows.forward()
    hid_ring[0].forward()
    pre_ring[0].forward()

    back = RowReduce(1)
    branch = RowReduce(0)
    pre_n[...] = pre_g[0].T

    def gain_part(cols, full):
        product = full * norm_all[:, cols].astype(F32)
        gain_sib[0, :, cols] = jnp.sum(product, axis=0, keepdims=True)

    back.multiply(pre_n, fc1_ref, gain_part)
    gain_pair = send(gain_sib.at[0], gain_sib.at[1], sibling)
    cut_rows.finish()
    hid_ring[1].forward()
    pre_ring[1].forward()
    back.start()
    hid_n[...] = hid_g[0].T
    branch.multiply(hid_n, fc2_ref)
    for made in slice_shared:
        made.wait_recv()
    for k in range(1, RING):
        grad_t[k] = grad_sl[k].T

    def add_start(buf, me, on_axis, total):
        buf[me] = total
        return [send(buf.at[me], buf.at[me], on_axis(k)) for k in (1, -1, 2)]

    def add_finish(buf, made):
        for one in made:
            one.wait_recv()
        return buf[0] + buf[1] + buf[2] + buf[3]

    gain_pair.wait_recv()
    adding = add_start(gain_x, x, on_x, gain_sib[0] + gain_sib[1])
    back.ring.forward()
    branch.start()

    def fc2_row(k):
        return y * (sz.group - sz.group_step) + ((z + STEP[k] + RING) % RING) * sz.owned

    def fc1_row(k):
        return ((y + STEP[k] + RING) % RING) * sz.owned

    fc2_grad = [
        WeightGrad(0, p, grad_t, hid_g, on_z, fc2_row, fc2_grad_ref) for p in range(2)
    ]
    fc1_grad = [
        WeightGrad(1, p, norm_t, pre_g, on_y, fc1_row, fc1_grad_ref) for p in range(2)
    ]
    hid_ring[0].finish()
    fc2_grad[0].multiply()

    for q in range(RING):

        @pl.when(z == q)
        def _():
            norm_t[0] = group_columns(norm_all[...], q).T

    for k in range(1, RING):
        norm_t[k] = norm_sl[k].T
    pre_ring[0].finish()
    fc1_grad[0].multiply()
    branch.ring.forward()
    back.ring.finish()

    normed_grad = back.ring.total()
    unit = row_in[...] * inv_ref[:, :1]
    scaled = normed_grad * gain
    inner = scaled - unit * jnp.mean(scaled * unit, axis=-1, keepdims=True)
    input_grad[...] = (
        (grad_all[my_rows, :].astype(F32) + inv_ref[:, :1] * inner).astype(BF16).astype(F32)
    )
    returned = []
    for j in range(sz.homes):
        total = pick(0, j) * input_grad[0 : sz.block_rows, :]
        for s in range(1, sz.slots):
            total += pick(s, j) * input_grad[s * sz.block_rows : (s + 1) * sz.block_rows, :]
        if j == 0:
            tgrad_ref[0] = total.astype(BF16)
        else:
            back_out[j - 1] = total.astype(BF16)
            returned.append(send(back_out.at[j - 1], tgrad_ref.at[j], on_dp(-j)))

    total = add_finish(gain_x, adding)
    adding = add_start(gain_y, y, on_y, total)
    fc2_grad[0].ring.forward()
    hid_ring[1].finish()
    fc2_grad[1].multiply()
    fc1_grad[0].ring.forward()
    pre_ring[1].finish()
    fc1_grad[1].multiply()
    total = add_finish(gain_y, adding)
    adding = add_start(gain_z, z, on_z, total)
    branch.ring.finish()
    mixed_ref[...] = (row_in[...] + branch.ring.total()).astype(BF16)
    fc2_grad[0].finish()
    fc2_grad[1].ring.forward()
    fc1_grad[0].finish()
    fc1_grad[1].ring.forward()
    total = add_finish(gain_z, adding)
    gain_grad_ref[...] = (total / gain).reshape(width)
    fc2_grad[1].finish()
    fc1_grad[1].finish()
    for made in returned:
        made.wait_recv()
    for made in started:
        made.wait_send()
    if len(started) != copies:
        raise ValueError(len(started))


def hand_over_kernel(*refs):
    count = len(refs) // 2
    sems = refs[-1]
    made = [
        pltpu.make_async_copy(refs[i], refs[count + i], sems.at[i]) for i in range(count)
    ]
    for one in made:
        one.start()
    for one in made:
        one.wait()


def hand_over(*arrays):
    anywhere = pl.BlockSpec(memory_space=pl.ANY)
    return pl.pallas_call(
        hand_over_kernel,
        out_shape=tuple(jax.ShapeDtypeStruct(a.shape, a.dtype) for a in arrays),
        in_specs=[anywhere] * len(arrays),
        out_specs=(pl.BlockSpec(memory_space=pltpu.VMEM),) * len(arrays),
        scratch_shapes=[pltpu.SemaphoreType.DMA((len(arrays),))],
        compiler_params=pltpu.CompilerParams(vmem_limit_bytes=60 * 1024 * 1024),
        name="hand_over",
    )(*arrays)


COPIES = 108


def local(tokens, norm_gain, fc1, fc2t, block_slot, out_grad):
    sz = Sizes(tokens.shape, fc1.shape, out_grad.shape)
    width, units = sz.width, sz.units
    vmem = pl.BlockSpec(memory_space=pltpu.VMEM)
    anywhere = pl.BlockSpec(memory_space=pl.ANY)
    slices = (RING, sz.rows, sz.group_pad)
    slices_t = (RING, sz.group_pad, sz.rows)
    pieces = (2, 2, 3, sz.owned_pad, sz.part_max)
    arrays = pl.pallas_call(
        functools.partial(kernel, sz, COPIES),
        out_shape=(
            jax.ShapeDtypeStruct((sz.own, width), BF16),
            jax.ShapeDtypeStruct(tokens.shape, BF16),
            jax.ShapeDtypeStruct((sz.owned, units), F32),
            jax.ShapeDtypeStruct((sz.owned, units), F32),
            jax.ShapeDtypeStruct((width,), F32),
        ),
        in_specs=[
            pl.BlockSpec(memory_space=pltpu.SMEM),
            vmem,
            anywhere,
            anywhere,
            anywhere,
            anywhere,
        ],
        out_specs=(vmem,) * 5,
        scratch_shapes=[
            pltpu.VMEM((units, width), BF16),
            pltpu.VMEM((units, width), BF16),
            pltpu.VMEM(tokens.shape, BF16),
            pltpu.VMEM((sz.own, width), F32),
            pltpu.VMEM((sz.own, 128), F32),
            pltpu.VMEM((sz.rows, width), BF16),
            pltpu.VMEM((sz.rows, width), BF16),
            pltpu.VMEM((RING, sz.own, sz.group_pad), BF16),
            pltpu.VMEM(slices, BF16),
            pltpu.VMEM(slices, BF16),
            pltpu.VMEM(slices_t, BF16),
            pltpu.VMEM(slices_t, BF16),
            pltpu.VMEM((RING, units, sz.rows), BF16),
            pltpu.VMEM((RING, units, sz.rows), BF16),
            pltpu.VMEM((sz.rows, units), BF16),
            pltpu.VMEM((sz.rows, units), BF16),
            pltpu.VMEM((units, sz.rows), F32),
            pltpu.VMEM((units, sz.rows), F32),
            pltpu.VMEM((2, RING, sz.own, width), F32),
            pltpu.VMEM((2, RING, sz.own, width), BF16),
            pltpu.VMEM((2, RING, sz.own, width), BF16),
            pltpu.VMEM((2, 3, sz.own, width), BF16),
            pltpu.VMEM((2, 3, sz.own, width), BF16),
            pltpu.VMEM((2, 2, sz.sum_rows, sz.part_max), F32),
            pltpu.VMEM(pieces, BF16),
            pltpu.VMEM(pieces, BF16),
            pltpu.VMEM((sz.homes - 1, sz.block_rows, width), BF16),
            pltpu.VMEM((sz.own, width), F32),
            pltpu.VMEM((2, 1, width), F32),
            pltpu.VMEM((RING, 1, width), F32),
            pltpu.VMEM((RING, 1, width), F32),
            pltpu.VMEM((RING, 1, width), F32),
            pltpu.SemaphoreType.DMA((4,)),
            pltpu.SemaphoreType.DMA((COPIES,)),
            pltpu.SemaphoreType.DMA((COPIES,)),
        ],
        compiler_params=pltpu.CompilerParams(
            collective_id=0, has_side_effects=True, vmem_limit_bytes=60 * 1024 * 1024
        ),
        cost_estimate=pl.CostEstimate(
            flops=12 * sz.rows * width * units,
            bytes_accessed=4 * width * units,
            transcendentals=2 * sz.rows * units,
        ),
        name="mlp_block",
    )(
        block_slot,
        norm_gain,
        tokens,
        fc1.T,
        fc2t.T,
        out_grad.reshape(sz.own, width),
    )
    mixed, tgrad, fc1_grad, fc2_grad, gain_grad = hand_over(*arrays)
    return mixed.reshape(out_grad.shape), tgrad, fc1_grad, fc2_grad, gain_grad


def solution(mesh):
    placed = (
        P("dp", "tensor", None),
        P(),
        P(None, "tensor"),
        P(None, "tensor"),
        P(),
        P("dp", "tensor", None),
    )
    return jax.shard_map(
        local,
        mesh=mesh,
        in_specs=placed,
        out_specs=(
            P("dp", "tensor", None),
            P("dp", "tensor", None),
            P("dp", "tensor"),
            P("dp", "tensor"),
            P(),
        ),
        check_vma=False,
    )
```

```python
import functools

import jax
import jax.numpy as jnp
from jax import lax
from jax.experimental import pallas as pl
from jax.experimental.pallas import tpu as pltpu
from jax.sharding import PartitionSpec as P

MESH = pl.DeviceIdType.MESH
ROW_DIMS = (((1,), (1,)), ((), ()))
RING = 4
RANKS = RING * RING
F32 = jnp.float32
BF16 = jnp.bfloat16

STEP = (0, -1, 1, 2)


def round_up(value, unit):
    return (value + unit - 1) // unit * unit


def chunk_of(width, limit):
    tiles = width // 128
    best = 1
    for count in range(1, tiles + 1):
        if tiles % count == 0 and count * 128 <= limit:
            best = count
    return best * 128


class Sizes:
    def __init__(self, tokens, fc1, out_grad):
        self.homes, self.block_rows, self.width = tokens
        self.units = fc1[1]
        self.slots = out_grad[0]
        self.own = self.slots * self.block_rows
        self.pair = 2 * self.own
        self.rows = RING * self.pair
        self.owned = self.width // RANKS
        self.owned_pad = round_up(self.owned, 16)
        self.group = RING * self.owned
        self.group_step = self.group // 128 * 128
        self.group_pad = round_up(self.group + (RING - 1) * (self.group - self.group_step), 128)
        self.sum_rows = self.group_pad + 8
        self.chunk = chunk_of(self.width, 640)
        first = round_up(self.units // 2, 128) - 128
        self.parts = ((0, first), (first, self.units - first))
        mid = round_up(self.width // 2, 128)
        self.cuts = ((0, mid), (mid, self.width - mid))
        self.part_max = max(count for _, count in self.parts)


def kernel(
    sz,
    copies,
    slot_ref,
    gain_ref,
    tokens_hbm,
    fc1_hbm,
    fc2_hbm,
    grad_hbm,
    mixed_ref,
    tgrad_ref,
    fc1_grad_ref,
    fc2_grad_ref,
    gain_grad_ref,
    fc1_ref,
    fc2_ref,
    arrived,
    row_all,
    inv_ref,
    grad_all,
    norm_all,
    norm_cut,
    grad_sl,
    norm_sl,
    grad_t,
    norm_t,
    hid_g,
    pre_g,
    hid_n,
    pre_n,
    pre_act,
    hid_grad,
    row_sum,
    sib_out,
    sib_in,
    rs_out,
    rs_in,
    wg_sum,
    wg_out,
    wg_in,
    back_out,
    input_grad,
    gain_sib,
    gain_x,
    gain_y,
    gain_z,
    local_sems,
    send_sems,
    recv_sems,
):
    dp = lax.axis_index("dp")
    t = lax.axis_index("tensor")
    y, z = dp // RING, dp % RING
    x, c = t // 2, t % 2
    own, width = sz.own, sz.width
    half = own // 2
    gain = gain_ref[...].reshape(1, width)

    def on_dp(k):
        return ((dp + k + RANKS) % RANKS, t)

    def on_x(k):
        return (dp, ((x + k + RING) % RING) * 2 + c)

    def on_y(k):
        return (((y + k + RING) % RING) * RING + z, t)

    def on_z(k):
        return (y * RING + (z + k + RING) % RING, t)

    sibling = (dp, t + 1 - 2 * c)

    started = []

    def send(src, dst, device):
        index = len(started)
        made = pltpu.make_async_remote_copy(
            src_ref=src,
            dst_ref=dst,
            send_sem=send_sems.at[index],
            recv_sem=recv_sems.at[index],
            device_id=device,
            device_id_type=MESH,
        )
        made.start()
        started.append(made)
        return made

    my_rows = pl.ds(pl.multiple_of(c * own, own), own)
    load_grad = pltpu.make_async_copy(grad_hbm, grad_all.at[my_rows], local_sems.at[0])
    load_token = pltpu.make_async_copy(tokens_hbm.at[0], arrived.at[0], local_sems.at[1])
    load_fc2 = pltpu.make_async_copy(fc2_hbm, fc2_ref, local_sems.at[2])
    load_fc1 = pltpu.make_async_copy(fc1_hbm, fc1_ref, local_sems.at[3])
    load_grad.start()
    load_token.start()
    load_fc2.start()
    load_fc1.start()

    partners = [on_dp(k) for k in range(1, sz.homes)]
    partners += [on_dp(-k) for k in range(1, sz.homes)]
    partners += [on_y(k) for k in (1, -1, 2)]
    partners += [on_z(k) for k in (1, -1, 2)]
    partners += [on_x(k) for k in (1, -1, 2)]
    partners += [sibling]
    barrier = pltpu.get_barrier_semaphore()
    for device in partners:
        pl.semaphore_signal(barrier, inc=1, device_id=device, device_id_type=MESH)
    pl.semaphore_wait(barrier, len(partners))

    class RowGather:
        def __init__(self, view):
            self.view = view

        def part(self, slot, lo, count):
            place = sz.pair * slot + c * own + lo
            return self.view(pl.ds(pl.multiple_of(place, 16), count))

        def start(self):
            mine = self.part(0, 0, own)
            self.right = send(mine, self.part(1, 0, own), on_x(1))
            self.left = send(mine, self.part(2, 0, own), on_x(-1))
            self.shared = [send(mine, mine, sibling)]

        def forward(self):
            self.right.wait_recv()
            self.right2 = send(self.part(1, 0, half), self.part(3, 0, half), on_x(1))
            whole = self.part(1, 0, own)
            self.shared.append(send(whole, whole, sibling))
            self.left.wait_recv()
            rest = own - half
            self.left2 = send(self.part(2, half, rest), self.part(3, half, rest), on_x(-1))
            whole = self.part(2, 0, own)
            self.shared.append(send(whole, whole, sibling))

        def finish(self):
            self.right2.wait_recv()
            low = self.part(3, 0, half)
            self.shared.append(send(low, low, sibling))
            self.left2.wait_recv()
            high = self.part(3, half, own - half)
            self.shared.append(send(high, high, sibling))
            for made in self.shared:
                made.wait_recv()

    class RingGather:
        def __init__(self, buf, lo, count, on_axis):
            self.buf, self.on_axis = buf, on_axis
            self.whole = pl.ds(lo, count)
            self.low = pl.ds(lo, count // 2)
            self.high = pl.ds(lo + count // 2, count // 2)

        def start(self):
            buf, on_axis = self.buf, self.on_axis
            mine = buf.at[0, self.whole]
            self.right = send(mine, buf.at[1, self.whole], on_axis(1))
            self.left = send(mine, buf.at[2, self.whole], on_axis(-1))

        def forward(self):
            buf, on_axis = self.buf, self.on_axis
            self.right.wait_recv()
            self.right2 = send(buf.at[1, self.low], buf.at[3, self.low], on_axis(1))
            self.left.wait_recv()
            self.left2 = send(buf.at[2, self.high], buf.at[3, self.high], on_axis(-1))

        def finish(self):
            self.right2.wait_recv()
            self.left2.wait_recv()

    class RingReduce:
        def __init__(self, part, out, into, on_axis, mid, count):
            self.part, self.out, self.into = part, out, into
            self.on_axis, self.mid, self.count = on_axis, mid, count

        def start(self):
            mid, rest = self.mid, self.count - self.mid
            lo, hi = pl.ds(0, mid), pl.ds(mid, rest)
            part, out, into, on_axis = self.part, self.out, self.into, self.on_axis
            out[0, lo] = part(3, 0, mid).astype(BF16)
            self.far_right = send(out.at[0, lo], into.at[0, lo], on_axis(1))
            out[0, hi] = part(3, mid, rest).astype(BF16)
            self.far_left = send(out.at[0, hi], into.at[0, hi], on_axis(-1))
            out[1, hi] = part(2, mid, rest).astype(BF16)
            self.near_right = send(out.at[1, hi], into.at[1, hi], on_axis(1))
            out[2, lo] = part(1, 0, mid).astype(BF16)
            self.near_left = send(out.at[2, lo], into.at[2, lo], on_axis(-1))

        def forward(self):
            mid, rest = self.mid, self.count - self.mid
            lo, hi = pl.ds(0, mid), pl.ds(mid, rest)
            part, out, into, on_axis = self.part, self.out, self.into, self.on_axis
            self.far_right.wait_recv()
            out[1, lo] = (part(2, 0, mid) + into[0, lo].astype(F32)).astype(BF16)
            self.sum_right = send(out.at[1, lo], into.at[1, lo], on_axis(1))
            self.far_left.wait_recv()
            out[2, hi] = (part(1, mid, rest) + into[0, hi].astype(F32)).astype(BF16)
            self.sum_left = send(out.at[2, hi], into.at[2, hi], on_axis(-1))

        def finish(self):
            self.near_right.wait_recv()
            self.near_left.wait_recv()
            self.sum_right.wait_recv()
            self.sum_left.wait_recv()

        def total(self):
            first = self.part(0, 0, self.count) + self.into[1].astype(F32)
            return first + self.into[2].astype(F32)

    class RowReduce:
        def __init__(self, index):
            self.index = index

        def multiply(self, lhs, weight, also=None):
            index = self.index

            @pl.loop(0, width // sz.chunk)
            def _(n):
                cols = pl.ds(pl.multiple_of(n * sz.chunk, sz.chunk), sz.chunk)
                full = jnp.dot(lhs[...], weight[:, cols], preferred_element_type=F32)
                for k in range(RING):
                    even = full[sz.pair * k : sz.pair * k + own]
                    odd = full[sz.pair * k + own : sz.pair * (k + 1)]
                    row_sum[index, k, :, cols] = jnp.where(c == 0, even, odd)
                    sib_out[index, k, :, cols] = jnp.where(c == 0, odd, even).astype(BF16)
                if also is not None:
                    also(cols, full)

            self.copy = send(sib_out.at[index], sib_in.at[index], sibling)

        def start(self):
            index = self.index
            self.copy.wait_recv()
            row_sum[index] = row_sum[index] + sib_in[index].astype(F32)

            def part(k, lo, count):
                return row_sum[index, k, lo : lo + count]

            self.ring = RingReduce(part, rs_out.at[index], rs_in.at[index], on_x, half, own)
            self.ring.start()

    class WeightGrad:
        def __init__(self, index, p, slices, blocks, on_axis, owner_row, out):
            self.index, self.p, self.out = index, p, out
            self.slices, self.blocks = slices, blocks
            self.lo, self.units = sz.parts[p]
            self.on_axis, self.owner_row = on_axis, owner_row

        def multiply(self):
            index, p, lo, units = self.index, self.p, self.lo, self.units
            step = sz.group_pad // RING

            @pl.loop(0, RING)
            def _(m):
                rows = pl.ds(pl.multiple_of(m * step, step), step)
                total = None
                for k in range(RING):
                    one = lax.dot_general(
                        self.slices[k, rows, :],
                        self.blocks[k, lo : lo + units, :],
                        ROW_DIMS,
                        preferred_element_type=F32,
                    )
                    total = one if total is None else total + one
                wg_sum[index, p, rows, 0:units] = total

            wg_sum[index, p, sz.group_pad : sz.sum_rows, 0:units] = jnp.zeros((8, units), F32)

            def part(k, first, count):
                place = pl.multiple_of(self.owner_row(k) + first, 8)
                return wg_sum[index, p, pl.ds(place, count), 0:units]

            self.ring = RingReduce(
                part,
                wg_out.at[index, p, :, :, pl.ds(0, units)],
                wg_in.at[index, p, :, :, pl.ds(0, units)],
                self.on_axis,
                round_up(sz.owned_pad // 2, 16),
                sz.owned_pad,
            )
            self.ring.start()

        def finish(self):
            self.ring.finish()
            self.out[:, self.lo : self.lo + self.units] = self.ring.total()[: sz.owned]

    grad_rows = RowGather(lambda rows: grad_all.at[rows])
    cut_rows = RowGather(lambda rows: norm_sl.at[pl.ds(1, RING - 1), rows])
    routed = []
    for lo, count in sz.cuts:
        cols = pl.ds(lo, count)
        for j in range(1, sz.homes):
            routed.append(send(tokens_hbm.at[j, :, cols], arrived.at[j, :, cols], on_dp(j)))
    load_grad.wait()
    grad_rows.start()

    def pick(s, j):
        home = (dp - j + RANKS) % RANKS
        named = slot_ref[home * sz.homes + j]
        return jnp.where(named == dp * sz.slots + s, 1.0, 0.0).astype(F32)

    def group_columns(rows, q):
        cuts = []
        for k in range(RING):
            first = sz.owned * (RING * k + q)
            cuts.append(rows[:, first : first + sz.owned])
        cuts.append(jnp.zeros((rows.shape[0], sz.group_pad - sz.group), rows.dtype))
        return jnp.concatenate(cuts, axis=1)

    load_token.wait()
    row_parts = []
    for n, (lo, count) in enumerate(sz.cuts):
        cols = slice(lo, lo + count)
        for made in routed[n * (sz.homes - 1) : (n + 1) * (sz.homes - 1)]:
            made.wait_recv()
        for s in range(sz.slots):
            total = pick(s, 0) * arrived[0, :, cols].astype(F32)
            for j in range(1, sz.homes):
                total += pick(s, j) * arrived[j, :, cols].astype(F32)
            place = c * own + s * sz.block_rows
            rows = pl.ds(pl.multiple_of(place, sz.block_rows), sz.block_rows)
            row_all[rows, cols] = total.astype(BF16)
        one = RowGather(lambda rows, lo=lo, count=count: row_all.at[rows, pl.ds(lo, count)])
        one.start()
        row_parts.append(one)
        if n == 0:
            grad_rows.forward()

    def normed_rows(rows):
        value = row_all[rows, :].astype(F32)
        inv = lax.rsqrt(jnp.mean(value * value, axis=-1, keepdims=True) + 1e-06)
        return value * inv, inv

    unit_own, inv = normed_rows(my_rows)
    inv_ref[...] = jnp.broadcast_to(inv, inv_ref.shape)
    norm_own = (unit_own * gain).astype(BF16)
    for q in range(RING):
        norm_cut[q] = group_columns(norm_own, q)
    cut_sent = []
    for k, slot in ((1, 1), (-1, 2), (2, 3)):
        cut_sent.append(
            send(norm_cut.at[(z + k + RING) % RING], norm_sl.at[slot, my_rows], on_z(k))
        )

    row_parts[0].forward()
    grad_rows.finish()
    side = sz.rows // 2
    side_rows = pl.ds(pl.multiple_of(c * side, side), side)
    slice_sent = []
    for k, slot in ((1, 1), (-1, 2), (2, 3)):
        first = pl.multiple_of(((y + k + RING) % RING) * sz.group_step, 128)
        slice_sent.append(
            send(
                grad_all.at[side_rows, pl.ds(first, sz.group_pad)],
                grad_sl.at[slot, side_rows],
                on_y(k),
            )
        )

    load_fc2.wait()

    def multiply_in(lhs, lo, count, rows, out):
        @pl.loop(0, width // sz.chunk)
        def _(n):
            cols = pl.ds(pl.multiple_of(n * sz.chunk, sz.chunk), sz.chunk)
            part = lax.dot_general(
                lhs[lo : lo + count, cols], rows[:, cols], ROW_DIMS, preferred_element_type=F32
            )

            @pl.when(n == 0)
            def _():
                out[lo : lo + count, :] = part

            @pl.when(n > 0)
            def _():
                out[lo : lo + count, :] += part

    row_parts[1].forward()
    multiply_in(fc2_ref, *sz.parts[0], grad_all, hid_grad)
    multiply_in(fc2_ref, *sz.parts[1], grad_all, hid_grad)
    own_first = pl.multiple_of(y * sz.group_step, 128)
    grad_t[0] = grad_all[:, pl.ds(own_first, sz.group_pad)].T
    load_fc1.wait()
    row_parts[0].finish()
    row_parts[1].finish()
    for made in cut_sent:
        made.wait_recv()
    cut_rows.start()

    @pl.loop(0, sz.rows // 16)
    def _(n):
        rows = pl.ds(pl.multiple_of(n * 16, 16), 16)
        unit, _ = normed_rows(rows)
        norm_all[rows, :] = (unit * gain).astype(BF16)

    hid_ring, pre_ring = [], []
    for lo, count in sz.parts:
        multiply_in(fc1_ref, lo, count, norm_all, pre_act)

        @pl.loop(0, count // 32)
        def _(n):
            rows = pl.ds(pl.multiple_of(lo + n * 32, 32), 32)
            value = pre_act[rows, :]
            cdf = 0.5 * (1.0 + lax.erf(value * 0.7071067811865476))
            slope = cdf + value * jnp.exp(-0.5 * value * value) * 0.3989422804014327
            hid_g[0, rows, :] = (value * cdf).astype(BF16)
            pre_g[0, rows, :] = (hid_grad[rows, :] * slope).astype(BF16)

        hid_ring.append(RingGather(hid_g, lo, count, on_y))
        pre_ring.append(RingGather(pre_g, lo, count, on_z))
        hid_ring[-1].start()
        pre_ring[-1].start()

    slice_shared = []
    for slot, made in zip((1, 2, 3), slice_sent):
        made.wait_recv()
        place = grad_sl.at[slot, side_rows]
        slice_shared.append(send(place, place, sibling))
    cut_rows.forward()
    hid_ring[0].forward()
    pre_ring[0].forward()

    back = RowReduce(1)
    branch = RowReduce(0)
    pre_n[...] = pre_g[0].T

    def gain_part(cols, full):
        product = full * norm_all[:, cols].astype(F32)
        gain_sib[0, :, cols] = jnp.sum(product, axis=0, keepdims=True)

    back.multiply(pre_n, fc1_ref, gain_part)
    gain_pair = send(gain_sib.at[0], gain_sib.at[1], sibling)
    cut_rows.finish()
    hid_ring[1].forward()
    pre_ring[1].forward()
    back.start()
    hid_n[...] = hid_g[0].T
    branch.multiply(hid_n, fc2_ref)
    for made in slice_shared:
        made.wait_recv()
    for k in range(1, RING):
        grad_t[k] = grad_sl[k].T

    def add_start(buf, me, on_axis, total):
        buf[me] = total
        return [send(buf.at[me], buf.at[me], on_axis(k)) for k in (1, -1, 2)]

    def add_finish(buf, made):
        for one in made:
            one.wait_recv()
        return buf[0] + buf[1] + buf[2] + buf[3]

    gain_pair.wait_recv()
    adding = add_start(gain_x, x, on_x, gain_sib[0] + gain_sib[1])
    back.ring.forward()
    branch.start()

    def fc2_row(k):
        return y * (sz.group - sz.group_step) + ((z + STEP[k] + RING) % RING) * sz.owned

    def fc1_row(k):
        return ((y + STEP[k] + RING) % RING) * sz.owned

    fc2_grad = [
        WeightGrad(0, p, grad_t, hid_g, on_z, fc2_row, fc2_grad_ref) for p in range(2)
    ]
    fc1_grad = [
        WeightGrad(1, p, norm_t, pre_g, on_y, fc1_row, fc1_grad_ref) for p in range(2)
    ]
    hid_ring[0].finish()
    fc2_grad[0].multiply()

    for q in range(RING):

        @pl.when(z == q)
        def _():
            norm_t[0] = group_columns(norm_all[...], q).T

    for k in range(1, RING):
        norm_t[k] = norm_sl[k].T
    pre_ring[0].finish()
    fc1_grad[0].multiply()
    branch.ring.forward()
    back.ring.finish()

    normed_grad = back.ring.total()
    unit = row_all[my_rows, :].astype(F32) * inv_ref[:, :1]
    scaled = normed_grad * gain
    inner = scaled - unit * jnp.mean(scaled * unit, axis=-1, keepdims=True)
    input_grad[...] = (
        (grad_all[my_rows, :].astype(F32) + inv_ref[:, :1] * inner).astype(BF16).astype(F32)
    )
    returned = []
    for j in range(sz.homes):
        total = pick(0, j) * input_grad[0 : sz.block_rows, :]
        for s in range(1, sz.slots):
            total += pick(s, j) * input_grad[s * sz.block_rows : (s + 1) * sz.block_rows, :]
        if j == 0:
            tgrad_ref[0] = total.astype(BF16)
        else:
            back_out[j - 1] = total.astype(BF16)
            returned.append(send(back_out.at[j - 1], tgrad_ref.at[j], on_dp(-j)))

    total = add_finish(gain_x, adding)
    adding = add_start(gain_y, y, on_y, total)
    fc2_grad[0].ring.forward()
    hid_ring[1].finish()
    fc2_grad[1].multiply()
    fc1_grad[0].ring.forward()
    pre_ring[1].finish()
    fc1_grad[1].multiply()
    total = add_finish(gain_y, adding)
    adding = add_start(gain_z, z, on_z, total)
    branch.ring.finish()
    mixed_ref[...] = (row_all[my_rows, :].astype(F32) + branch.ring.total()).astype(BF16)
    fc2_grad[0].finish()
    fc2_grad[1].ring.forward()
    fc1_grad[0].finish()
    fc1_grad[1].ring.forward()
    total = add_finish(gain_z, adding)
    gain_grad_ref[...] = (total / gain).reshape(width)
    fc2_grad[1].finish()
    fc1_grad[1].finish()
    for made in returned:
        made.wait_recv()
    for made in started:
        made.wait_send()
    if len(started) != copies:
        raise ValueError(len(started))


def hand_over_kernel(*refs):
    count = (len(refs) - 2) // 3
    source, target, held = refs[:count], refs[count : 2 * count], refs[2 * count : 3 * count]
    in_sems, out_sems = refs[-2:]
    loads, stores = [], []
    for i in range(count):
        loads.append(pltpu.make_async_copy(source[i], held[i], in_sems.at[i]))
        stores.append(pltpu.make_async_copy(held[i], target[i], out_sems.at[i]))
    for one in loads:
        one.start()
    for load, store in zip(loads, stores):
        load.wait()
        store.start()
    for one in stores:
        one.wait()


def hand_over(*arrays):
    anywhere = pl.BlockSpec(memory_space=pl.ANY)
    return pl.pallas_call(
        hand_over_kernel,
        out_shape=tuple(jax.ShapeDtypeStruct(a.shape, a.dtype) for a in arrays),
        in_specs=[anywhere] * len(arrays),
        out_specs=(anywhere,) * len(arrays),
        scratch_shapes=[pltpu.VMEM(a.shape, a.dtype) for a in arrays]
        + [pltpu.SemaphoreType.DMA((len(arrays),))] * 2,
        compiler_params=pltpu.CompilerParams(vmem_limit_bytes=60 * 1024 * 1024),
        name="hand_over",
    )(*arrays)


COPIES = 121


def local(tokens, norm_gain, fc1, fc2t, block_slot, out_grad):
    sz = Sizes(tokens.shape, fc1.shape, out_grad.shape)
    width, units = sz.width, sz.units
    vmem = pl.BlockSpec(memory_space=pltpu.VMEM)
    anywhere = pl.BlockSpec(memory_space=pl.ANY)
    slices = (RING, sz.rows, sz.group_pad)
    slices_t = (RING, sz.group_pad, sz.rows)
    pieces = (2, 2, 3, sz.owned_pad, sz.part_max)
    arrays = pl.pallas_call(
        functools.partial(kernel, sz, COPIES),
        out_shape=(
            jax.ShapeDtypeStruct((sz.own, width), BF16),
            jax.ShapeDtypeStruct(tokens.shape, BF16),
            jax.ShapeDtypeStruct((sz.owned, units), F32),
            jax.ShapeDtypeStruct((sz.owned, units), F32),
            jax.ShapeDtypeStruct((width,), F32),
        ),
        in_specs=[
            pl.BlockSpec(memory_space=pltpu.SMEM),
            vmem,
            anywhere,
            anywhere,
            anywhere,
            anywhere,
        ],
        out_specs=(vmem,) * 5,
        scratch_shapes=[
            pltpu.VMEM((units, width), BF16),
            pltpu.VMEM((units, width), BF16),
            pltpu.VMEM(tokens.shape, BF16),
            pltpu.VMEM((sz.rows, width), BF16),
            pltpu.VMEM((sz.own, 128), F32),
            pltpu.VMEM((sz.rows, width), BF16),
            pltpu.VMEM((sz.rows, width), BF16),
            pltpu.VMEM((RING, sz.own, sz.group_pad), BF16),
            pltpu.VMEM(slices, BF16),
            pltpu.VMEM(slices, BF16),
            pltpu.VMEM(slices_t, BF16),
            pltpu.VMEM(slices_t, BF16),
            pltpu.VMEM((RING, units, sz.rows), BF16),
            pltpu.VMEM((RING, units, sz.rows), BF16),
            pltpu.VMEM((sz.rows, units), BF16),
            pltpu.VMEM((sz.rows, units), BF16),
            pltpu.VMEM((units, sz.rows), F32),
            pltpu.VMEM((units, sz.rows), F32),
            pltpu.VMEM((2, RING, sz.own, width), F32),
            pltpu.VMEM((2, RING, sz.own, width), BF16),
            pltpu.VMEM((2, RING, sz.own, width), BF16),
            pltpu.VMEM((2, 3, sz.own, width), BF16),
            pltpu.VMEM((2, 3, sz.own, width), BF16),
            pltpu.VMEM((2, 2, sz.sum_rows, sz.part_max), F32),
            pltpu.VMEM(pieces, BF16),
            pltpu.VMEM(pieces, BF16),
            pltpu.VMEM((sz.homes - 1, sz.block_rows, width), BF16),
            pltpu.VMEM((sz.own, width), F32),
            pltpu.VMEM((2, 1, width), F32),
            pltpu.VMEM((RING, 1, width), F32),
            pltpu.VMEM((RING, 1, width), F32),
            pltpu.VMEM((RING, 1, width), F32),
            pltpu.SemaphoreType.DMA((4,)),
            pltpu.SemaphoreType.DMA((COPIES,)),
            pltpu.SemaphoreType.DMA((COPIES,)),
        ],
        compiler_params=pltpu.CompilerParams(
            collective_id=0, has_side_effects=True, vmem_limit_bytes=60 * 1024 * 1024
        ),
        cost_estimate=pl.CostEstimate(
            flops=12 * sz.rows * width * units,
            bytes_accessed=4 * width * units,
            transcendentals=2 * sz.rows * units,
        ),
        name="mlp_block",
    )(
        block_slot,
        norm_gain,
        tokens,
        fc1.T,
        fc2t.T,
        out_grad.reshape(sz.own, width),
    )
    mixed, tgrad, fc1_grad, fc2_grad, gain_grad = hand_over(*arrays)
    return mixed.reshape(out_grad.shape), tgrad, fc1_grad, fc2_grad, gain_grad


def solution(mesh):
    placed = (
        P("dp", "tensor", None),
        P(),
        P(None, "tensor"),
        P(None, "tensor"),
        P(),
        P("dp", "tensor", None),
    )
    return jax.shard_map(
        local,
        mesh=mesh,
        in_specs=placed,
        out_specs=(
            P("dp", "tensor", None),
            P("dp", "tensor", None),
            P("dp", "tensor"),
            P("dp", "tensor"),
            P(),
        ),
        check_vma=False,
    )
```

```python
import functools

import jax
import jax.numpy as jnp
from jax import lax
from jax.experimental import pallas as pl
from jax.experimental.pallas import tpu as pltpu
from jax.sharding import PartitionSpec as P

MESH = pl.DeviceIdType.MESH
ROW_DIMS = (((1,), (1,)), ((), ()))
RING = 4
RANKS = RING * RING
F32 = jnp.float32
BF16 = jnp.bfloat16

STEP = (0, -1, 1, 2)


def round_up(value, unit):
    return (value + unit - 1) // unit * unit


def chunk_of(width, limit):
    tiles = width // 128
    best = 1
    for count in range(1, tiles + 1):
        if tiles % count == 0 and count * 128 <= limit:
            best = count
    return best * 128


class Sizes:
    def __init__(self, tokens, fc1, out_grad):
        self.homes, self.block_rows, self.width = tokens
        self.units = fc1[1]
        self.slots = out_grad[0]
        self.own = self.slots * self.block_rows
        self.pair = 2 * self.own
        self.rows = RING * self.pair
        self.owned = self.width // RANKS
        self.owned_pad = round_up(self.owned, 16)
        self.group = RING * self.owned
        self.group_step = self.group // 128 * 128
        self.group_pad = round_up(self.group + (RING - 1) * (self.group - self.group_step), 128)
        self.sum_rows = self.group_pad + 8
        self.chunk = chunk_of(self.width, 640)
        first = round_up(self.units // 2, 128) - 128
        self.parts = ((0, first), (first, self.units - first))
        mid = round_up(self.width // 2, 128)
        self.cuts = ((0, mid), (mid, self.width - mid))
        self.part_max = max(count for _, count in self.parts)


def kernel(
    sz,
    copies,
    slot_ref,
    gain_ref,
    tokens_hbm,
    fc1_hbm,
    fc2_hbm,
    grad_hbm,
    mixed_ref,
    tgrad_ref,
    fc1_grad_ref,
    fc2_grad_ref,
    gain_grad_ref,
    fc1_ref,
    fc2_ref,
    arrived,
    row_all,
    inv_ref,
    grad_all,
    norm_all,
    norm_cut,
    grad_sl,
    norm_sl,
    grad_t,
    norm_t,
    hid_g,
    pre_g,
    hid_n,
    pre_n,
    pre_act,
    hid_grad,
    row_sum,
    sib_out,
    sib_in,
    rs_out,
    rs_in,
    wg_sum,
    wg_out,
    wg_in,
    back_out,
    input_grad,
    gain_sib,
    gain_x,
    gain_y,
    gain_z,
    local_sems,
    send_sems,
    recv_sems,
):
    dp = lax.axis_index("dp")
    t = lax.axis_index("tensor")
    y, z = dp // RING, dp % RING
    x, c = t // 2, t % 2
    own, width = sz.own, sz.width
    half = own // 2
    gain = gain_ref[...].reshape(1, width)

    def on_dp(k):
        return ((dp + k + RANKS) % RANKS, t)

    def on_x(k):
        return (dp, ((x + k + RING) % RING) * 2 + c)

    def on_y(k):
        return (((y + k + RING) % RING) * RING + z, t)

    def on_z(k):
        return (y * RING + (z + k + RING) % RING, t)

    sibling = (dp, t + 1 - 2 * c)

    started = []

    def send(src, dst, device):
        index = len(started)
        made = pltpu.make_async_remote_copy(
            src_ref=src,
            dst_ref=dst,
            send_sem=send_sems.at[index],
            recv_sem=recv_sems.at[index],
            device_id=device,
            device_id_type=MESH,
        )
        made.start()
        started.append(made)
        return made

    my_rows = pl.ds(pl.multiple_of(c * own, own), own)
    load_grad = pltpu.make_async_copy(grad_hbm, grad_all.at[my_rows], local_sems.at[0])
    load_token = pltpu.make_async_copy(tokens_hbm.at[0], arrived.at[0], local_sems.at[1])
    load_fc2 = pltpu.make_async_copy(fc2_hbm, fc2_ref, local_sems.at[2])
    load_fc1 = pltpu.make_async_copy(fc1_hbm, fc1_ref, local_sems.at[3])
    load_grad.start()
    load_token.start()
    load_fc2.start()
    load_fc1.start()

    partners = [on_dp(k) for k in range(1, sz.homes)]
    partners += [on_dp(-k) for k in range(1, sz.homes)]
    partners += [on_y(k) for k in (1, -1, 2)]
    partners += [on_z(k) for k in (1, -1, 2)]
    partners += [on_x(k) for k in (1, -1, 2)]
    partners += [sibling]
    barrier = pltpu.get_barrier_semaphore()
    for device in partners:
        pl.semaphore_signal(barrier, inc=1, device_id=device, device_id_type=MESH)
    pl.semaphore_wait(barrier, len(partners))

    class RowGather:
        def __init__(self, view):
            self.view = view

        def part(self, slot, lo, count):
            place = sz.pair * slot + c * own + lo
            return self.view(pl.ds(pl.multiple_of(place, 16), count))

        def start(self):
            mine = self.part(0, 0, own)
            self.right = send(mine, self.part(1, 0, own), on_x(1))
            self.left = send(mine, self.part(2, 0, own), on_x(-1))
            self.shared = [send(mine, mine, sibling)]

        def forward(self):
            self.right.wait_recv()
            self.right2 = send(self.part(1, 0, half), self.part(3, 0, half), on_x(1))
            whole = self.part(1, 0, own)
            self.shared.append(send(whole, whole, sibling))
            self.left.wait_recv()
            rest = own - half
            self.left2 = send(self.part(2, half, rest), self.part(3, half, rest), on_x(-1))
            whole = self.part(2, 0, own)
            self.shared.append(send(whole, whole, sibling))

        def last(self):
            self.right2.wait_recv()
            low = self.part(3, 0, half)
            self.shared.append(send(low, low, sibling))
            self.left2.wait_recv()
            high = self.part(3, half, own - half)
            self.shared.append(send(high, high, sibling))

        def wait(self, first, stop):
            for made in self.shared[first:stop]:
                made.wait_recv()

    class RingGather:
        def __init__(self, buf, lo, count, on_axis):
            self.buf, self.on_axis = buf, on_axis
            self.whole = pl.ds(lo, count)
            self.low = pl.ds(lo, count // 2)
            self.high = pl.ds(lo + count // 2, count // 2)

        def start(self):
            buf, on_axis = self.buf, self.on_axis
            mine = buf.at[0, self.whole]
            self.right = send(mine, buf.at[1, self.whole], on_axis(1))
            self.left = send(mine, buf.at[2, self.whole], on_axis(-1))

        def forward(self):
            buf, on_axis = self.buf, self.on_axis
            self.right.wait_recv()
            self.right2 = send(buf.at[1, self.low], buf.at[3, self.low], on_axis(1))
            self.left.wait_recv()
            self.left2 = send(buf.at[2, self.high], buf.at[3, self.high], on_axis(-1))

        def finish(self):
            self.right2.wait_recv()
            self.left2.wait_recv()

    class RingReduce:
        def __init__(self, part, out, into, on_axis, mid, count):
            self.part, self.out, self.into = part, out, into
            self.on_axis, self.mid, self.count = on_axis, mid, count

        def start(self):
            mid, rest = self.mid, self.count - self.mid
            lo, hi = pl.ds(0, mid), pl.ds(mid, rest)
            part, out, into, on_axis = self.part, self.out, self.into, self.on_axis
            out[0, lo] = part(3, 0, mid).astype(BF16)
            self.far_right = send(out.at[0, lo], into.at[0, lo], on_axis(1))
            out[0, hi] = part(3, mid, rest).astype(BF16)
            self.far_left = send(out.at[0, hi], into.at[0, hi], on_axis(-1))
            out[1, hi] = part(2, mid, rest).astype(BF16)
            self.near_right = send(out.at[1, hi], into.at[1, hi], on_axis(1))
            out[2, lo] = part(1, 0, mid).astype(BF16)
            self.near_left = send(out.at[2, lo], into.at[2, lo], on_axis(-1))

        def forward(self):
            mid, rest = self.mid, self.count - self.mid
            lo, hi = pl.ds(0, mid), pl.ds(mid, rest)
            part, out, into, on_axis = self.part, self.out, self.into, self.on_axis
            self.far_right.wait_recv()
            out[1, lo] = (part(2, 0, mid) + into[0, lo].astype(F32)).astype(BF16)
            self.sum_right = send(out.at[1, lo], into.at[1, lo], on_axis(1))
            self.far_left.wait_recv()
            out[2, hi] = (part(1, mid, rest) + into[0, hi].astype(F32)).astype(BF16)
            self.sum_left = send(out.at[2, hi], into.at[2, hi], on_axis(-1))

        def finish(self):
            self.near_right.wait_recv()
            self.near_left.wait_recv()
            self.sum_right.wait_recv()
            self.sum_left.wait_recv()

        def total(self):
            first = self.part(0, 0, self.count) + self.into[1].astype(F32)
            return first + self.into[2].astype(F32)

    class RowReduce:
        def __init__(self, index):
            self.index = index

        def multiply(self, lhs, weight, also=None):
            index = self.index

            @pl.loop(0, width // sz.chunk)
            def _(n):
                cols = pl.ds(pl.multiple_of(n * sz.chunk, sz.chunk), sz.chunk)
                full = jnp.dot(lhs[...], weight[:, cols], preferred_element_type=F32)
                for k in range(RING):
                    even = full[sz.pair * k : sz.pair * k + own]
                    odd = full[sz.pair * k + own : sz.pair * (k + 1)]
                    row_sum[index, k, :, cols] = jnp.where(c == 0, even, odd)
                    sib_out[index, k, :, cols] = jnp.where(c == 0, odd, even).astype(BF16)
                if also is not None:
                    also(cols, full)

            self.copy = send(sib_out.at[index], sib_in.at[index], sibling)

        def start(self):
            index = self.index
            self.copy.wait_recv()
            row_sum[index] = row_sum[index] + sib_in[index].astype(F32)

            def part(k, lo, count):
                return row_sum[index, k, lo : lo + count]

            self.ring = RingReduce(part, rs_out.at[index], rs_in.at[index], on_x, half, own)
            self.ring.start()

    class WeightGrad:
        def __init__(self, index, p, slices, blocks, on_axis, owner_row, out):
            self.index, self.p, self.out = index, p, out
            self.slices, self.blocks = slices, blocks
            self.lo, self.units = sz.parts[p]
            self.on_axis, self.owner_row = on_axis, owner_row

        def multiply(self):
            index, p, lo, units = self.index, self.p, self.lo, self.units
            step = sz.group_pad // RING

            @pl.loop(0, RING)
            def _(m):
                rows = pl.ds(pl.multiple_of(m * step, step), step)
                total = None
                for k in range(RING):
                    one = lax.dot_general(
                        self.slices[k, rows, :],
                        self.blocks[k, lo : lo + units, :],
                        ROW_DIMS,
                        preferred_element_type=F32,
                    )
                    total = one if total is None else total + one
                wg_sum[index, p, rows, 0:units] = total

            wg_sum[index, p, sz.group_pad : sz.sum_rows, 0:units] = jnp.zeros((8, units), F32)

            def part(k, first, count):
                place = pl.multiple_of(self.owner_row(k) + first, 8)
                return wg_sum[index, p, pl.ds(place, count), 0:units]

            self.ring = RingReduce(
                part,
                wg_out.at[index, p, :, :, pl.ds(0, units)],
                wg_in.at[index, p, :, :, pl.ds(0, units)],
                self.on_axis,
                round_up(sz.owned_pad // 2, 16),
                sz.owned_pad,
            )
            self.ring.start()

        def finish(self):
            self.ring.finish()
            self.out[:, self.lo : self.lo + self.units] = self.ring.total()[: sz.owned]

    grad_rows = RowGather(lambda rows: grad_all.at[rows])
    cut_rows = RowGather(lambda rows: norm_sl.at[pl.ds(1, RING - 1), rows])
    routed = []
    for lo, count in sz.cuts:
        cols = pl.ds(lo, count)
        for j in range(1, sz.homes):
            routed.append(send(tokens_hbm.at[j, :, cols], arrived.at[j, :, cols], on_dp(j)))
    load_grad.wait()
    grad_rows.start()

    def pick(s, j):
        home = (dp - j + RANKS) % RANKS
        named = slot_ref[home * sz.homes + j]
        return jnp.where(named == dp * sz.slots + s, 1.0, 0.0).astype(F32)

    def group_columns(rows, q):
        cuts = []
        for k in range(RING):
            first = sz.owned * (RING * k + q)
            cuts.append(rows[:, first : first + sz.owned])
        cuts.append(jnp.zeros((rows.shape[0], sz.group_pad - sz.group), rows.dtype))
        return jnp.concatenate(cuts, axis=1)

    load_token.wait()
    grad_rows.forward()
    row_parts = []
    for n, (lo, count) in enumerate(sz.cuts):
        cols = slice(lo, lo + count)
        for made in routed[n * (sz.homes - 1) : (n + 1) * (sz.homes - 1)]:
            made.wait_recv()
        for s in range(sz.slots):
            total = pick(s, 0) * arrived[0, :, cols].astype(F32)
            for j in range(1, sz.homes):
                total += pick(s, j) * arrived[j, :, cols].astype(F32)
            place = c * own + s * sz.block_rows
            rows = pl.ds(pl.multiple_of(place, sz.block_rows), sz.block_rows)
            row_all[rows, cols] = total.astype(BF16)
        one = RowGather(lambda rows, lo=lo, count=count: row_all.at[rows, pl.ds(lo, count)])
        one.start()
        row_parts.append(one)
    row_parts[0].forward()
    grad_rows.last()

    def normed_rows(rows):
        value = row_all[rows, :].astype(F32)
        inv = lax.rsqrt(jnp.mean(value * value, axis=-1, keepdims=True) + 1e-06)
        return value * inv, inv

    def norm_range(first, stop):
        @pl.loop(first // 16, stop // 16)
        def _(n):
            rows = pl.ds(pl.multiple_of(n * 16, 16), 16)
            unit, _ = normed_rows(rows)
            norm_all[rows, :] = (unit * gain).astype(BF16)

    unit_own, inv = normed_rows(my_rows)
    inv_ref[...] = jnp.broadcast_to(inv, inv_ref.shape)
    norm_own = (unit_own * gain).astype(BF16)
    for q in range(RING):
        norm_cut[q] = group_columns(norm_own, q)
    cut_sent = []
    for k, slot in ((1, 1), (-1, 2), (2, 3)):
        cut_sent.append(
            send(norm_cut.at[(z + k + RING) % RING], norm_sl.at[slot, my_rows], on_z(k))
        )
    row_parts[1].forward()
    grad_rows.wait(0, 5)
    side = sz.rows // 2
    side_rows = pl.ds(pl.multiple_of(c * side, side), side)
    slice_sent = []
    for k, slot in ((1, 1), (-1, 2), (2, 3)):
        first = pl.multiple_of(((y + k + RING) % RING) * sz.group_step, 128)
        slice_sent.append(
            send(
                grad_all.at[side_rows, pl.ds(first, sz.group_pad)],
                grad_sl.at[slot, side_rows],
                on_y(k),
            )
        )
    row_parts[0].last()

    load_fc2.wait()

    def multiply_in(lhs, lo, count, rows, out):
        @pl.loop(0, width // sz.chunk)
        def _(n):
            cols = pl.ds(pl.multiple_of(n * sz.chunk, sz.chunk), sz.chunk)
            part = lax.dot_general(
                lhs[lo : lo + count, cols], rows[:, cols], ROW_DIMS, preferred_element_type=F32
            )

            @pl.when(n == 0)
            def _():
                out[lo : lo + count, :] = part

            @pl.when(n > 0)
            def _():
                out[lo : lo + count, :] += part

    multiply_in(fc2_ref, *sz.parts[0], grad_all, hid_grad)
    row_parts[1].last()
    multiply_in(fc2_ref, *sz.parts[1], grad_all, hid_grad)
    for one in row_parts:
        one.wait(0, 3)
    norm_range(0, 3 * sz.pair)
    for made in cut_sent:
        made.wait_recv()
    for one in row_parts:
        one.wait(3, 5)
    cut_rows.start()
    norm_range(3 * sz.pair, sz.rows)
    load_fc1.wait()

    hid_ring, pre_ring = [], []
    for lo, count in sz.parts:
        multiply_in(fc1_ref, lo, count, norm_all, pre_act)

        @pl.loop(0, count // 32)
        def _(n):
            rows = pl.ds(pl.multiple_of(lo + n * 32, 32), 32)
            value = pre_act[rows, :]
            cdf = 0.5 * (1.0 + lax.erf(value * 0.7071067811865476))
            slope = cdf + value * jnp.exp(-0.5 * value * value) * 0.3989422804014327
            hid_g[0, rows, :] = (value * cdf).astype(BF16)
            pre_g[0, rows, :] = (hid_grad[rows, :] * slope).astype(BF16)

        hid_ring.append(RingGather(hid_g, lo, count, on_y))
        pre_ring.append(RingGather(pre_g, lo, count, on_z))
        hid_ring[-1].start()
        pre_ring[-1].start()

    slice_shared = []
    for slot, made in zip((1, 2, 3), slice_sent):
        made.wait_recv()
        place = grad_sl.at[slot, side_rows]
        slice_shared.append(send(place, place, sibling))
    cut_rows.forward()
    hid_ring[0].forward()
    pre_ring[0].forward()

    back = RowReduce(1)
    branch = RowReduce(0)
    pre_n[...] = pre_g[0].T

    def gain_part(cols, full):
        product = full * norm_all[:, cols].astype(F32)
        gain_sib[0, :, cols] = jnp.sum(product, axis=0, keepdims=True)

    back.multiply(pre_n, fc1_ref, gain_part)
    gain_pair = send(gain_sib.at[0], gain_sib.at[1], sibling)
    cut_rows.last()
    hid_ring[1].forward()
    pre_ring[1].forward()
    back.start()
    hid_n[...] = hid_g[0].T
    branch.multiply(hid_n, fc2_ref)
    cut_rows.wait(0, 5)
    own_first = pl.multiple_of(y * sz.group_step, 128)
    grad_t[0] = grad_all[:, pl.ds(own_first, sz.group_pad)].T
    for made in slice_shared:
        made.wait_recv()
    for k in range(1, RING):
        grad_t[k] = grad_sl[k].T

    def add_start(buf, me, on_axis, total):
        buf[me] = total
        return [send(buf.at[me], buf.at[me], on_axis(k)) for k in (1, -1, 2)]

    def add_finish(buf, made):
        for one in made:
            one.wait_recv()
        return buf[0] + buf[1] + buf[2] + buf[3]

    gain_pair.wait_recv()
    adding = add_start(gain_x, x, on_x, gain_sib[0] + gain_sib[1])
    back.ring.forward()
    branch.start()

    def fc2_row(k):
        return y * (sz.group - sz.group_step) + ((z + STEP[k] + RING) % RING) * sz.owned

    def fc1_row(k):
        return ((y + STEP[k] + RING) % RING) * sz.owned

    fc2_grad = [
        WeightGrad(0, p, grad_t, hid_g, on_z, fc2_row, fc2_grad_ref) for p in range(2)
    ]
    fc1_grad = [
        WeightGrad(1, p, norm_t, pre_g, on_y, fc1_row, fc1_grad_ref) for p in range(2)
    ]
    hid_ring[0].finish()
    fc2_grad[0].multiply()

    for q in range(RING):

        @pl.when(z == q)
        def _():
            norm_t[0] = group_columns(norm_all[...], q).T

    for k in range(1, RING):
        norm_t[k] = norm_sl[k].T
    pre_ring[0].finish()
    fc1_grad[0].multiply()
    branch.ring.forward()
    back.ring.finish()

    normed_grad = back.ring.total()
    unit = row_all[my_rows, :].astype(F32) * inv_ref[:, :1]
    scaled = normed_grad * gain
    inner = scaled - unit * jnp.mean(scaled * unit, axis=-1, keepdims=True)
    input_grad[...] = (
        (grad_all[my_rows, :].astype(F32) + inv_ref[:, :1] * inner).astype(BF16).astype(F32)
    )
    returned = []
    for j in range(sz.homes):
        total = pick(0, j) * input_grad[0 : sz.block_rows, :]
        for s in range(1, sz.slots):
            total += pick(s, j) * input_grad[s * sz.block_rows : (s + 1) * sz.block_rows, :]
        if j == 0:
            tgrad_ref[0] = total.astype(BF16)
        else:
            back_out[j - 1] = total.astype(BF16)
            returned.append(send(back_out.at[j - 1], tgrad_ref.at[j], on_dp(-j)))

    total = add_finish(gain_x, adding)
    adding = add_start(gain_y, y, on_y, total)
    fc2_grad[0].ring.forward()
    hid_ring[1].finish()
    fc2_grad[1].multiply()
    fc1_grad[0].ring.forward()
    pre_ring[1].finish()
    fc1_grad[1].multiply()
    total = add_finish(gain_y, adding)
    adding = add_start(gain_z, z, on_z, total)
    branch.ring.finish()
    mixed_ref[...] = (row_all[my_rows, :].astype(F32) + branch.ring.total()).astype(BF16)
    fc2_grad[0].finish()
    fc2_grad[1].ring.forward()
    fc1_grad[0].finish()
    fc1_grad[1].ring.forward()
    total = add_finish(gain_z, adding)
    gain_grad_ref[...] = (total / gain).reshape(width)
    fc2_grad[1].finish()
    fc1_grad[1].finish()
    for made in returned:
        made.wait_recv()
    for made in started:
        made.wait_send()
    if len(started) != copies:
        raise ValueError(len(started))


def hand_over_kernel(*refs):
    count = (len(refs) - 2) // 3
    source, target, held = refs[:count], refs[count : 2 * count], refs[2 * count : 3 * count]
    in_sems, out_sems = refs[-2:]
    loads, stores = [], []
    for i in range(count):
        loads.append(pltpu.make_async_copy(source[i], held[i], in_sems.at[i]))
        stores.append(pltpu.make_async_copy(held[i], target[i], out_sems.at[i]))
    for one in loads:
        one.start()
    for load, store in zip(loads, stores):
        load.wait()
        store.start()
    for one in stores:
        one.wait()


def hand_over(*arrays):
    anywhere = pl.BlockSpec(memory_space=pl.ANY)
    return pl.pallas_call(
        hand_over_kernel,
        out_shape=tuple(jax.ShapeDtypeStruct(a.shape, a.dtype) for a in arrays),
        in_specs=[anywhere] * len(arrays),
        out_specs=(anywhere,) * len(arrays),
        scratch_shapes=[pltpu.VMEM(a.shape, a.dtype) for a in arrays]
        + [pltpu.SemaphoreType.DMA((len(arrays),))] * 2,
        compiler_params=pltpu.CompilerParams(vmem_limit_bytes=60 * 1024 * 1024),
        name="hand_over",
    )(*arrays)


COPIES = 121


def local(tokens, norm_gain, fc1, fc2t, block_slot, out_grad):
    sz = Sizes(tokens.shape, fc1.shape, out_grad.shape)
    width, units = sz.width, sz.units
    vmem = pl.BlockSpec(memory_space=pltpu.VMEM)
    anywhere = pl.BlockSpec(memory_space=pl.ANY)
    slices = (RING, sz.rows, sz.group_pad)
    slices_t = (RING, sz.group_pad, sz.rows)
    pieces = (2, 2, 3, sz.owned_pad, sz.part_max)
    arrays = pl.pallas_call(
        functools.partial(kernel, sz, COPIES),
        out_shape=(
            jax.ShapeDtypeStruct((sz.own, width), BF16),
            jax.ShapeDtypeStruct(tokens.shape, BF16),
            jax.ShapeDtypeStruct((sz.owned, units), F32),
            jax.ShapeDtypeStruct((sz.owned, units), F32),
            jax.ShapeDtypeStruct((width,), F32),
        ),
        in_specs=[
            pl.BlockSpec(memory_space=pltpu.SMEM),
            vmem,
            anywhere,
            anywhere,
            anywhere,
            anywhere,
        ],
        out_specs=(vmem,) * 5,
        scratch_shapes=[
            pltpu.VMEM((units, width), BF16),
            pltpu.VMEM((units, width), BF16),
            pltpu.VMEM(tokens.shape, BF16),
            pltpu.VMEM((sz.rows, width), BF16),
            pltpu.VMEM((sz.own, 128), F32),
            pltpu.VMEM((sz.rows, width), BF16),
            pltpu.VMEM((sz.rows, width), BF16),
            pltpu.VMEM((RING, sz.own, sz.group_pad), BF16),
            pltpu.VMEM(slices, BF16),
            pltpu.VMEM(slices, BF16),
            pltpu.VMEM(slices_t, BF16),
            pltpu.VMEM(slices_t, BF16),
            pltpu.VMEM((RING, units, sz.rows), BF16),
            pltpu.VMEM((RING, units, sz.rows), BF16),
            pltpu.VMEM((sz.rows, units), BF16),
            pltpu.VMEM((sz.rows, units), BF16),
            pltpu.VMEM((units, sz.rows), F32),
            pltpu.VMEM((units, sz.rows), F32),
            pltpu.VMEM((2, RING, sz.own, width), F32),
            pltpu.VMEM((2, RING, sz.own, width), BF16),
            pltpu.VMEM((2, RING, sz.own, width), BF16),
            pltpu.VMEM((2, 3, sz.own, width), BF16),
            pltpu.VMEM((2, 3, sz.own, width), BF16),
            pltpu.VMEM((2, 2, sz.sum_rows, sz.part_max), F32),
            pltpu.VMEM(pieces, BF16),
            pltpu.VMEM(pieces, BF16),
            pltpu.VMEM((sz.homes - 1, sz.block_rows, width), BF16),
            pltpu.VMEM((sz.own, width), F32),
            pltpu.VMEM((2, 1, width), F32),
            pltpu.VMEM((RING, 1, width), F32),
            pltpu.VMEM((RING, 1, width), F32),
            pltpu.VMEM((RING, 1, width), F32),
            pltpu.SemaphoreType.DMA((4,)),
            pltpu.SemaphoreType.DMA((COPIES,)),
            pltpu.SemaphoreType.DMA((COPIES,)),
        ],
        compiler_params=pltpu.CompilerParams(
            collective_id=0, has_side_effects=True, vmem_limit_bytes=60 * 1024 * 1024
        ),
        cost_estimate=pl.CostEstimate(
            flops=12 * sz.rows * width * units,
            bytes_accessed=4 * width * units,
            transcendentals=2 * sz.rows * units,
        ),
        name="mlp_block",
    )(
        block_slot,
        norm_gain,
        tokens,
        fc1.T,
        fc2t.T,
        out_grad.reshape(sz.own, width),
    )
    mixed, tgrad, fc1_grad, fc2_grad, gain_grad = hand_over(*arrays)
    return mixed.reshape(out_grad.shape), tgrad, fc1_grad, fc2_grad, gain_grad


def solution(mesh):
    placed = (
        P("dp", "tensor", None),
        P(),
        P(None, "tensor"),
        P(None, "tensor"),
        P(),
        P("dp", "tensor", None),
    )
    return jax.shard_map(
        local,
        mesh=mesh,
        in_specs=placed,
        out_specs=(
            P("dp", "tensor", None),
            P("dp", "tensor", None),
            P("dp", "tensor"),
            P("dp", "tensor"),
            P(),
        ),
        check_vma=False,
    )
```

```python
import functools

import jax
import jax.numpy as jnp
from jax import lax
from jax.experimental import pallas as pl
from jax.experimental.pallas import tpu as pltpu
from jax.sharding import PartitionSpec as P

MESH = pl.DeviceIdType.MESH
ROW_DIMS = (((1,), (1,)), ((), ()))
RING = 4
RANKS = RING * RING
F32 = jnp.float32
BF16 = jnp.bfloat16

STEP = (0, -1, 1, 2)


def round_up(value, unit):
    return (value + unit - 1) // unit * unit


def chunk_of(width, limit):
    tiles = width // 128
    best = 1
    for count in range(1, tiles + 1):
        if tiles % count == 0 and count * 128 <= limit:
            best = count
    return best * 128


class Sizes:
    def __init__(self, tokens, fc1, out_grad):
        self.homes, self.block_rows, self.width = tokens
        self.units = fc1[1]
        self.slots = out_grad[0]
        self.own = self.slots * self.block_rows
        self.pair = 2 * self.own
        self.rows = RING * self.pair
        self.owned = self.width // RANKS
        self.owned_pad = round_up(self.owned, 16)
        self.group = RING * self.owned
        self.group_step = self.group // 128 * 128
        self.group_pad = round_up(self.group + (RING - 1) * (self.group - self.group_step), 128)
        self.sum_rows = self.group_pad + 8
        self.chunk = chunk_of(self.width, 640)
        first = round_up(self.units // 2, 128) - 128
        self.parts = ((0, first), (first, self.units - first))
        mid = round_up(self.width // 2, 128)
        self.cuts = ((0, mid), (mid, self.width - mid))
        self.part_max = max(count for _, count in self.parts)


def kernel(
    sz,
    copies,
    slot_ref,
    gain_ref,
    tokens_hbm,
    fc1_hbm,
    fc2_hbm,
    grad_hbm,
    mixed_ref,
    tgrad_ref,
    fc1_grad_ref,
    fc2_grad_ref,
    gain_grad_ref,
    fc1_ref,
    fc2_ref,
    arrived,
    row_all,
    inv_ref,
    grad_all,
    norm_all,
    norm_cut,
    grad_sl,
    norm_sl,
    grad_t,
    norm_t,
    hid_g,
    pre_g,
    hid_n,
    pre_n,
    pre_act,
    hid_grad,
    row_sum,
    sib_out,
    sib_in,
    rs_out,
    rs_in,
    wg_sum,
    wg_out,
    wg_in,
    back_out,
    input_grad,
    gain_sib,
    gain_x,
    gain_y,
    gain_z,
    local_sems,
    send_sems,
    recv_sems,
):
    dp = lax.axis_index("dp")
    t = lax.axis_index("tensor")
    y, z = dp // RING, dp % RING
    x, c = t // 2, t % 2
    own, width = sz.own, sz.width
    half = own // 2
    gain = gain_ref[...].reshape(1, width)

    def on_dp(k):
        return ((dp + k + RANKS) % RANKS, t)

    def on_x(k):
        return (dp, ((x + k + RING) % RING) * 2 + c)

    def on_y(k):
        return (((y + k + RING) % RING) * RING + z, t)

    def on_z(k):
        return (y * RING + (z + k + RING) % RING, t)

    sibling = (dp, t + 1 - 2 * c)

    started = []

    def send(src, dst, device):
        index = len(started)
        made = pltpu.make_async_remote_copy(
            src_ref=src,
            dst_ref=dst,
            send_sem=send_sems.at[index],
            recv_sem=recv_sems.at[index],
            device_id=device,
            device_id_type=MESH,
        )
        made.start()
        started.append(made)
        return made

    my_rows = pl.ds(pl.multiple_of(c * own, own), own)
    load_grad = pltpu.make_async_copy(grad_hbm, grad_all.at[my_rows], local_sems.at[0])
    load_token = pltpu.make_async_copy(tokens_hbm.at[0], arrived.at[0], local_sems.at[1])
    load_fc2 = pltpu.make_async_copy(fc2_hbm, fc2_ref, local_sems.at[2])
    load_fc1 = pltpu.make_async_copy(fc1_hbm, fc1_ref, local_sems.at[3])
    load_grad.start()
    load_token.start()
    load_fc2.start()
    load_fc1.start()

    partners = [on_dp(k) for k in range(1, sz.homes)]
    partners += [on_dp(-k) for k in range(1, sz.homes)]
    partners += [on_y(k) for k in (1, -1, 2)]
    partners += [on_z(k) for k in (1, -1, 2)]
    partners += [on_x(k) for k in (1, -1, 2)]
    partners += [sibling]
    barrier = pltpu.get_barrier_semaphore()
    for device in partners:
        pl.semaphore_signal(barrier, inc=1, device_id=device, device_id_type=MESH)
    pl.semaphore_wait(barrier, len(partners))

    class RowGather:
        def __init__(self, view):
            self.view = view

        def part(self, slot, lo, count):
            place = sz.pair * slot + c * own + lo
            return self.view(pl.ds(pl.multiple_of(place, 16), count))

        def start(self):
            mine = self.part(0, 0, own)
            self.right = send(mine, self.part(1, 0, own), on_x(1))
            self.left = send(mine, self.part(2, 0, own), on_x(-1))
            self.shared = [send(mine, mine, sibling)]

        def forward(self):
            self.right.wait_recv()
            self.right2 = send(self.part(1, 0, half), self.part(3, 0, half), on_x(1))
            whole = self.part(1, 0, own)
            self.shared.append(send(whole, whole, sibling))
            self.left.wait_recv()
            rest = own - half
            self.left2 = send(self.part(2, half, rest), self.part(3, half, rest), on_x(-1))
            whole = self.part(2, 0, own)
            self.shared.append(send(whole, whole, sibling))

        def last(self):
            self.right2.wait_recv()
            low = self.part(3, 0, half)
            self.shared.append(send(low, low, sibling))
            self.left2.wait_recv()
            high = self.part(3, half, own - half)
            self.shared.append(send(high, high, sibling))

        def wait(self, first, stop):
            for made in self.shared[first:stop]:
                made.wait_recv()

    class RingGather:
        def __init__(self, buf, lo, count, on_axis):
            self.buf, self.on_axis = buf, on_axis
            self.whole = pl.ds(lo, count)
            self.low = pl.ds(lo, count // 2)
            self.high = pl.ds(lo + count // 2, count // 2)

        def start(self):
            buf, on_axis = self.buf, self.on_axis
            mine = buf.at[0, self.whole]
            self.right = send(mine, buf.at[1, self.whole], on_axis(1))
            self.left = send(mine, buf.at[2, self.whole], on_axis(-1))

        def forward(self):
            buf, on_axis = self.buf, self.on_axis
            self.right.wait_recv()
            self.right2 = send(buf.at[1, self.low], buf.at[3, self.low], on_axis(1))
            self.left.wait_recv()
            self.left2 = send(buf.at[2, self.high], buf.at[3, self.high], on_axis(-1))

        def finish(self):
            self.right2.wait_recv()
            self.left2.wait_recv()

    class RingReduce:
        def __init__(self, part, out, into, on_axis, mid, count):
            self.part, self.out, self.into = part, out, into
            self.on_axis, self.mid, self.count = on_axis, mid, count

        def start(self):
            mid, rest = self.mid, self.count - self.mid
            lo, hi = pl.ds(0, mid), pl.ds(mid, rest)
            part, out, into, on_axis = self.part, self.out, self.into, self.on_axis
            out[0, lo] = part(3, 0, mid).astype(BF16)
            self.far_right = send(out.at[0, lo], into.at[0, lo], on_axis(1))
            out[0, hi] = part(3, mid, rest).astype(BF16)
            self.far_left = send(out.at[0, hi], into.at[0, hi], on_axis(-1))
            out[1, hi] = part(2, mid, rest).astype(BF16)
            self.near_right = send(out.at[1, hi], into.at[1, hi], on_axis(1))
            out[2, lo] = part(1, 0, mid).astype(BF16)
            self.near_left = send(out.at[2, lo], into.at[2, lo], on_axis(-1))

        def forward(self):
            mid, rest = self.mid, self.count - self.mid
            lo, hi = pl.ds(0, mid), pl.ds(mid, rest)
            part, out, into, on_axis = self.part, self.out, self.into, self.on_axis
            self.far_right.wait_recv()
            out[1, lo] = (part(2, 0, mid) + into[0, lo].astype(F32)).astype(BF16)
            self.sum_right = send(out.at[1, lo], into.at[1, lo], on_axis(1))
            self.far_left.wait_recv()
            out[2, hi] = (part(1, mid, rest) + into[0, hi].astype(F32)).astype(BF16)
            self.sum_left = send(out.at[2, hi], into.at[2, hi], on_axis(-1))

        def finish(self):
            self.near_right.wait_recv()
            self.near_left.wait_recv()
            self.sum_right.wait_recv()
            self.sum_left.wait_recv()

        def total(self):
            first = self.part(0, 0, self.count) + self.into[1].astype(F32)
            return first + self.into[2].astype(F32)

    class RowReduce:
        def __init__(self, index):
            self.index = index

        def multiply(self, lhs, weight, also=None):
            index = self.index

            @pl.loop(0, width // sz.chunk)
            def _(n):
                cols = pl.ds(pl.multiple_of(n * sz.chunk, sz.chunk), sz.chunk)
                full = jnp.dot(lhs[...], weight[:, cols], preferred_element_type=F32)
                for k in range(RING):
                    even = full[sz.pair * k : sz.pair * k + own]
                    odd = full[sz.pair * k + own : sz.pair * (k + 1)]
                    row_sum[index, k, :, cols] = jnp.where(c == 0, even, odd)
                    sib_out[index, k, :, cols] = jnp.where(c == 0, odd, even).astype(BF16)
                if also is not None:
                    also(cols, full)

            self.copy = send(sib_out.at[index], sib_in.at[index], sibling)

        def start(self):
            index = self.index
            self.copy.wait_recv()
            row_sum[index] = row_sum[index] + sib_in[index].astype(F32)

            def part(k, lo, count):
                return row_sum[index, k, lo : lo + count]

            self.ring = RingReduce(part, rs_out.at[index], rs_in.at[index], on_x, half, own)
            self.ring.start()

    class WeightGrad:
        def __init__(self, index, p, slices, blocks, on_axis, owner_row, out):
            self.index, self.p, self.out = index, p, out
            self.slices, self.blocks = slices, blocks
            self.lo, self.units = sz.parts[p]
            self.on_axis, self.owner_row = on_axis, owner_row

        def multiply(self):
            index, p, lo, units = self.index, self.p, self.lo, self.units
            step = sz.group_pad // 2

            @pl.loop(0, 2)
            def _(m):
                rows = pl.ds(pl.multiple_of(m * step, step), step)
                total = None
                for k in range(RING):
                    one = lax.dot_general(
                        self.slices[k, rows, :],
                        self.blocks[k, lo : lo + units, :],
                        ROW_DIMS,
                        preferred_element_type=F32,
                    )
                    total = one if total is None else total + one
                wg_sum[index, p, rows, 0:units] = total

            wg_sum[index, p, sz.group_pad : sz.sum_rows, 0:units] = jnp.zeros((8, units), F32)

            def part(k, first, count):
                place = pl.multiple_of(self.owner_row(k) + first, 8)
                return wg_sum[index, p, pl.ds(place, count), 0:units]

            self.ring = RingReduce(
                part,
                wg_out.at[index, p, :, :, pl.ds(0, units)],
                wg_in.at[index, p, :, :, pl.ds(0, units)],
                self.on_axis,
                round_up(sz.owned_pad // 2, 16),
                sz.owned_pad,
            )
            self.ring.start()

        def finish(self):
            self.ring.finish()
            self.out[:, self.lo : self.lo + self.units] = self.ring.total()[: sz.owned]

    grad_rows = RowGather(lambda rows: grad_all.at[rows])
    cut_rows = RowGather(lambda rows: norm_sl.at[pl.ds(1, RING - 1), rows])
    routed = []
    for lo, count in sz.cuts:
        cols = pl.ds(lo, count)
        for j in range(1, sz.homes):
            routed.append(send(tokens_hbm.at[j, :, cols], arrived.at[j, :, cols], on_dp(j)))
    load_grad.wait()
    grad_rows.start()

    def pick(s, j):
        home = (dp - j + RANKS) % RANKS
        named = slot_ref[home * sz.homes + j]
        return jnp.where(named == dp * sz.slots + s, 1.0, 0.0).astype(F32)

    def group_columns(rows, q):
        cuts = []
        for k in range(RING):
            first = sz.owned * (RING * k + q)
            cuts.append(rows[:, first : first + sz.owned])
        cuts.append(jnp.zeros((rows.shape[0], sz.group_pad - sz.group), rows.dtype))
        return jnp.concatenate(cuts, axis=1)

    load_token.wait()
    grad_rows.forward()
    row_parts = []
    for n, (lo, count) in enumerate(sz.cuts):
        cols = slice(lo, lo + count)
        for made in routed[n * (sz.homes - 1) : (n + 1) * (sz.homes - 1)]:
            made.wait_recv()
        for s in range(sz.slots):
            total = pick(s, 0) * arrived[0, :, cols].astype(F32)
            for j in range(1, sz.homes):
                total += pick(s, j) * arrived[j, :, cols].astype(F32)
            place = c * own + s * sz.block_rows
            rows = pl.ds(pl.multiple_of(place, sz.block_rows), sz.block_rows)
            row_all[rows, cols] = total.astype(BF16)
        one = RowGather(lambda rows, lo=lo, count=count: row_all.at[rows, pl.ds(lo, count)])
        one.start()
        row_parts.append(one)
    row_parts[0].forward()
    grad_rows.last()

    def normed_rows(rows):
        value = row_all[rows, :].astype(F32)
        inv = lax.rsqrt(jnp.mean(value * value, axis=-1, keepdims=True) + 1e-06)
        return value * inv, inv

    def norm_range(first, stop):
        @pl.loop(first // 16, stop // 16)
        def _(n):
            rows = pl.ds(pl.multiple_of(n * 16, 16), 16)
            unit, _ = normed_rows(rows)
            norm_all[rows, :] = (unit * gain).astype(BF16)

    unit_own, inv = normed_rows(my_rows)
    inv_ref[...] = jnp.broadcast_to(inv, inv_ref.shape)
    norm_own = (unit_own * gain).astype(BF16)
    for q in range(RING):
        norm_cut[q] = group_columns(norm_own, q)
    cut_sent = []
    for k, slot in ((1, 1), (-1, 2), (2, 3)):
        cut_sent.append(
            send(norm_cut.at[(z + k + RING) % RING], norm_sl.at[slot, my_rows], on_z(k))
        )
    row_parts[1].forward()
    grad_rows.wait(0, 5)
    side = sz.rows // 2
    side_rows = pl.ds(pl.multiple_of(c * side, side), side)
    slice_sent = []
    for k, slot in ((1, 1), (-1, 2), (2, 3)):
        first = pl.multiple_of(((y + k + RING) % RING) * sz.group_step, 128)
        slice_sent.append(
            send(
                grad_all.at[side_rows, pl.ds(first, sz.group_pad)],
                grad_sl.at[slot, side_rows],
                on_y(k),
            )
        )
    row_parts[0].last()

    load_fc2.wait()

    def multiply_in(lhs, lo, count, rows, out):
        @pl.loop(0, width // sz.chunk)
        def _(n):
            cols = pl.ds(pl.multiple_of(n * sz.chunk, sz.chunk), sz.chunk)
            part = lax.dot_general(
                lhs[lo : lo + count, cols], rows[:, cols], ROW_DIMS, preferred_element_type=F32
            )

            @pl.when(n == 0)
            def _():
                out[lo : lo + count, :] = part

            @pl.when(n > 0)
            def _():
                out[lo : lo + count, :] += part

    multiply_in(fc2_ref, *sz.parts[0], grad_all, hid_grad)
    row_parts[1].last()
    multiply_in(fc2_ref, *sz.parts[1], grad_all, hid_grad)
    for one in row_parts:
        one.wait(0, 3)
    norm_range(0, 3 * sz.pair)
    for made in cut_sent:
        made.wait_recv()
    for one in row_parts:
        one.wait(3, 5)
    cut_rows.start()
    norm_range(3 * sz.pair, sz.rows)
    load_fc1.wait()

    hid_ring, pre_ring = [], []
    for lo, count in sz.parts:
        multiply_in(fc1_ref, lo, count, norm_all, pre_act)

        @pl.loop(0, count // 32)
        def _(n):
            rows = pl.ds(pl.multiple_of(lo + n * 32, 32), 32)
            value = pre_act[rows, :]
            cdf = 0.5 * (1.0 + lax.erf(value * 0.7071067811865476))
            slope = cdf + value * jnp.exp(-0.5 * value * value) * 0.3989422804014327
            hid_g[0, rows, :] = (value * cdf).astype(BF16)
            pre_g[0, rows, :] = (hid_grad[rows, :] * slope).astype(BF16)

        hid_ring.append(RingGather(hid_g, lo, count, on_y))
        pre_ring.append(RingGather(pre_g, lo, count, on_z))
        hid_ring[-1].start()
        pre_ring[-1].start()

    back = RowReduce(1)
    branch = RowReduce(0)

    def gain_part(cols, full):
        product = full * norm_all[:, cols].astype(F32)
        gain_sib[0, :, cols] = jnp.sum(product, axis=0, keepdims=True)

    pre_n[...] = pre_g[0].T
    back.multiply(pre_n, fc1_ref, gain_part)
    gain_pair = send(gain_sib.at[0], gain_sib.at[1], sibling)
    hid_ring[0].forward()
    pre_ring[0].forward()
    cut_rows.forward()
    slice_shared = []
    for slot, made in zip((1, 2, 3), slice_sent):
        made.wait_recv()
        place = grad_sl.at[slot, side_rows]
        slice_shared.append(send(place, place, sibling))
    hid_n[...] = hid_g[0].T
    branch.multiply(hid_n, fc2_ref)
    back.start()
    hid_ring[1].forward()
    pre_ring[1].forward()
    cut_rows.last()
    own_first = pl.multiple_of(y * sz.group_step, 128)
    grad_t[0] = grad_all[:, pl.ds(own_first, sz.group_pad)].T
    for made in slice_shared:
        made.wait_recv()
    for k in range(1, RING):
        grad_t[k] = grad_sl[k].T

    def add_start(buf, me, on_axis, total):
        buf[me] = total
        return [send(buf.at[me], buf.at[me], on_axis(k)) for k in (1, -1, 2)]

    def add_finish(buf, made):
        for one in made:
            one.wait_recv()
        return buf[0] + buf[1] + buf[2] + buf[3]

    branch.start()
    back.ring.forward()
    gain_pair.wait_recv()
    adding = add_start(gain_x, x, on_x, gain_sib[0] + gain_sib[1])

    def fc2_row(k):
        return y * (sz.group - sz.group_step) + ((z + STEP[k] + RING) % RING) * sz.owned

    def fc1_row(k):
        return ((y + STEP[k] + RING) % RING) * sz.owned

    fc2_grad = [
        WeightGrad(0, p, grad_t, hid_g, on_z, fc2_row, fc2_grad_ref) for p in range(2)
    ]
    fc1_grad = [
        WeightGrad(1, p, norm_t, pre_g, on_y, fc1_row, fc1_grad_ref) for p in range(2)
    ]
    hid_ring[0].finish()
    fc2_grad[0].multiply()
    cut_rows.wait(0, 5)
    for q in range(RING):

        @pl.when(z == q)
        def _():
            norm_t[0] = group_columns(norm_all[...], q).T

    for k in range(1, RING):
        norm_t[k] = norm_sl[k].T
    pre_ring[0].finish()
    fc1_grad[0].multiply()
    branch.ring.forward()
    total = add_finish(gain_x, adding)
    adding = add_start(gain_y, y, on_y, total)
    fc2_grad[0].ring.forward()
    hid_ring[1].finish()
    fc2_grad[1].multiply()
    fc1_grad[0].ring.forward()
    back.ring.finish()

    normed_grad = back.ring.total()
    unit = row_all[my_rows, :].astype(F32) * inv_ref[:, :1]
    scaled = normed_grad * gain
    inner = scaled - unit * jnp.mean(scaled * unit, axis=-1, keepdims=True)
    input_grad[...] = (
        (grad_all[my_rows, :].astype(F32) + inv_ref[:, :1] * inner).astype(BF16).astype(F32)
    )
    returned = []
    for j in range(sz.homes):
        total = pick(0, j) * input_grad[0 : sz.block_rows, :]
        for s in range(1, sz.slots):
            total += pick(s, j) * input_grad[s * sz.block_rows : (s + 1) * sz.block_rows, :]
        if j == 0:
            tgrad_ref[0] = total.astype(BF16)
        else:
            back_out[j - 1] = total.astype(BF16)
            returned.append(send(back_out.at[j - 1], tgrad_ref.at[j], on_dp(-j)))

    pre_ring[1].finish()
    fc1_grad[1].multiply()
    total = add_finish(gain_y, adding)
    adding = add_start(gain_z, z, on_z, total)
    branch.ring.finish()
    mixed_ref[...] = (row_all[my_rows, :].astype(F32) + branch.ring.total()).astype(BF16)
    fc2_grad[0].finish()
    fc2_grad[1].ring.forward()
    fc1_grad[0].finish()
    fc1_grad[1].ring.forward()
    total = add_finish(gain_z, adding)
    gain_grad_ref[...] = (total / gain).reshape(width)
    fc2_grad[1].finish()
    fc1_grad[1].finish()
    for made in returned:
        made.wait_recv()
    for made in started:
        made.wait_send()
    if len(started) != copies:
        raise ValueError(len(started))


def hand_over_kernel(*refs):
    count = (len(refs) - 2) // 3
    source, target, held = refs[:count], refs[count : 2 * count], refs[2 * count : 3 * count]
    in_sems, out_sems = refs[-2:]
    loads, stores = [], []
    for i in range(count):
        loads.append(pltpu.make_async_copy(source[i], held[i], in_sems.at[i]))
        stores.append(pltpu.make_async_copy(held[i], target[i], out_sems.at[i]))
    for one in loads:
        one.start()
    for load, store in zip(loads, stores):
        load.wait()
        store.start()
    for one in stores:
        one.wait()


def hand_over(*arrays):
    anywhere = pl.BlockSpec(memory_space=pl.ANY)
    return pl.pallas_call(
        hand_over_kernel,
        out_shape=tuple(jax.ShapeDtypeStruct(a.shape, a.dtype) for a in arrays),
        in_specs=[anywhere] * len(arrays),
        out_specs=(anywhere,) * len(arrays),
        scratch_shapes=[pltpu.VMEM(a.shape, a.dtype) for a in arrays]
        + [pltpu.SemaphoreType.DMA((len(arrays),))] * 2,
        compiler_params=pltpu.CompilerParams(vmem_limit_bytes=60 * 1024 * 1024),
        name="hand_over",
    )(*arrays)


COPIES = 121


def local(tokens, norm_gain, fc1, fc2t, block_slot, out_grad):
    sz = Sizes(tokens.shape, fc1.shape, out_grad.shape)
    width, units = sz.width, sz.units
    vmem = pl.BlockSpec(memory_space=pltpu.VMEM)
    anywhere = pl.BlockSpec(memory_space=pl.ANY)
    slices = (RING, sz.rows, sz.group_pad)
    slices_t = (RING, sz.group_pad, sz.rows)
    pieces = (2, 2, 3, sz.owned_pad, sz.part_max)
    arrays = pl.pallas_call(
        functools.partial(kernel, sz, COPIES),
        out_shape=(
            jax.ShapeDtypeStruct((sz.own, width), BF16),
            jax.ShapeDtypeStruct(tokens.shape, BF16),
            jax.ShapeDtypeStruct((sz.owned, units), F32),
            jax.ShapeDtypeStruct((sz.owned, units), F32),
            jax.ShapeDtypeStruct((width,), F32),
        ),
        in_specs=[
            pl.BlockSpec(memory_space=pltpu.SMEM),
            vmem,
            anywhere,
            anywhere,
            anywhere,
            anywhere,
        ],
        out_specs=(vmem,) * 5,
        scratch_shapes=[
            pltpu.VMEM((units, width), BF16),
            pltpu.VMEM((units, width), BF16),
            pltpu.VMEM(tokens.shape, BF16),
            pltpu.VMEM((sz.rows, width), BF16),
            pltpu.VMEM((sz.own, 128), F32),
            pltpu.VMEM((sz.rows, width), BF16),
            pltpu.VMEM((sz.rows, width), BF16),
            pltpu.VMEM((RING, sz.own, sz.group_pad), BF16),
            pltpu.VMEM(slices, BF16),
            pltpu.VMEM(slices, BF16),
            pltpu.VMEM(slices_t, BF16),
            pltpu.VMEM(slices_t, BF16),
            pltpu.VMEM((RING, units, sz.rows), BF16),
            pltpu.VMEM((RING, units, sz.rows), BF16),
            pltpu.VMEM((sz.rows, units), BF16),
            pltpu.VMEM((sz.rows, units), BF16),
            pltpu.VMEM((units, sz.rows), F32),
            pltpu.VMEM((units, sz.rows), F32),
            pltpu.VMEM((2, RING, sz.own, width), F32),
            pltpu.VMEM((2, RING, sz.own, width), BF16),
            pltpu.VMEM((2, RING, sz.own, width), BF16),
            pltpu.VMEM((2, 3, sz.own, width), BF16),
            pltpu.VMEM((2, 3, sz.own, width), BF16),
            pltpu.VMEM((2, 2, sz.sum_rows, sz.part_max), F32),
            pltpu.VMEM(pieces, BF16),
            pltpu.VMEM(pieces, BF16),
            pltpu.VMEM((sz.homes - 1, sz.block_rows, width), BF16),
            pltpu.VMEM((sz.own, width), F32),
            pltpu.VMEM((2, 1, width), F32),
            pltpu.VMEM((RING, 1, width), F32),
            pltpu.VMEM((RING, 1, width), F32),
            pltpu.VMEM((RING, 1, width), F32),
            pltpu.SemaphoreType.DMA((4,)),
            pltpu.SemaphoreType.DMA((COPIES,)),
            pltpu.SemaphoreType.DMA((COPIES,)),
        ],
        compiler_params=pltpu.CompilerParams(
            collective_id=0, has_side_effects=True, vmem_limit_bytes=60 * 1024 * 1024
        ),
        cost_estimate=pl.CostEstimate(
            flops=12 * sz.rows * width * units,
            bytes_accessed=4 * width * units,
            transcendentals=2 * sz.rows * units,
        ),
        name="mlp_block",
    )(
        block_slot,
        norm_gain,
        tokens,
        fc1.T,
        fc2t.T,
        out_grad.reshape(sz.own, width),
    )
    mixed, tgrad, fc1_grad, fc2_grad, gain_grad = hand_over(*arrays)
    return mixed.reshape(out_grad.shape), tgrad, fc1_grad, fc2_grad, gain_grad


def solution(mesh):
    placed = (
        P("dp", "tensor", None),
        P(),
        P(None, "tensor"),
        P(None, "tensor"),
        P(),
        P("dp", "tensor", None),
    )
    return jax.shard_map(
        local,
        mesh=mesh,
        in_specs=placed,
        out_specs=(
            P("dp", "tensor", None),
            P("dp", "tensor", None),
            P("dp", "tensor"),
            P("dp", "tensor"),
            P(),
        ),
        check_vma=False,
    )
```

```python
import functools

import jax
import jax.numpy as jnp
from jax import lax
from jax.experimental import pallas as pl
from jax.experimental.pallas import tpu as pltpu
from jax.sharding import PartitionSpec as P

MESH = pl.DeviceIdType.MESH
ROW_DIMS = (((1,), (1,)), ((), ()))
RING = 4
RANKS = RING * RING
F32 = jnp.float32
BF16 = jnp.bfloat16

STEP = (0, -1, 1, 2)


def round_up(value, unit):
    return (value + unit - 1) // unit * unit


def chunk_of(width, limit):
    tiles = width // 128
    best = 1
    for count in range(1, tiles + 1):
        if tiles % count == 0 and count * 128 <= limit:
            best = count
    return best * 128


class Sizes:
    def __init__(self, tokens, fc1, out_grad):
        self.homes, self.block_rows, self.width = tokens
        self.units = fc1[1]
        self.slots = out_grad[0]
        self.own = self.slots * self.block_rows
        self.pair = 2 * self.own
        self.rows = RING * self.pair
        self.owned = self.width // RANKS
        self.owned_pad = round_up(self.owned, 16)
        self.group = RING * self.owned
        self.group_step = self.group // 128 * 128
        self.group_pad = round_up(self.group + (RING - 1) * (self.group - self.group_step), 128)
        self.sum_rows = self.group_pad + 8
        self.chunk = chunk_of(self.width, 640)
        first = round_up(self.units // 2, 128) - 128
        self.parts = ((0, first), (first, self.units - first))
        mid = round_up(self.width // 2, 128)
        self.cuts = ((0, mid), (mid, self.width - mid))
        self.part_max = max(count for _, count in self.parts)


def kernel(
    sz,
    copies,
    slot_ref,
    gain_ref,
    tokens_hbm,
    fc1_hbm,
    fc2_hbm,
    grad_hbm,
    mixed_ref,
    tgrad_ref,
    fc1_grad_ref,
    fc2_grad_ref,
    gain_grad_ref,
    fc1_ref,
    fc2_ref,
    arrived,
    midway,
    midway_back,
    mixed,
    tgrad,
    fc1_out,
    fc2_out,
    gain_out,
    row_all,
    inv_ref,
    grad_all,
    norm_all,
    norm_cut,
    grad_sl,
    norm_sl,
    grad_t,
    norm_t,
    hid_g,
    pre_g,
    hid_n,
    pre_n,
    pre_act,
    hid_grad,
    row_sum,
    sib_out,
    sib_in,
    rs_out,
    rs_in,
    wg_sum,
    wg_out,
    wg_in,
    back_out,
    input_grad,
    gain_sib,
    gain_x,
    gain_y,
    gain_z,
    local_sems,
    store_sems,
    send_sems,
    recv_sems,
):
    dp = lax.axis_index("dp")
    t = lax.axis_index("tensor")
    y, z = dp // RING, dp % RING
    x, c = t // 2, t % 2
    own, width = sz.own, sz.width
    half = own // 2
    gain = gain_ref[...].reshape(1, width)

    def on_dp(k):
        return ((dp + k + RANKS) % RANKS, t)

    def on_x(k):
        return (dp, ((x + k + RING) % RING) * 2 + c)

    def on_y(k):
        return (((y + k + RING) % RING) * RING + z, t)

    def on_z(k):
        return (y * RING + (z + k + RING) % RING, t)

    sibling = (dp, t + 1 - 2 * c)

    started = []

    class Guarded:
        def __init__(self, made, when, arrives):
            self.made, self.when, self.arrives = made, when, arrives

        def wait_recv(self):
            pl.when(self.arrives)(self.made.wait_recv)

        def wait_send(self):
            pl.when(self.when)(self.made.wait_send)

    def send(src, dst, device, when=None, arrives=None):
        index = len(started)
        made = pltpu.make_async_remote_copy(
            src_ref=src,
            dst_ref=dst,
            send_sem=send_sems.at[index],
            recv_sem=recv_sems.at[index],
            device_id=device,
            device_id_type=MESH,
        )
        if when is None:
            made.start()
        else:
            pl.when(when)(made.start)
            made = Guarded(made, when, when if arrives is None else arrives)
        started.append(made)
        return made

    my_rows = pl.ds(pl.multiple_of(c * own, own), own)
    load_grad = pltpu.make_async_copy(grad_hbm, grad_all.at[my_rows], local_sems.at[0])
    load_token = pltpu.make_async_copy(tokens_hbm.at[0], arrived.at[0], local_sems.at[1])
    load_fc2 = pltpu.make_async_copy(fc2_hbm, fc2_ref, local_sems.at[2])
    load_fc1 = pltpu.make_async_copy(fc1_hbm, fc1_ref, local_sems.at[3])
    load_grad.start()
    load_token.start()
    load_fc2.start()
    load_fc1.start()

    partners = [on_dp(k) for k in range(1, sz.homes)]
    partners += [on_dp(-k) for k in range(1, sz.homes)]
    partners += [on_y(k) for k in (1, -1, 2)]
    partners += [on_z(k) for k in (1, -1, 2)]
    partners += [on_x(k) for k in (1, -1, 2)]
    partners += [sibling]
    barrier = pltpu.get_barrier_semaphore()
    for device in partners:
        pl.semaphore_signal(barrier, inc=1, device_id=device, device_id_type=MESH)
    pl.semaphore_wait(barrier, len(partners))

    class RowGather:
        def __init__(self, view):
            self.view = view

        def part(self, slot, lo, count):
            place = sz.pair * slot + c * own + lo
            return self.view(pl.ds(pl.multiple_of(place, 16), count))

        def start(self):
            mine = self.part(0, 0, own)
            self.right = send(mine, self.part(1, 0, own), on_x(1))
            self.left = send(mine, self.part(2, 0, own), on_x(-1))
            self.shared = [send(mine, mine, sibling)]

        def forward(self):
            self.right.wait_recv()
            self.right2 = send(self.part(1, 0, half), self.part(3, 0, half), on_x(1))
            whole = self.part(1, 0, own)
            self.shared.append(send(whole, whole, sibling))
            self.left.wait_recv()
            rest = own - half
            self.left2 = send(self.part(2, half, rest), self.part(3, half, rest), on_x(-1))
            whole = self.part(2, 0, own)
            self.shared.append(send(whole, whole, sibling))

        def last(self):
            self.right2.wait_recv()
            low = self.part(3, 0, half)
            self.shared.append(send(low, low, sibling))
            self.left2.wait_recv()
            high = self.part(3, half, own - half)
            self.shared.append(send(high, high, sibling))

        def wait(self, first, stop):
            for made in self.shared[first:stop]:
                made.wait_recv()

    class RingGather:
        def __init__(self, buf, lo, count, on_axis):
            self.buf, self.on_axis = buf, on_axis
            self.whole = pl.ds(lo, count)
            self.low = pl.ds(lo, count // 2)
            self.high = pl.ds(lo + count // 2, count // 2)

        def start(self):
            buf, on_axis = self.buf, self.on_axis
            mine = buf.at[0, self.whole]
            self.right = send(mine, buf.at[1, self.whole], on_axis(1))
            self.left = send(mine, buf.at[2, self.whole], on_axis(-1))

        def forward(self):
            buf, on_axis = self.buf, self.on_axis
            self.right.wait_recv()
            self.right2 = send(buf.at[1, self.low], buf.at[3, self.low], on_axis(1))
            self.left.wait_recv()
            self.left2 = send(buf.at[2, self.high], buf.at[3, self.high], on_axis(-1))

        def finish(self):
            self.right2.wait_recv()
            self.left2.wait_recv()

    class RingReduce:
        def __init__(self, part, out, into, on_axis, mid, count):
            self.part, self.out, self.into = part, out, into
            self.on_axis, self.mid, self.count = on_axis, mid, count

        def start(self):
            mid, rest = self.mid, self.count - self.mid
            lo, hi = pl.ds(0, mid), pl.ds(mid, rest)
            part, out, into, on_axis = self.part, self.out, self.into, self.on_axis
            out[0, lo] = part(3, 0, mid).astype(BF16)
            self.far_right = send(out.at[0, lo], into.at[0, lo], on_axis(1))
            out[0, hi] = part(3, mid, rest).astype(BF16)
            self.far_left = send(out.at[0, hi], into.at[0, hi], on_axis(-1))
            out[1, hi] = part(2, mid, rest).astype(BF16)
            self.near_right = send(out.at[1, hi], into.at[1, hi], on_axis(1))
            out[2, lo] = part(1, 0, mid).astype(BF16)
            self.near_left = send(out.at[2, lo], into.at[2, lo], on_axis(-1))

        def forward(self):
            mid, rest = self.mid, self.count - self.mid
            lo, hi = pl.ds(0, mid), pl.ds(mid, rest)
            part, out, into, on_axis = self.part, self.out, self.into, self.on_axis
            self.far_right.wait_recv()
            out[1, lo] = (part(2, 0, mid) + into[0, lo].astype(F32)).astype(BF16)
            self.sum_right = send(out.at[1, lo], into.at[1, lo], on_axis(1))
            self.far_left.wait_recv()
            out[2, hi] = (part(1, mid, rest) + into[0, hi].astype(F32)).astype(BF16)
            self.sum_left = send(out.at[2, hi], into.at[2, hi], on_axis(-1))

        def finish(self):
            self.near_right.wait_recv()
            self.near_left.wait_recv()
            self.sum_right.wait_recv()
            self.sum_left.wait_recv()

        def total(self):
            first = self.part(0, 0, self.count) + self.into[1].astype(F32)
            return first + self.into[2].astype(F32)

    class RowReduce:
        def __init__(self, index):
            self.index = index

        def multiply(self, lhs, weight, also=None):
            index = self.index

            @pl.loop(0, width // sz.chunk)
            def _(n):
                cols = pl.ds(pl.multiple_of(n * sz.chunk, sz.chunk), sz.chunk)
                full = jnp.dot(lhs[...], weight[:, cols], preferred_element_type=F32)
                for k in range(RING):
                    even = full[sz.pair * k : sz.pair * k + own]
                    odd = full[sz.pair * k + own : sz.pair * (k + 1)]
                    row_sum[index, k, :, cols] = jnp.where(c == 0, even, odd)
                    sib_out[index, k, :, cols] = jnp.where(c == 0, odd, even).astype(BF16)
                if also is not None:
                    also(cols, full)

            self.copy = send(sib_out.at[index], sib_in.at[index], sibling)

        def start(self):
            index = self.index
            self.copy.wait_recv()
            row_sum[index] = row_sum[index] + sib_in[index].astype(F32)

            def part(k, lo, count):
                return row_sum[index, k, lo : lo + count]

            self.ring = RingReduce(part, rs_out.at[index], rs_in.at[index], on_x, half, own)
            self.ring.start()

    class WeightGrad:
        def __init__(self, index, p, slices, blocks, on_axis, owner_row, out):
            self.index, self.p, self.out = index, p, out
            self.slices, self.blocks = slices, blocks
            self.lo, self.units = sz.parts[p]
            self.on_axis, self.owner_row = on_axis, owner_row

        def multiply(self):
            index, p, lo, units = self.index, self.p, self.lo, self.units
            step = sz.group_pad // 2

            @pl.loop(0, 2)
            def _(m):
                rows = pl.ds(pl.multiple_of(m * step, step), step)
                total = None
                for k in range(RING):
                    one = lax.dot_general(
                        self.slices[k, rows, :],
                        self.blocks[k, lo : lo + units, :],
                        ROW_DIMS,
                        preferred_element_type=F32,
                    )
                    total = one if total is None else total + one
                wg_sum[index, p, rows, 0:units] = total

            wg_sum[index, p, sz.group_pad : sz.sum_rows, 0:units] = jnp.zeros((8, units), F32)

            def part(k, first, count):
                place = pl.multiple_of(self.owner_row(k) + first, 8)
                return wg_sum[index, p, pl.ds(place, count), 0:units]

            self.ring = RingReduce(
                part,
                wg_out.at[index, p, :, :, pl.ds(0, units)],
                wg_in.at[index, p, :, :, pl.ds(0, units)],
                self.on_axis,
                round_up(sz.owned_pad // 2, 16),
                sz.owned_pad,
            )
            self.ring.start()

        def finish(self):
            self.ring.finish()
            self.out[:, self.lo : self.lo + self.units] = self.ring.total()[: sz.owned]

    grad_rows = RowGather(lambda rows: grad_all.at[rows])
    cut_rows = RowGather(lambda rows: norm_sl.at[pl.ds(1, RING - 1), rows])
    (lo0, count0), (lo1, count1) = sz.cuts
    cols0, cols1 = pl.ds(lo0, count0), pl.ds(lo1, count1)
    via = []
    for j in range(1, RING):
        via.append(send(tokens_hbm.at[j, :, cols1], midway.at[j - 1], on_z(j)))
    direct = []
    for j in range(1, sz.homes):
        direct.append(send(tokens_hbm.at[j, :, cols0], arrived.at[j, :, cols0], on_dp(j)))
    last = []
    for j in range(RING, sz.homes):
        last.append(send(tokens_hbm.at[j, :, cols1], arrived.at[j, :, cols1], on_dp(j)))
    load_grad.wait()
    grad_rows.start()

    def pick(s, j):
        home = (dp - j + RANKS) % RANKS
        named = slot_ref[home * sz.homes + j]
        return jnp.where(named == dp * sz.slots + s, 1.0, 0.0).astype(F32)

    def group_columns(rows, q):
        cuts = []
        for k in range(RING):
            first = sz.owned * (RING * k + q)
            cuts.append(rows[:, first : first + sz.owned])
        cuts.append(jnp.zeros((rows.shape[0], sz.group_pad - sz.group), rows.dtype))
        return jnp.concatenate(cuts, axis=1)

    for j in range(1, RING):
        via[j - 1].wait_recv()
        last.append(
            send(midway.at[j - 1], arrived.at[j, :, cols1], on_y(1), when=z < j)
        )

        @pl.when(z >= j)
        def _():
            arrived[j, :, lo1:] = midway[j - 1]

    routed = (direct, last)
    load_token.wait()
    grad_rows.forward()
    row_parts = []
    for n, (lo, count) in enumerate(sz.cuts):
        cols = slice(lo, lo + count)
        for made in routed[n]:
            made.wait_recv()
        for s in range(sz.slots):
            total = pick(s, 0) * arrived[0, :, cols].astype(F32)
            for j in range(1, sz.homes):
                total += pick(s, j) * arrived[j, :, cols].astype(F32)
            place = c * own + s * sz.block_rows
            rows = pl.ds(pl.multiple_of(place, sz.block_rows), sz.block_rows)
            row_all[rows, cols] = total.astype(BF16)
        one = RowGather(lambda rows, lo=lo, count=count: row_all.at[rows, pl.ds(lo, count)])
        one.start()
        row_parts.append(one)
    row_parts[0].forward()
    grad_rows.last()

    def normed_rows(rows):
        value = row_all[rows, :].astype(F32)
        inv = lax.rsqrt(jnp.mean(value * value, axis=-1, keepdims=True) + 1e-06)
        return value * inv, inv

    def norm_range(first, stop):
        @pl.loop(first // 16, stop // 16)
        def _(n):
            rows = pl.ds(pl.multiple_of(n * 16, 16), 16)
            unit, _ = normed_rows(rows)
            norm_all[rows, :] = (unit * gain).astype(BF16)

    unit_own, inv = normed_rows(my_rows)
    inv_ref[...] = jnp.broadcast_to(inv, inv_ref.shape)
    norm_own = (unit_own * gain).astype(BF16)
    for q in range(RING):
        norm_cut[q] = group_columns(norm_own, q)
    cut_sent = []
    for k, slot in ((1, 1), (-1, 2), (2, 3)):
        cut_sent.append(
            send(norm_cut.at[(z + k + RING) % RING], norm_sl.at[slot, my_rows], on_z(k))
        )
    row_parts[1].forward()
    grad_rows.wait(0, 5)
    side = sz.rows // 2
    side_rows = pl.ds(pl.multiple_of(c * side, side), side)
    slice_sent = []
    for k, slot in ((1, 1), (-1, 2), (2, 3)):
        first = pl.multiple_of(((y + k + RING) % RING) * sz.group_step, 128)
        slice_sent.append(
            send(
                grad_all.at[side_rows, pl.ds(first, sz.group_pad)],
                grad_sl.at[slot, side_rows],
                on_y(k),
            )
        )
    row_parts[0].last()

    load_fc2.wait()

    def multiply_in(lhs, lo, count, rows, out):
        @pl.loop(0, width // sz.chunk)
        def _(n):
            cols = pl.ds(pl.multiple_of(n * sz.chunk, sz.chunk), sz.chunk)
            part = lax.dot_general(
                lhs[lo : lo + count, cols], rows[:, cols], ROW_DIMS, preferred_element_type=F32
            )

            @pl.when(n == 0)
            def _():
                out[lo : lo + count, :] = part

            @pl.when(n > 0)
            def _():
                out[lo : lo + count, :] += part

    multiply_in(fc2_ref, *sz.parts[0], grad_all, hid_grad)
    row_parts[1].last()
    multiply_in(fc2_ref, *sz.parts[1], grad_all, hid_grad)
    for one in row_parts:
        one.wait(0, 3)
    norm_range(0, 3 * sz.pair)
    for made in cut_sent:
        made.wait_recv()
    for one in row_parts:
        one.wait(3, 5)
    cut_rows.start()
    norm_range(3 * sz.pair, sz.rows)
    load_fc1.wait()

    hid_ring, pre_ring = [], []
    for lo, count in sz.parts:
        multiply_in(fc1_ref, lo, count, norm_all, pre_act)

        @pl.loop(0, count // 32)
        def _(n):
            rows = pl.ds(pl.multiple_of(lo + n * 32, 32), 32)
            value = pre_act[rows, :]
            cdf = 0.5 * (1.0 + lax.erf(value * 0.7071067811865476))
            slope = cdf + value * jnp.exp(-0.5 * value * value) * 0.3989422804014327
            hid_g[0, rows, :] = (value * cdf).astype(BF16)
            pre_g[0, rows, :] = (hid_grad[rows, :] * slope).astype(BF16)

        hid_ring.append(RingGather(hid_g, lo, count, on_y))
        pre_ring.append(RingGather(pre_g, lo, count, on_z))
        hid_ring[-1].start()
        pre_ring[-1].start()

    back = RowReduce(1)
    branch = RowReduce(0)

    def gain_part(cols, full):
        product = full * norm_all[:, cols].astype(F32)
        gain_sib[0, :, cols] = jnp.sum(product, axis=0, keepdims=True)

    pre_n[...] = pre_g[0].T
    back.multiply(pre_n, fc1_ref, gain_part)
    gain_pair = send(gain_sib.at[0], gain_sib.at[1], sibling)
    hid_ring[0].forward()
    pre_ring[0].forward()
    cut_rows.forward()
    slice_shared = []
    for slot, made in zip((1, 2, 3), slice_sent):
        made.wait_recv()
        place = grad_sl.at[slot, side_rows]
        slice_shared.append(send(place, place, sibling))
    hid_n[...] = hid_g[0].T
    branch.multiply(hid_n, fc2_ref)
    back.start()
    hid_ring[1].forward()
    pre_ring[1].forward()
    cut_rows.last()
    own_first = pl.multiple_of(y * sz.group_step, 128)
    grad_t[0] = grad_all[:, pl.ds(own_first, sz.group_pad)].T
    for made in slice_shared:
        made.wait_recv()
    for k in range(1, RING):
        grad_t[k] = grad_sl[k].T

    def add_start(buf, me, on_axis, total):
        buf[me] = total
        return [send(buf.at[me], buf.at[me], on_axis(k)) for k in (1, -1, 2)]

    def add_finish(buf, made):
        for one in made:
            one.wait_recv()
        return buf[0] + buf[1] + buf[2] + buf[3]

    def fc2_row(k):
        return y * (sz.group - sz.group_step) + ((z + STEP[k] + RING) % RING) * sz.owned

    def fc1_row(k):
        return ((y + STEP[k] + RING) % RING) * sz.owned

    fc2_grad = [
        WeightGrad(0, p, grad_t, hid_g, on_z, fc2_row, fc2_out) for p in range(2)
    ]
    fc1_grad = [
        WeightGrad(1, p, norm_t, pre_g, on_y, fc1_row, fc1_out) for p in range(2)
    ]
    hid_ring[0].finish()
    fc2_grad[0].multiply()
    back.ring.forward()
    branch.start()
    gain_pair.wait_recv()
    adding = add_start(gain_x, x, on_x, gain_sib[0] + gain_sib[1])
    cut_rows.wait(0, 5)
    for q in range(RING):

        @pl.when(z == q)
        def _():
            norm_t[0] = group_columns(norm_all[...], q).T

    for k in range(1, RING):
        norm_t[k] = norm_sl[k].T
    pre_ring[0].finish()
    fc1_grad[0].multiply()
    hid_ring[1].finish()
    fc2_grad[1].multiply()
    fc2_grad[0].ring.forward()
    pre_ring[1].finish()
    fc1_grad[1].multiply()
    total = add_finish(gain_x, adding)
    adding = add_start(gain_y, y, on_y, total)
    back.ring.finish()

    normed_grad = back.ring.total()
    unit = row_all[my_rows, :].astype(F32) * inv_ref[:, :1]
    scaled = normed_grad * gain
    inner = scaled - unit * jnp.mean(scaled * unit, axis=-1, keepdims=True)
    input_grad[...] = (
        (grad_all[my_rows, :].astype(F32) + inv_ref[:, :1] * inner).astype(BF16).astype(F32)
    )
    returned, via = [], []
    for j in range(sz.homes):
        total = pick(0, j) * input_grad[0 : sz.block_rows, :]
        for s in range(1, sz.slots):
            total += pick(s, j) * input_grad[s * sz.block_rows : (s + 1) * sz.block_rows, :]
        total = total.astype(BF16)
        if j == 0:
            tgrad[0] = total
            continue
        back_out[j - 1] = total
        source, place = back_out.at[j - 1], tgrad.at[j]
        if j < RING:
            via.append(send(source.at[:, cols1], midway_back.at[j - 1], on_z(-j)))
            returned.append(send(source.at[:, cols0], place.at[:, cols0], on_dp(-j)))
        else:
            returned.append(send(source, place, on_dp(-j)))
    branch.ring.forward()
    fc1_grad[0].ring.forward()
    total = add_finish(gain_y, adding)
    adding = add_start(gain_z, z, on_z, total)
    for j in range(1, RING):
        via[j - 1].wait_recv()
        returned.append(
            send(midway_back.at[j - 1], tgrad.at[j, :, cols1], on_y(-1), when=z + j >= RING)
        )

        @pl.when(z + j < RING)
        def _():
            tgrad[j, :, lo1:] = midway_back[j - 1]

    fc2_grad[1].ring.forward()
    fc1_grad[1].ring.forward()
    branch.ring.finish()
    mixed[...] = (row_all[my_rows, :].astype(F32) + branch.ring.total()).astype(BF16)
    stores = []

    def store(src, dst):
        stores.append(pltpu.make_async_copy(src, dst, store_sems.at[len(stores)]))
        stores[-1].start()

    def store_grad(grad, out):
        grad.finish()
        cols = pl.ds(grad.lo, grad.units)
        store(grad.out.at[:, cols], out.at[:, cols])

    store(mixed, mixed_ref)
    store_grad(fc2_grad[0], fc2_grad_ref)
    store_grad(fc1_grad[0], fc1_grad_ref)
    total = add_finish(gain_z, adding)
    gain_out[...] = (total / gain).reshape(width)
    store(gain_out, gain_grad_ref)
    for made in returned:
        made.wait_recv()
    store(tgrad, tgrad_ref)
    store_grad(fc2_grad[1], fc2_grad_ref)
    store_grad(fc1_grad[1], fc1_grad_ref)
    for made in stores:
        made.wait()
    for made in started:
        made.wait_send()
    if len(started) != copies:
        raise ValueError(len(started))


def hand_over_kernel(*refs):
    count = (len(refs) - 2) // 3
    source, target, held = refs[:count], refs[count : 2 * count], refs[2 * count : 3 * count]
    in_sems, out_sems = refs[-2:]
    loads, stores = [], []
    for i in range(count):
        loads.append(pltpu.make_async_copy(source[i], held[i], in_sems.at[i]))
        stores.append(pltpu.make_async_copy(held[i], target[i], out_sems.at[i]))
    for one in loads:
        one.start()
    for load, store in zip(loads, stores):
        load.wait()
        store.start()
    for one in stores:
        one.wait()


def hand_over(*arrays):
    anywhere = pl.BlockSpec(memory_space=pl.ANY)
    return pl.pallas_call(
        hand_over_kernel,
        out_shape=tuple(jax.ShapeDtypeStruct(a.shape, a.dtype) for a in arrays),
        in_specs=[anywhere] * len(arrays),
        out_specs=(anywhere,) * len(arrays),
        scratch_shapes=[pltpu.VMEM(a.shape, a.dtype) for a in arrays]
        + [pltpu.SemaphoreType.DMA((len(arrays),))] * 2,
        compiler_params=pltpu.CompilerParams(vmem_limit_bytes=60 * 1024 * 1024),
        name="hand_over",
    )(*arrays)


COPIES = 130


def local(tokens, norm_gain, fc1, fc2t, block_slot, out_grad):
    sz = Sizes(tokens.shape, fc1.shape, out_grad.shape)
    width, units = sz.width, sz.units
    vmem = pl.BlockSpec(memory_space=pltpu.VMEM)
    anywhere = pl.BlockSpec(memory_space=pl.ANY)
    slices = (RING, sz.rows, sz.group_pad)
    slices_t = (RING, sz.group_pad, sz.rows)
    pieces = (2, 2, 3, sz.owned_pad, sz.part_max)
    arrays = pl.pallas_call(
        functools.partial(kernel, sz, COPIES),
        out_shape=(
            jax.ShapeDtypeStruct((sz.own, width), BF16),
            jax.ShapeDtypeStruct(tokens.shape, BF16),
            jax.ShapeDtypeStruct((sz.owned, units), F32),
            jax.ShapeDtypeStruct((sz.owned, units), F32),
            jax.ShapeDtypeStruct((width,), F32),
        ),
        in_specs=[
            pl.BlockSpec(memory_space=pltpu.SMEM),
            vmem,
            anywhere,
            anywhere,
            anywhere,
            anywhere,
        ],
        out_specs=(anywhere,) * 5,
        scratch_shapes=[
            pltpu.VMEM((units, width), BF16),
            pltpu.VMEM((units, width), BF16),
            pltpu.VMEM(tokens.shape, BF16),
            pltpu.VMEM((RING - 1, sz.block_rows, sz.cuts[1][1]), BF16),
            pltpu.VMEM((RING - 1, sz.block_rows, sz.cuts[1][1]), BF16),
            pltpu.VMEM((sz.own, width), BF16),
            pltpu.VMEM(tokens.shape, BF16),
            pltpu.VMEM((sz.owned, units), F32),
            pltpu.VMEM((sz.owned, units), F32),
            pltpu.VMEM((width,), F32),
            pltpu.VMEM((sz.rows, width), BF16),
            pltpu.VMEM((sz.own, 128), F32),
            pltpu.VMEM((sz.rows, width), BF16),
            pltpu.VMEM((sz.rows, width), BF16),
            pltpu.VMEM((RING, sz.own, sz.group_pad), BF16),
            pltpu.VMEM(slices, BF16),
            pltpu.VMEM(slices, BF16),
            pltpu.VMEM(slices_t, BF16),
            pltpu.VMEM(slices_t, BF16),
            pltpu.VMEM((RING, units, sz.rows), BF16),
            pltpu.VMEM((RING, units, sz.rows), BF16),
            pltpu.VMEM((sz.rows, units), BF16),
            pltpu.VMEM((sz.rows, units), BF16),
            pltpu.VMEM((units, sz.rows), F32),
            pltpu.VMEM((units, sz.rows), F32),
            pltpu.VMEM((2, RING, sz.own, width), F32),
            pltpu.VMEM((2, RING, sz.own, width), BF16),
            pltpu.VMEM((2, RING, sz.own, width), BF16),
            pltpu.VMEM((2, 3, sz.own, width), BF16),
            pltpu.VMEM((2, 3, sz.own, width), BF16),
            pltpu.VMEM((2, 2, sz.sum_rows, sz.part_max), F32),
            pltpu.VMEM(pieces, BF16),
            pltpu.VMEM(pieces, BF16),
            pltpu.VMEM((sz.homes - 1, sz.block_rows, width), BF16),
            pltpu.VMEM((sz.own, width), F32),
            pltpu.VMEM((2, 1, width), F32),
            pltpu.VMEM((RING, 1, width), F32),
            pltpu.VMEM((RING, 1, width), F32),
            pltpu.VMEM((RING, 1, width), F32),
            pltpu.SemaphoreType.DMA((4,)),
            pltpu.SemaphoreType.DMA((7,)),
            pltpu.SemaphoreType.DMA((COPIES,)),
            pltpu.SemaphoreType.DMA((COPIES,)),
        ],
        compiler_params=pltpu.CompilerParams(
            collective_id=0, has_side_effects=True, vmem_limit_bytes=60 * 1024 * 1024
        ),
        cost_estimate=pl.CostEstimate(
            flops=12 * sz.rows * width * units,
            bytes_accessed=4 * width * units,
            transcendentals=2 * sz.rows * units,
        ),
        name="mlp_block",
    )(
        block_slot,
        norm_gain,
        tokens,
        fc1.T,
        fc2t.T,
        out_grad.reshape(sz.own, width),
    )
    mixed, tgrad, fc1_grad, fc2_grad, gain_grad = hand_over(*arrays)
    return mixed.reshape(out_grad.shape), tgrad, fc1_grad, fc2_grad, gain_grad


def solution(mesh):
    placed = (
        P("dp", "tensor", None),
        P(),
        P(None, "tensor"),
        P(None, "tensor"),
        P(),
        P("dp", "tensor", None),
    )
    return jax.shard_map(
        local,
        mesh=mesh,
        in_specs=placed,
        out_specs=(
            P("dp", "tensor", None),
            P("dp", "tensor", None),
            P("dp", "tensor"),
            P("dp", "tensor"),
            P(),
        ),
        check_vma=False,
    )
```

```python
import functools

import jax
import jax.numpy as jnp
from jax import lax
from jax.experimental import pallas as pl
from jax.experimental.pallas import tpu as pltpu
from jax.sharding import PartitionSpec as P

MESH = pl.DeviceIdType.MESH
ROW_DIMS = (((1,), (1,)), ((), ()))
RING = 4
RANKS = RING * RING
F32 = jnp.float32
BF16 = jnp.bfloat16

STEP = (0, -1, 1, 2)


def round_up(value, unit):
    return (value + unit - 1) // unit * unit


def chunk_of(width, limit):
    tiles = width // 128
    best = 1
    for count in range(1, tiles + 1):
        if tiles % count == 0 and count * 128 <= limit:
            best = count
    return best * 128


class Sizes:
    def __init__(self, tokens, fc1, out_grad):
        self.homes, self.block_rows, self.width = tokens
        self.units = fc1[1]
        self.slots = out_grad[0]
        self.own = self.slots * self.block_rows
        self.pair = 2 * self.own
        self.rows = RING * self.pair
        self.owned = self.width // RANKS
        self.owned_pad = round_up(self.owned, 16)
        self.group = RING * self.owned
        self.group_step = self.group // 128 * 128
        self.group_pad = round_up(self.group + (RING - 1) * (self.group - self.group_step), 128)
        self.sum_rows = self.group_pad + 8
        self.chunk = chunk_of(self.width, 640)
        first = round_up(self.units // 2, 128) - 128
        self.parts = ((0, first), (first, self.units - first))
        mid = round_up(self.width // 2, 128)
        self.cuts = ((0, mid), (mid, self.width - mid))
        self.part_max = max(count for _, count in self.parts)


def kernel(
    sz,
    copies,
    slot_ref,
    gain_ref,
    tokens_hbm,
    fc1_hbm,
    fc2_hbm,
    grad_hbm,
    mixed,
    tgrad,
    fc1_out,
    fc2_out,
    gain_out,
    fc1_ref,
    fc2_ref,
    arrived,
    midway,
    midway_back,
    row_all,
    inv_ref,
    grad_all,
    norm_all,
    norm_cut,
    grad_sl,
    norm_sl,
    grad_t,
    norm_t,
    hid_g,
    pre_g,
    hid_n,
    pre_n,
    pre_act,
    hid_grad,
    row_sum,
    sib_out,
    sib_in,
    rs_out,
    rs_in,
    wg_sum,
    wg_out,
    wg_in,
    back_out,
    input_grad,
    gain_sib,
    gain_x,
    gain_y,
    gain_z,
    local_sems,
    send_sems,
    recv_sems,
):
    dp = lax.axis_index("dp")
    t = lax.axis_index("tensor")
    y, z = dp // RING, dp % RING
    x, c = t // 2, t % 2
    own, width = sz.own, sz.width
    half = own // 2
    gain = gain_ref[...].reshape(1, width)

    def on_dp(k):
        return ((dp + k + RANKS) % RANKS, t)

    def on_x(k):
        return (dp, ((x + k + RING) % RING) * 2 + c)

    def on_y(k):
        return (((y + k + RING) % RING) * RING + z, t)

    def on_z(k):
        return (y * RING + (z + k + RING) % RING, t)

    sibling = (dp, t + 1 - 2 * c)

    started = []

    class Guarded:
        def __init__(self, made, when, arrives):
            self.made, self.when, self.arrives = made, when, arrives

        def wait_recv(self):
            pl.when(self.arrives)(self.made.wait_recv)

        def wait_send(self):
            pl.when(self.when)(self.made.wait_send)

    def send(src, dst, device, when=None, arrives=None):
        index = len(started)
        made = pltpu.make_async_remote_copy(
            src_ref=src,
            dst_ref=dst,
            send_sem=send_sems.at[index],
            recv_sem=recv_sems.at[index],
            device_id=device,
            device_id_type=MESH,
        )
        if when is None:
            made.start()
        else:
            pl.when(when)(made.start)
            made = Guarded(made, when, when if arrives is None else arrives)
        started.append(made)
        return made

    my_rows = pl.ds(pl.multiple_of(c * own, own), own)
    load_grad = pltpu.make_async_copy(grad_hbm, grad_all.at[my_rows], local_sems.at[0])
    load_token = pltpu.make_async_copy(tokens_hbm.at[0], arrived.at[0], local_sems.at[1])
    load_fc2 = pltpu.make_async_copy(fc2_hbm, fc2_ref, local_sems.at[2])
    load_fc1 = pltpu.make_async_copy(fc1_hbm, fc1_ref, local_sems.at[3])
    load_grad.start()
    load_token.start()

    partners = [on_dp(k) for k in range(1, sz.homes)]
    partners += [on_dp(-k) for k in range(1, sz.homes)]
    partners += [on_y(k) for k in (1, -1, 2)]
    partners += [on_z(k) for k in (1, -1, 2)]
    partners += [on_x(k) for k in (1, -1, 2)]
    partners += [sibling]
    barrier = pltpu.get_barrier_semaphore()
    for device in partners:
        pl.semaphore_signal(barrier, inc=1, device_id=device, device_id_type=MESH)
    pl.semaphore_wait(barrier, len(partners))

    class RowGather:
        def __init__(self, view):
            self.view = view

        def part(self, slot, lo, count):
            place = sz.pair * slot + c * own + lo
            return self.view(pl.ds(pl.multiple_of(place, 16), count))

        def start(self):
            mine = self.part(0, 0, own)
            self.right = send(mine, self.part(1, 0, own), on_x(1))
            self.left = send(mine, self.part(2, 0, own), on_x(-1))
            self.shared = [send(mine, mine, sibling)]

        def forward(self):
            self.right.wait_recv()
            self.right2 = send(self.part(1, 0, half), self.part(3, 0, half), on_x(1))
            whole = self.part(1, 0, own)
            self.shared.append(send(whole, whole, sibling))
            self.left.wait_recv()
            rest = own - half
            self.left2 = send(self.part(2, half, rest), self.part(3, half, rest), on_x(-1))
            whole = self.part(2, 0, own)
            self.shared.append(send(whole, whole, sibling))

        def last(self):
            self.right2.wait_recv()
            low = self.part(3, 0, half)
            self.shared.append(send(low, low, sibling))
            self.left2.wait_recv()
            high = self.part(3, half, own - half)
            self.shared.append(send(high, high, sibling))

        def wait(self, first, stop):
            for made in self.shared[first:stop]:
                made.wait_recv()

    class RingGather:
        def __init__(self, buf, lo, count, on_axis):
            self.buf, self.on_axis = buf, on_axis
            self.whole = pl.ds(lo, count)
            self.low = pl.ds(lo, count // 2)
            self.high = pl.ds(lo + count // 2, count // 2)

        def start(self):
            buf, on_axis = self.buf, self.on_axis
            mine = buf.at[0, self.whole]
            self.right = send(mine, buf.at[1, self.whole], on_axis(1))
            self.left = send(mine, buf.at[2, self.whole], on_axis(-1))

        def forward(self):
            buf, on_axis = self.buf, self.on_axis
            self.right.wait_recv()
            self.right2 = send(buf.at[1, self.low], buf.at[3, self.low], on_axis(1))
            self.left.wait_recv()
            self.left2 = send(buf.at[2, self.high], buf.at[3, self.high], on_axis(-1))

        def finish(self):
            self.right2.wait_recv()
            self.left2.wait_recv()

    class RingReduce:
        def __init__(self, part, out, into, on_axis, mid, count):
            self.part, self.out, self.into = part, out, into
            self.on_axis, self.mid, self.count = on_axis, mid, count

        def start(self):
            mid, rest = self.mid, self.count - self.mid
            lo, hi = pl.ds(0, mid), pl.ds(mid, rest)
            part, out, into, on_axis = self.part, self.out, self.into, self.on_axis
            out[0, lo] = part(3, 0, mid).astype(BF16)
            self.far_right = send(out.at[0, lo], into.at[0, lo], on_axis(1))
            out[0, hi] = part(3, mid, rest).astype(BF16)
            self.far_left = send(out.at[0, hi], into.at[0, hi], on_axis(-1))
            out[1, hi] = part(2, mid, rest).astype(BF16)
            self.near_right = send(out.at[1, hi], into.at[1, hi], on_axis(1))
            out[2, lo] = part(1, 0, mid).astype(BF16)
            self.near_left = send(out.at[2, lo], into.at[2, lo], on_axis(-1))

        def forward(self):
            mid, rest = self.mid, self.count - self.mid
            lo, hi = pl.ds(0, mid), pl.ds(mid, rest)
            part, out, into, on_axis = self.part, self.out, self.into, self.on_axis
            self.far_right.wait_recv()
            out[1, lo] = (part(2, 0, mid) + into[0, lo].astype(F32)).astype(BF16)
            self.sum_right = send(out.at[1, lo], into.at[1, lo], on_axis(1))
            self.far_left.wait_recv()
            out[2, hi] = (part(1, mid, rest) + into[0, hi].astype(F32)).astype(BF16)
            self.sum_left = send(out.at[2, hi], into.at[2, hi], on_axis(-1))

        def finish(self):
            self.near_right.wait_recv()
            self.near_left.wait_recv()
            self.sum_right.wait_recv()
            self.sum_left.wait_recv()

        def total(self):
            first = self.part(0, 0, self.count) + self.into[1].astype(F32)
            return first + self.into[2].astype(F32)

    class RowReduce:
        def __init__(self, index):
            self.index = index

        def multiply(self, lhs, weight, also=None):
            index = self.index

            @pl.loop(0, width // sz.chunk)
            def _(n):
                cols = pl.ds(pl.multiple_of(n * sz.chunk, sz.chunk), sz.chunk)
                full = jnp.dot(lhs[...], weight[:, cols], preferred_element_type=F32)
                for k in range(RING):
                    even = full[sz.pair * k : sz.pair * k + own]
                    odd = full[sz.pair * k + own : sz.pair * (k + 1)]
                    row_sum[index, k, :, cols] = jnp.where(c == 0, even, odd)
                    sib_out[index, k, :, cols] = jnp.where(c == 0, odd, even).astype(BF16)
                if also is not None:
                    also(cols, full)

            self.copy = send(sib_out.at[index], sib_in.at[index], sibling)

        def start(self):
            index = self.index
            self.copy.wait_recv()
            row_sum[index] = row_sum[index] + sib_in[index].astype(F32)

            def part(k, lo, count):
                return row_sum[index, k, lo : lo + count]

            self.ring = RingReduce(part, rs_out.at[index], rs_in.at[index], on_x, half, own)
            self.ring.start()

    class WeightGrad:
        def __init__(self, index, p, slices, blocks, on_axis, owner_row, out):
            self.index, self.p, self.out = index, p, out
            self.slices, self.blocks = slices, blocks
            self.lo, self.units = sz.parts[p]
            self.on_axis, self.owner_row = on_axis, owner_row

        def multiply(self):
            index, p, lo, units = self.index, self.p, self.lo, self.units
            step = sz.group_pad // 2

            @pl.loop(0, 2)
            def _(m):
                rows = pl.ds(pl.multiple_of(m * step, step), step)
                total = None
                for k in range(RING):
                    one = lax.dot_general(
                        self.slices[k, rows, :],
                        self.blocks[k, lo : lo + units, :],
                        ROW_DIMS,
                        preferred_element_type=F32,
                    )
                    total = one if total is None else total + one
                wg_sum[index, p, rows, 0:units] = total

            wg_sum[index, p, sz.group_pad : sz.sum_rows, 0:units] = jnp.zeros((8, units), F32)

            def part(k, first, count):
                place = pl.multiple_of(self.owner_row(k) + first, 8)
                return wg_sum[index, p, pl.ds(place, count), 0:units]

            self.ring = RingReduce(
                part,
                wg_out.at[index, p, :, :, pl.ds(0, units)],
                wg_in.at[index, p, :, :, pl.ds(0, units)],
                self.on_axis,
                round_up(sz.owned_pad // 2, 16),
                sz.owned_pad,
            )
            self.ring.start()

        def finish(self):
            self.ring.finish()
            self.out[:, self.lo : self.lo + self.units] = self.ring.total()[: sz.owned]

    grad_rows = RowGather(lambda rows: grad_all.at[rows])
    cut_rows = RowGather(lambda rows: norm_sl.at[pl.ds(1, RING - 1), rows])
    (lo0, count0), (lo1, count1) = sz.cuts
    cols0, cols1 = pl.ds(lo0, count0), pl.ds(lo1, count1)
    via = []
    for j in range(1, RING):
        via.append(send(tokens_hbm.at[j, :, cols1], midway.at[j - 1], on_z(j)))
    direct = []
    for j in range(1, sz.homes):
        direct.append(send(tokens_hbm.at[j, :, cols0], arrived.at[j, :, cols0], on_dp(j)))
    last = []
    for j in range(RING, sz.homes):
        last.append(send(tokens_hbm.at[j, :, cols1], arrived.at[j, :, cols1], on_dp(j)))
    load_grad.wait()
    grad_rows.start()
    load_fc2.start()
    load_fc1.start()

    def pick(s, j):
        home = (dp - j + RANKS) % RANKS
        named = slot_ref[home * sz.homes + j]
        return jnp.where(named == dp * sz.slots + s, 1.0, 0.0).astype(F32)

    def group_columns(rows, q):
        cuts = []
        for k in range(RING):
            first = sz.owned * (RING * k + q)
            cuts.append(rows[:, first : first + sz.owned])
        cuts.append(jnp.zeros((rows.shape[0], sz.group_pad - sz.group), rows.dtype))
        return jnp.concatenate(cuts, axis=1)

    for j in range(1, RING):
        via[j - 1].wait_recv()
        last.append(
            send(midway.at[j - 1], arrived.at[j, :, cols1], on_y(1), when=z < j)
        )

        @pl.when(z >= j)
        def _():
            arrived[j, :, lo1:] = midway[j - 1]

    routed = (direct, last)
    load_token.wait()
    grad_rows.forward()
    row_parts = []
    for n, (lo, count) in enumerate(sz.cuts):
        cols = slice(lo, lo + count)
        for made in routed[n]:
            made.wait_recv()
        for s in range(sz.slots):
            total = pick(s, 0) * arrived[0, :, cols].astype(F32)
            for j in range(1, sz.homes):
                total += pick(s, j) * arrived[j, :, cols].astype(F32)
            place = c * own + s * sz.block_rows
            rows = pl.ds(pl.multiple_of(place, sz.block_rows), sz.block_rows)
            row_all[rows, cols] = total.astype(BF16)
        one = RowGather(lambda rows, lo=lo, count=count: row_all.at[rows, pl.ds(lo, count)])
        one.start()
        row_parts.append(one)
    row_parts[0].forward()
    grad_rows.last()

    def normed_rows(rows):
        value = row_all[rows, :].astype(F32)
        inv = lax.rsqrt(jnp.mean(value * value, axis=-1, keepdims=True) + 1e-06)
        return value * inv, inv

    def norm_range(first, stop):
        @pl.loop(first // 16, stop // 16)
        def _(n):
            rows = pl.ds(pl.multiple_of(n * 16, 16), 16)
            unit, _ = normed_rows(rows)
            norm_all[rows, :] = (unit * gain).astype(BF16)

    unit_own, inv = normed_rows(my_rows)
    inv_ref[...] = jnp.broadcast_to(inv, inv_ref.shape)
    norm_own = (unit_own * gain).astype(BF16)
    for q in range(RING):
        norm_cut[q] = group_columns(norm_own, q)
    cut_sent = []
    for k, slot in ((1, 1), (-1, 2), (2, 3)):
        cut_sent.append(
            send(norm_cut.at[(z + k + RING) % RING], norm_sl.at[slot, my_rows], on_z(k))
        )
    row_parts[1].forward()
    grad_rows.wait(0, 5)
    side = sz.rows // 2
    side_rows = pl.ds(pl.multiple_of(c * side, side), side)
    slice_sent = []
    for k, slot in ((1, 1), (-1, 2), (2, 3)):
        first = pl.multiple_of(((y + k + RING) % RING) * sz.group_step, 128)
        slice_sent.append(
            send(
                grad_all.at[side_rows, pl.ds(first, sz.group_pad)],
                grad_sl.at[slot, side_rows],
                on_y(k),
            )
        )
    row_parts[0].last()

    load_fc2.wait()

    def multiply_in(lhs, lo, count, rows, out):
        @pl.loop(0, width // sz.chunk)
        def _(n):
            cols = pl.ds(pl.multiple_of(n * sz.chunk, sz.chunk), sz.chunk)
            part = lax.dot_general(
                lhs[lo : lo + count, cols], rows[:, cols], ROW_DIMS, preferred_element_type=F32
            )

            @pl.when(n == 0)
            def _():
                out[lo : lo + count, :] = part

            @pl.when(n > 0)
            def _():
                out[lo : lo + count, :] += part

    multiply_in(fc2_ref, *sz.parts[0], grad_all, hid_grad)
    row_parts[1].last()
    multiply_in(fc2_ref, *sz.parts[1], grad_all, hid_grad)
    for one in row_parts:
        one.wait(0, 3)
    norm_range(0, 3 * sz.pair)
    for made in cut_sent:
        made.wait_recv()
    for one in row_parts:
        one.wait(3, 5)
    cut_rows.start()
    norm_range(3 * sz.pair, sz.rows)
    load_fc1.wait()

    hid_ring, pre_ring = [], []
    for lo, count in sz.parts:
        multiply_in(fc1_ref, lo, count, norm_all, pre_act)

        @pl.loop(0, count // 32)
        def _(n):
            rows = pl.ds(pl.multiple_of(lo + n * 32, 32), 32)
            value = pre_act[rows, :]
            cdf = 0.5 * (1.0 + lax.erf(value * 0.7071067811865476))
            slope = cdf + value * jnp.exp(-0.5 * value * value) * 0.3989422804014327
            hid_g[0, rows, :] = (value * cdf).astype(BF16)
            pre_g[0, rows, :] = (hid_grad[rows, :] * slope).astype(BF16)

        hid_ring.append(RingGather(hid_g, lo, count, on_y))
        pre_ring.append(RingGather(pre_g, lo, count, on_z))
        hid_ring[-1].start()
        pre_ring[-1].start()

    back = RowReduce(1)
    branch = RowReduce(0)

    def gain_part(cols, full):
        product = full * norm_all[:, cols].astype(F32)
        gain_sib[0, :, cols] = jnp.sum(product, axis=0, keepdims=True)

    pre_n[...] = pre_g[0].T
    back.multiply(pre_n, fc1_ref, gain_part)
    gain_pair = send(gain_sib.at[0], gain_sib.at[1], sibling)
    hid_ring[0].forward()
    pre_ring[0].forward()
    cut_rows.forward()
    slice_shared = []
    for slot, made in zip((1, 2, 3), slice_sent):
        made.wait_recv()
        place = grad_sl.at[slot, side_rows]
        slice_shared.append(send(place, place, sibling))
    hid_n[...] = hid_g[0].T
    branch.multiply(hid_n, fc2_ref)
    back.start()
    hid_ring[1].forward()
    pre_ring[1].forward()
    cut_rows.last()
    own_first = pl.multiple_of(y * sz.group_step, 128)
    grad_t[0] = grad_all[:, pl.ds(own_first, sz.group_pad)].T
    for made in slice_shared:
        made.wait_recv()
    for k in range(1, RING):
        grad_t[k] = grad_sl[k].T

    def add_start(buf, me, on_axis, total):
        buf[me] = total
        return [send(buf.at[me], buf.at[me], on_axis(k)) for k in (1, -1, 2)]

    def add_finish(buf, made):
        for one in made:
            one.wait_recv()
        return buf[0] + buf[1] + buf[2] + buf[3]

    def fc2_row(k):
        return y * (sz.group - sz.group_step) + ((z + STEP[k] + RING) % RING) * sz.owned

    def fc1_row(k):
        return ((y + STEP[k] + RING) % RING) * sz.owned

    fc2_grad = [
        WeightGrad(0, p, grad_t, hid_g, on_z, fc2_row, fc2_out) for p in range(2)
    ]
    fc1_grad = [
        WeightGrad(1, p, norm_t, pre_g, on_y, fc1_row, fc1_out) for p in range(2)
    ]
    hid_ring[0].finish()
    fc2_grad[0].multiply()
    back.ring.forward()
    branch.start()
    gain_pair.wait_recv()
    adding = add_start(gain_x, x, on_x, gain_sib[0] + gain_sib[1])
    cut_rows.wait(0, 5)
    for q in range(RING):

        @pl.when(z == q)
        def _():
            norm_t[0] = group_columns(norm_all[...], q).T

    for k in range(1, RING):
        norm_t[k] = norm_sl[k].T
    pre_ring[0].finish()
    fc1_grad[0].multiply()
    hid_ring[1].finish()
    fc2_grad[1].multiply()
    fc2_grad[0].ring.forward()
    pre_ring[1].finish()
    fc1_grad[1].multiply()
    total = add_finish(gain_x, adding)
    adding = add_start(gain_y, y, on_y, total)
    back.ring.finish()

    normed_grad = back.ring.total()
    unit = row_all[my_rows, :].astype(F32) * inv_ref[:, :1]
    scaled = normed_grad * gain
    inner = scaled - unit * jnp.mean(scaled * unit, axis=-1, keepdims=True)
    input_grad[...] = (
        (grad_all[my_rows, :].astype(F32) + inv_ref[:, :1] * inner).astype(BF16).astype(F32)
    )
    returned, via = [], []
    for j in range(sz.homes):
        total = pick(0, j) * input_grad[0 : sz.block_rows, :]
        for s in range(1, sz.slots):
            total += pick(s, j) * input_grad[s * sz.block_rows : (s + 1) * sz.block_rows, :]
        total = total.astype(BF16)
        if j == 0:
            tgrad[0] = total
            continue
        back_out[j - 1] = total
        source, place = back_out.at[j - 1], tgrad.at[j]
        if j < RING:
            via.append(send(source.at[:, cols1], midway_back.at[j - 1], on_z(-j)))
            returned.append(send(source.at[:, cols0], place.at[:, cols0], on_dp(-j)))
        else:
            returned.append(send(source, place, on_dp(-j)))
    branch.ring.forward()
    fc1_grad[0].ring.forward()
    total = add_finish(gain_y, adding)
    adding = add_start(gain_z, z, on_z, total)
    for j in range(1, RING):
        via[j - 1].wait_recv()
        returned.append(
            send(midway_back.at[j - 1], tgrad.at[j, :, cols1], on_y(-1), when=z + j >= RING)
        )

        @pl.when(z + j < RING)
        def _():
            tgrad[j, :, lo1:] = midway_back[j - 1]

    fc2_grad[1].ring.forward()
    fc1_grad[1].ring.forward()
    branch.ring.finish()
    mixed[...] = (row_all[my_rows, :].astype(F32) + branch.ring.total()).astype(BF16)
    fc2_grad[0].finish()
    fc1_grad[0].finish()
    total = add_finish(gain_z, adding)
    gain_out[...] = (total / gain).reshape(width)
    for made in returned:
        made.wait_recv()
    fc2_grad[-1].finish()
    fc1_grad[-1].finish()
    for made in started:
        made.wait_send()
    if len(started) != copies:
        raise ValueError(len(started))


def hand_over_kernel(*refs):
    count = len(refs) // 2
    sems = refs[-1]
    made = [
        pltpu.make_async_copy(refs[i], refs[count + i], sems.at[i]) for i in range(count)
    ]
    for one in made:
        one.start()
    for one in made:
        one.wait()


def hand_over(*arrays):
    vmem = pl.BlockSpec(memory_space=pltpu.VMEM)
    anywhere = pl.BlockSpec(memory_space=pl.ANY)
    return pl.pallas_call(
        hand_over_kernel,
        out_shape=tuple(jax.ShapeDtypeStruct(a.shape, a.dtype) for a in arrays),
        in_specs=[vmem] * len(arrays),
        out_specs=(anywhere,) * len(arrays),
        scratch_shapes=[pltpu.SemaphoreType.DMA((len(arrays),))],
        compiler_params=pltpu.CompilerParams(vmem_limit_bytes=1024 * 1024),
        name="hand_over",
    )(*arrays)


COPIES = 130


def local(tokens, norm_gain, fc1, fc2t, block_slot, out_grad):
    sz = Sizes(tokens.shape, fc1.shape, out_grad.shape)
    width, units = sz.width, sz.units
    vmem = pl.BlockSpec(memory_space=pltpu.VMEM)
    anywhere = pl.BlockSpec(memory_space=pl.ANY)
    slices = (RING, sz.rows, sz.group_pad)
    slices_t = (RING, sz.group_pad, sz.rows)
    pieces = (2, 2, 3, sz.owned_pad, sz.part_max)
    arrays = pl.pallas_call(
        functools.partial(kernel, sz, COPIES),
        out_shape=(
            pltpu.VMEM((sz.own, width), BF16),
            pltpu.VMEM(tokens.shape, BF16),
            pltpu.VMEM((sz.owned, units), F32),
            pltpu.VMEM((sz.owned, units), F32),
            pltpu.VMEM((width,), F32),
        ),
        in_specs=[
            pl.BlockSpec(memory_space=pltpu.SMEM),
            vmem,
            anywhere,
            anywhere,
            anywhere,
            anywhere,
        ],
        out_specs=(vmem,) * 5,
        scratch_shapes=[
            pltpu.VMEM((units, width), BF16),
            pltpu.VMEM((units, width), BF16),
            pltpu.VMEM(tokens.shape, BF16),
            pltpu.VMEM((RING - 1, sz.block_rows, sz.cuts[1][1]), BF16),
            pltpu.VMEM((RING - 1, sz.block_rows, sz.cuts[1][1]), BF16),
            pltpu.VMEM((sz.rows, width), BF16),
            pltpu.VMEM((sz.own, 128), F32),
            pltpu.VMEM((sz.rows, width), BF16),
            pltpu.VMEM((sz.rows, width), BF16),
            pltpu.VMEM((RING, sz.own, sz.group_pad), BF16),
            pltpu.VMEM(slices, BF16),
            pltpu.VMEM(slices, BF16),
            pltpu.VMEM(slices_t, BF16),
            pltpu.VMEM(slices_t, BF16),
            pltpu.VMEM((RING, units, sz.rows), BF16),
            pltpu.VMEM((RING, units, sz.rows), BF16),
            pltpu.VMEM((sz.rows, units), BF16),
            pltpu.VMEM((sz.rows, units), BF16),
            pltpu.VMEM((units, sz.rows), F32),
            pltpu.VMEM((units, sz.rows), F32),
            pltpu.VMEM((2, RING, sz.own, width), F32),
            pltpu.VMEM((2, RING, sz.own, width), BF16),
            pltpu.VMEM((2, RING, sz.own, width), BF16),
            pltpu.VMEM((2, 3, sz.own, width), BF16),
            pltpu.VMEM((2, 3, sz.own, width), BF16),
            pltpu.VMEM((2, 2, sz.sum_rows, sz.part_max), F32),
            pltpu.VMEM(pieces, BF16),
            pltpu.VMEM(pieces, BF16),
            pltpu.VMEM((sz.homes - 1, sz.block_rows, width), BF16),
            pltpu.VMEM((sz.own, width), F32),
            pltpu.VMEM((2, 1, width), F32),
            pltpu.VMEM((RING, 1, width), F32),
            pltpu.VMEM((RING, 1, width), F32),
            pltpu.VMEM((RING, 1, width), F32),
            pltpu.SemaphoreType.DMA((4,)),
            pltpu.SemaphoreType.DMA((COPIES,)),
            pltpu.SemaphoreType.DMA((COPIES,)),
        ],
        compiler_params=pltpu.CompilerParams(
            collective_id=0, has_side_effects=True, vmem_limit_bytes=60 * 1024 * 1024
        ),
        cost_estimate=pl.CostEstimate(
            flops=12 * sz.rows * width * units,
            bytes_accessed=4 * width * units,
            transcendentals=2 * sz.rows * units,
        ),
        name="mlp_block",
    )(
        block_slot,
        norm_gain,
        tokens,
        fc1.T,
        fc2t.T,
        out_grad.reshape(sz.own, width),
    )
    mixed, tgrad, fc1_grad, fc2_grad, gain_grad = hand_over(*arrays)
    return mixed.reshape(out_grad.shape), tgrad, fc1_grad, fc2_grad, gain_grad


def solution(mesh):
    placed = (
        P("dp", "tensor", None),
        P(),
        P(None, "tensor"),
        P(None, "tensor"),
        P(),
        P("dp", "tensor", None),
    )
    return jax.shard_map(
        local,
        mesh=mesh,
        in_specs=placed,
        out_specs=(
            P("dp", "tensor", None),
            P("dp", "tensor", None),
            P("dp", "tensor"),
            P("dp", "tensor"),
            P(),
        ),
        check_vma=False,
    )
```

```python
import functools

import jax
import jax.numpy as jnp
from jax import lax
from jax.experimental import pallas as pl
from jax.experimental.pallas import tpu as pltpu
from jax.sharding import PartitionSpec as P

MESH = pl.DeviceIdType.MESH
ROW_DIMS = (((1,), (1,)), ((), ()))
RING = 4
RANKS = RING * RING
F32 = jnp.float32
BF16 = jnp.bfloat16

STEP = (0, -1, 1, 2)


def round_up(value, unit):
    return (value + unit - 1) // unit * unit


def chunk_of(width, limit):
    tiles = width // 128
    best = 1
    for count in range(1, tiles + 1):
        if tiles % count == 0 and count * 128 <= limit:
            best = count
    return best * 128


class Sizes:
    def __init__(self, tokens, fc1, out_grad):
        self.homes, self.block_rows, self.width = tokens
        self.units = fc1[1]
        self.slots = out_grad[0]
        self.own = self.slots * self.block_rows
        self.pair = 2 * self.own
        self.rows = RING * self.pair
        self.owned = self.width // RANKS
        self.owned_pad = round_up(self.owned, 16)
        self.group = RING * self.owned
        self.group_step = self.group // 128 * 128
        self.group_pad = round_up(self.group + (RING - 1) * (self.group - self.group_step), 128)
        self.sum_rows = self.group_pad + 8
        self.chunk = chunk_of(self.width, 640)
        first = round_up(self.units // 2, 128) - 128
        self.parts = ((0, first), (first, self.units - first))
        mid = round_up(self.width // 2, 128)
        self.cuts = ((0, mid), (mid, self.width - mid))
        self.part_max = max(count for _, count in self.parts)


def kernel(
    sz,
    copies,
    slot_ref,
    gain_ref,
    tokens_hbm,
    fc1_hbm,
    fc2_hbm,
    grad_hbm,
    mixed,
    tgrad,
    fc1_out,
    fc2_out,
    gain_out,
    fc1_ref,
    fc2_ref,
    arrived,
    midway,
    midway_back,
    row_all,
    inv_ref,
    grad_all,
    norm_all,
    norm_cut,
    grad_sl,
    norm_sl,
    grad_t,
    norm_t,
    hid_g,
    pre_g,
    hid_n,
    pre_n,
    pre_act,
    hid_grad,
    row_sum,
    sib_out,
    sib_in,
    rs_out,
    rs_in,
    wg_sum,
    wg_out,
    wg_in,
    back_out,
    input_grad,
    gain_sib,
    gain_x,
    gain_y,
    gain_z,
    local_sems,
    send_sems,
    recv_sems,
):
    dp = lax.axis_index("dp")
    t = lax.axis_index("tensor")
    y, z = dp // RING, dp % RING
    x, c = t // 2, t % 2
    own, width = sz.own, sz.width
    half = own // 2
    gain = gain_ref[...].reshape(1, width)

    def on_dp(k):
        return ((dp + k + RANKS) % RANKS, t)

    def on_x(k):
        return (dp, ((x + k + RING) % RING) * 2 + c)

    def on_y(k):
        return (((y + k + RING) % RING) * RING + z, t)

    def on_z(k):
        return (y * RING + (z + k + RING) % RING, t)

    sibling = (dp, t + 1 - 2 * c)

    started = []

    class Guarded:
        def __init__(self, made, when, arrives):
            self.made, self.when, self.arrives = made, when, arrives

        def wait_recv(self):
            pl.when(self.arrives)(self.made.wait_recv)

        def wait_send(self):
            pl.when(self.when)(self.made.wait_send)

    def send(src, dst, device, when=None, arrives=None):
        index = len(started)
        made = pltpu.make_async_remote_copy(
            src_ref=src,
            dst_ref=dst,
            send_sem=send_sems.at[index],
            recv_sem=recv_sems.at[index],
            device_id=device,
            device_id_type=MESH,
        )
        if when is None:
            made.start()
        else:
            pl.when(when)(made.start)
            made = Guarded(made, when, when if arrives is None else arrives)
        started.append(made)
        return made

    my_rows = pl.ds(pl.multiple_of(c * own, own), own)
    load_grad = pltpu.make_async_copy(grad_hbm, grad_all.at[my_rows], local_sems.at[0])
    load_token = pltpu.make_async_copy(tokens_hbm.at[0], arrived.at[0], local_sems.at[1])
    load_fc2 = pltpu.make_async_copy(fc2_hbm, fc2_ref, local_sems.at[2])
    load_fc1 = pltpu.make_async_copy(fc1_hbm, fc1_ref, local_sems.at[3])
    load_grad.start()
    load_token.start()

    partners = [on_dp(k) for k in range(1, sz.homes)]
    partners += [on_dp(-k) for k in range(1, sz.homes)]
    partners += [on_y(k) for k in (1, -1, 2)]
    partners += [on_z(k) for k in (1, -1, 2)]
    partners += [on_x(k) for k in (1, -1, 2)]
    partners += [sibling]
    barrier = pltpu.get_barrier_semaphore()
    for device in partners:
        pl.semaphore_signal(barrier, inc=1, device_id=device, device_id_type=MESH)
    pl.semaphore_wait(barrier, len(partners))

    class RowGather:
        def __init__(self, view):
            self.view = view

        def part(self, slot, lo, count):
            place = sz.pair * slot + c * own + lo
            return self.view(pl.ds(pl.multiple_of(place, 16), count))

        def start(self):
            mine = self.part(0, 0, own)
            self.right = send(mine, self.part(1, 0, own), on_x(1))
            self.left = send(mine, self.part(2, 0, own), on_x(-1))
            self.shared = [send(mine, mine, sibling)]

        def forward(self):
            self.right.wait_recv()
            self.right2 = send(self.part(1, 0, half), self.part(3, 0, half), on_x(1))
            whole = self.part(1, 0, own)
            self.shared.append(send(whole, whole, sibling))
            self.left.wait_recv()
            rest = own - half
            self.left2 = send(self.part(2, half, rest), self.part(3, half, rest), on_x(-1))
            whole = self.part(2, 0, own)
            self.shared.append(send(whole, whole, sibling))

        def last(self):
            self.right2.wait_recv()
            low = self.part(3, 0, half)
            self.shared.append(send(low, low, sibling))
            self.left2.wait_recv()
            high = self.part(3, half, own - half)
            self.shared.append(send(high, high, sibling))

        def wait(self, first, stop):
            for made in self.shared[first:stop]:
                made.wait_recv()

    class RingGather:
        def __init__(self, buf, lo, count, on_axis, low):
            self.buf, self.on_axis = buf, on_axis
            self.whole = pl.ds(lo, count)
            self.low = pl.ds(lo, low)
            self.high = pl.ds(lo + low, count - low)

        def start(self):
            buf, on_axis = self.buf, self.on_axis
            mine = buf.at[0, self.whole]
            self.right = send(mine, buf.at[1, self.whole], on_axis(1))
            self.left = send(mine, buf.at[2, self.whole], on_axis(-1))

        def forward(self):
            buf, on_axis = self.buf, self.on_axis
            self.right.wait_recv()
            self.right2 = send(buf.at[1, self.low], buf.at[3, self.low], on_axis(1))
            self.left.wait_recv()
            self.left2 = send(buf.at[2, self.high], buf.at[3, self.high], on_axis(-1))

        def finish(self):
            self.right2.wait_recv()
            self.left2.wait_recv()

    class RingReduce:
        def __init__(self, part, out, into, on_axis, mid, count):
            self.part, self.out, self.into = part, out, into
            self.on_axis, self.mid, self.count = on_axis, mid, count

        def start(self):
            mid, rest = self.mid, self.count - self.mid
            lo, hi = pl.ds(0, mid), pl.ds(mid, rest)
            part, out, into, on_axis = self.part, self.out, self.into, self.on_axis
            out[0, lo] = part(3, 0, mid).astype(BF16)
            self.far_right = send(out.at[0, lo], into.at[0, lo], on_axis(1))
            out[0, hi] = part(3, mid, rest).astype(BF16)
            self.far_left = send(out.at[0, hi], into.at[0, hi], on_axis(-1))
            out[1, hi] = part(2, mid, rest).astype(BF16)
            self.near_right = send(out.at[1, hi], into.at[1, hi], on_axis(1))
            out[2, lo] = part(1, 0, mid).astype(BF16)
            self.near_left = send(out.at[2, lo], into.at[2, lo], on_axis(-1))

        def forward(self):
            mid, rest = self.mid, self.count - self.mid
            lo, hi = pl.ds(0, mid), pl.ds(mid, rest)
            part, out, into, on_axis = self.part, self.out, self.into, self.on_axis
            self.far_right.wait_recv()
            out[1, lo] = (part(2, 0, mid) + into[0, lo].astype(F32)).astype(BF16)
            self.sum_right = send(out.at[1, lo], into.at[1, lo], on_axis(1))
            self.far_left.wait_recv()
            out[2, hi] = (part(1, mid, rest) + into[0, hi].astype(F32)).astype(BF16)
            self.sum_left = send(out.at[2, hi], into.at[2, hi], on_axis(-1))

        def finish(self):
            self.near_right.wait_recv()
            self.near_left.wait_recv()
            self.sum_right.wait_recv()
            self.sum_left.wait_recv()

        def total(self):
            first = self.part(0, 0, self.count) + self.into[1].astype(F32)
            return first + self.into[2].astype(F32)

    class RowReduce:
        def __init__(self, index):
            self.index = index

        def multiply(self, lhs, weight, also=None):
            index = self.index

            @pl.loop(0, width // sz.chunk)
            def _(n):
                cols = pl.ds(pl.multiple_of(n * sz.chunk, sz.chunk), sz.chunk)
                full = jnp.dot(lhs[...], weight[:, cols], preferred_element_type=F32)
                for k in range(RING):
                    even = full[sz.pair * k : sz.pair * k + own]
                    odd = full[sz.pair * k + own : sz.pair * (k + 1)]
                    row_sum[index, k, :, cols] = jnp.where(c == 0, even, odd)
                    sib_out[index, k, :, cols] = jnp.where(c == 0, odd, even).astype(BF16)
                if also is not None:
                    also(cols, full)

            self.copy = send(sib_out.at[index], sib_in.at[index], sibling)

        def start(self):
            index = self.index
            self.copy.wait_recv()
            row_sum[index] = row_sum[index] + sib_in[index].astype(F32)

            def part(k, lo, count):
                return row_sum[index, k, lo : lo + count]

            self.ring = RingReduce(part, rs_out.at[index], rs_in.at[index], on_x, half, own)
            self.ring.start()

    class WeightGrad:
        def __init__(self, index, p, slices, blocks, on_axis, owner_row, out, mid):
            self.index, self.p, self.out, self.mid = index, p, out, mid
            self.slices, self.blocks = slices, blocks
            self.lo, self.units = sz.parts[p]
            self.on_axis, self.owner_row = on_axis, owner_row

        def multiply(self):
            index, p, lo, units = self.index, self.p, self.lo, self.units
            step = sz.group_pad // 2

            @pl.loop(0, 2)
            def _(m):
                rows = pl.ds(pl.multiple_of(m * step, step), step)
                total = None
                for k in range(RING):
                    one = lax.dot_general(
                        self.slices[k, rows, :],
                        self.blocks[k, lo : lo + units, :],
                        ROW_DIMS,
                        preferred_element_type=F32,
                    )
                    total = one if total is None else total + one
                wg_sum[index, p, rows, 0:units] = total

            wg_sum[index, p, sz.group_pad : sz.sum_rows, 0:units] = jnp.zeros((8, units), F32)

            def part(k, first, count):
                place = pl.multiple_of(self.owner_row(k) + first, 8)
                return wg_sum[index, p, pl.ds(place, count), 0:units]

            self.ring = RingReduce(
                part,
                wg_out.at[index, p, :, :, pl.ds(0, units)],
                wg_in.at[index, p, :, :, pl.ds(0, units)],
                self.on_axis,
                self.mid,
                sz.owned_pad,
            )
            self.ring.start()

        def finish(self):
            self.ring.finish()
            self.out[:, self.lo : self.lo + self.units] = self.ring.total()[: sz.owned]

    grad_rows = RowGather(lambda rows: grad_all.at[rows])
    cut_rows = RowGather(lambda rows: norm_sl.at[pl.ds(1, RING - 1), rows])
    (lo0, count0), (lo1, count1) = sz.cuts
    cols0, cols1 = pl.ds(lo0, count0), pl.ds(lo1, count1)
    via = []
    for j in range(1, RING):
        via.append(send(tokens_hbm.at[j, :, cols1], midway.at[j - 1], on_z(j)))
    direct = []
    for j in range(1, sz.homes):
        direct.append(send(tokens_hbm.at[j, :, cols0], arrived.at[j, :, cols0], on_dp(j)))
    last = []
    for j in range(RING, sz.homes):
        last.append(send(tokens_hbm.at[j, :, cols1], arrived.at[j, :, cols1], on_dp(j)))
    load_grad.wait()
    grad_rows.start()
    load_fc2.start()
    load_fc1.start()

    def pick(s, j):
        home = (dp - j + RANKS) % RANKS
        named = slot_ref[home * sz.homes + j]
        return jnp.where(named == dp * sz.slots + s, 1.0, 0.0).astype(F32)

    def group_columns(rows, q):
        cuts = []
        for k in range(RING):
            first = sz.owned * (RING * k + q)
            cuts.append(rows[:, first : first + sz.owned])
        cuts.append(jnp.zeros((rows.shape[0], sz.group_pad - sz.group), rows.dtype))
        return jnp.concatenate(cuts, axis=1)

    for j in range(1, RING):
        via[j - 1].wait_recv()
        last.append(
            send(midway.at[j - 1], arrived.at[j, :, cols1], on_y(1), when=z < j)
        )

        @pl.when(z >= j)
        def _():
            arrived[j, :, lo1:] = midway[j - 1]

    routed = (direct, last)
    load_token.wait()
    grad_rows.forward()
    row_parts = []
    for n, (lo, count) in enumerate(sz.cuts):
        cols = slice(lo, lo + count)
        for made in routed[n]:
            made.wait_recv()
        for s in range(sz.slots):
            total = pick(s, 0) * arrived[0, :, cols].astype(F32)
            for j in range(1, sz.homes):
                total += pick(s, j) * arrived[j, :, cols].astype(F32)
            place = c * own + s * sz.block_rows
            rows = pl.ds(pl.multiple_of(place, sz.block_rows), sz.block_rows)
            row_all[rows, cols] = total.astype(BF16)
        one = RowGather(lambda rows, lo=lo, count=count: row_all.at[rows, pl.ds(lo, count)])
        one.start()
        row_parts.append(one)
    row_parts[0].forward()
    grad_rows.last()

    def normed_rows(rows):
        value = row_all[rows, :].astype(F32)
        inv = lax.rsqrt(jnp.mean(value * value, axis=-1, keepdims=True) + 1e-06)
        return value * inv, inv

    def norm_shard(slot, core):
        @pl.loop(0, own // 16)
        def _(n):
            place = sz.pair * slot + core * own + n * 16
            rows = pl.ds(pl.multiple_of(place, 16), 16)
            unit, _ = normed_rows(rows)
            norm_all[rows, :] = (unit * gain).astype(BF16)

    unit_own, inv = normed_rows(my_rows)
    inv_ref[...] = jnp.broadcast_to(inv, inv_ref.shape)
    norm_own = (unit_own * gain).astype(BF16)
    norm_all[my_rows, :] = norm_own
    for q in range(RING):
        norm_cut[q] = group_columns(norm_own, q)
    cut_sent = []
    for k, slot in ((1, 1), (-1, 2), (2, 3)):
        cut_sent.append(
            send(norm_cut.at[(z + k + RING) % RING], norm_sl.at[slot, my_rows], on_z(k))
        )
    row_parts[1].forward()
    grad_rows.wait(0, 5)
    side = sz.rows // 2
    side_rows = pl.ds(pl.multiple_of(c * side, side), side)
    slice_sent = []
    for k, slot in ((1, 1), (-1, 2), (2, 3)):
        first = pl.multiple_of(((y + k + RING) % RING) * sz.group_step, 128)
        slice_sent.append(
            send(
                grad_all.at[side_rows, pl.ds(first, sz.group_pad)],
                grad_sl.at[slot, side_rows],
                on_y(k),
            )
        )
    row_parts[0].last()

    load_fc2.wait()

    def multiply_in(lhs, lo, count, rows, out):
        @pl.loop(0, width // sz.chunk)
        def _(n):
            cols = pl.ds(pl.multiple_of(n * sz.chunk, sz.chunk), sz.chunk)
            part = lax.dot_general(
                lhs[lo : lo + count, cols], rows[:, cols], ROW_DIMS, preferred_element_type=F32
            )

            @pl.when(n == 0)
            def _():
                out[lo : lo + count, :] = part

            @pl.when(n > 0)
            def _():
                out[lo : lo + count, :] += part

    multiply_in(fc2_ref, *sz.parts[0], grad_all, hid_grad)
    for slot in (1, 2):
        norm_shard(slot, c)
    row_parts[1].last()
    for slot in range(3):
        for one in row_parts:
            one.wait(slot, slot + 1)
        norm_shard(slot, 1 - c)
    norm_shard(3, c)
    for made in cut_sent:
        made.wait_recv()
    for one in row_parts:
        one.wait(3, 5)
    norm_shard(3, 1 - c)
    cut_rows.start()
    load_fc1.wait()

    hid_ring, pre_ring = [], []
    for lo, count in sz.parts:
        if lo > 0:
            multiply_in(fc2_ref, lo, count, grad_all, hid_grad)
        multiply_in(fc1_ref, lo, count, norm_all, pre_act)

        @pl.loop(0, count // 32)
        def _(n):
            rows = pl.ds(pl.multiple_of(lo + n * 32, 32), 32)
            value = pre_act[rows, :]
            cdf = 0.5 * (1.0 + lax.erf(value * 0.7071067811865476))
            slope = cdf + value * jnp.exp(-0.5 * value * value) * 0.3989422804014327
            hid_g[0, rows, :] = (value * cdf).astype(BF16)
            pre_g[0, rows, :] = (hid_grad[rows, :] * slope).astype(BF16)

        hid_ring.append(RingGather(hid_g, lo, count, on_y, count * 2 // 3 // 16 * 16))
        pre_ring.append(RingGather(pre_g, lo, count, on_z, count // 2 // 16 * 16))
        hid_ring[-1].start()
        pre_ring[-1].start()

    back = RowReduce(1)
    branch = RowReduce(0)

    def gain_part(cols, full):
        product = full * norm_all[:, cols].astype(F32)
        gain_sib[0, :, cols] = jnp.sum(product, axis=0, keepdims=True)

    pre_n[...] = pre_g[0].T
    back.multiply(pre_n, fc1_ref, gain_part)
    gain_pair = send(gain_sib.at[0], gain_sib.at[1], sibling)
    hid_ring[0].forward()
    pre_ring[0].forward()
    cut_rows.forward()
    slice_shared = []
    for slot, made in zip((1, 2, 3), slice_sent):
        made.wait_recv()
        place = grad_sl.at[slot, side_rows]
        slice_shared.append(send(place, place, sibling))
    hid_n[...] = hid_g[0].T
    branch.multiply(hid_n, fc2_ref)
    back.start()
    hid_ring[1].forward()
    pre_ring[1].forward()
    cut_rows.last()
    own_first = pl.multiple_of(y * sz.group_step, 128)
    grad_t[0] = grad_all[:, pl.ds(own_first, sz.group_pad)].T
    for made in slice_shared:
        made.wait_recv()
    for k in range(1, RING):
        grad_t[k] = grad_sl[k].T

    def add_start(buf, me, on_axis, total):
        buf[me] = total
        return [send(buf.at[me], buf.at[me], on_axis(k)) for k in (1, -1, 2)]

    def add_finish(buf, made):
        for one in made:
            one.wait_recv()
        return buf[0] + buf[1] + buf[2] + buf[3]

    def fc2_row(k):
        return y * (sz.group - sz.group_step) + ((z + STEP[k] + RING) % RING) * sz.owned

    def fc1_row(k):
        return ((y + STEP[k] + RING) % RING) * sz.owned

    even = round_up(sz.owned_pad // 2, 16)
    more = round_up(sz.owned_pad * 2 // 3, 16)
    fc2_grad = [
        WeightGrad(0, p, grad_t, hid_g, on_z, fc2_row, fc2_out, even) for p in range(2)
    ]
    fc1_grad = [
        WeightGrad(1, p, norm_t, pre_g, on_y, fc1_row, fc1_out, more) for p in range(2)
    ]
    hid_ring[0].finish()
    fc2_grad[0].multiply()
    back.ring.forward()
    branch.start()
    gain_pair.wait_recv()
    adding = add_start(gain_x, x, on_x, gain_sib[0] + gain_sib[1])
    cut_rows.wait(0, 5)
    for q in range(RING):

        @pl.when(z == q)
        def _():
            norm_t[0] = group_columns(norm_all[...], q).T

    for k in range(1, RING):
        norm_t[k] = norm_sl[k].T
    pre_ring[0].finish()
    fc1_grad[0].multiply()
    hid_ring[1].finish()
    fc2_grad[1].multiply()
    pre_ring[1].finish()
    fc1_grad[1].multiply()
    fc2_grad[0].ring.forward()
    fc1_grad[0].ring.forward()
    total = add_finish(gain_x, adding)
    adding = add_start(gain_y, y, on_y, total)
    back.ring.finish()

    normed_grad = back.ring.total()
    unit = row_all[my_rows, :].astype(F32) * inv_ref[:, :1]
    scaled = normed_grad * gain
    inner = scaled - unit * jnp.mean(scaled * unit, axis=-1, keepdims=True)
    input_grad[...] = (
        (grad_all[my_rows, :].astype(F32) + inv_ref[:, :1] * inner).astype(BF16).astype(F32)
    )
    returned, via = [], []
    for j in range(sz.homes):
        total = pick(0, j) * input_grad[0 : sz.block_rows, :]
        for s in range(1, sz.slots):
            total += pick(s, j) * input_grad[s * sz.block_rows : (s + 1) * sz.block_rows, :]
        total = total.astype(BF16)
        if j == 0:
            tgrad[0] = total
            continue
        back_out[j - 1] = total
        source, place = back_out.at[j - 1], tgrad.at[j]
        if j < RING:
            via.append(send(source.at[:, cols1], midway_back.at[j - 1], on_z(-j)))
            returned.append(send(source.at[:, cols0], place.at[:, cols0], on_dp(-j)))
        else:
            returned.append(send(source, place, on_dp(-j)))
    branch.ring.forward()
    fc2_grad[1].ring.forward()
    fc1_grad[1].ring.forward()
    total = add_finish(gain_y, adding)
    adding = add_start(gain_z, z, on_z, total)
    for j in range(1, RING):
        via[j - 1].wait_recv()
        returned.append(
            send(midway_back.at[j - 1], tgrad.at[j, :, cols1], on_y(-1), when=z + j >= RING)
        )

        @pl.when(z + j < RING)
        def _():
            tgrad[j, :, lo1:] = midway_back[j - 1]

    branch.ring.finish()
    mixed[...] = (row_all[my_rows, :].astype(F32) + branch.ring.total()).astype(BF16)
    fc2_grad[0].finish()
    fc1_grad[0].finish()
    total = add_finish(gain_z, adding)
    gain_out[...] = (total / gain).reshape(width)
    for made in returned:
        made.wait_recv()
    fc2_grad[-1].finish()
    fc1_grad[-1].finish()
    for made in started:
        made.wait_send()
    if len(started) != copies:
        raise ValueError(len(started))


def hand_over_kernel(*refs):
    count = len(refs) // 2
    sems = refs[-1]
    made = [
        pltpu.make_async_copy(refs[i], refs[count + i], sems.at[i]) for i in range(count)
    ]
    for one in made:
        one.start()
    for one in made:
        one.wait()


def hand_over(*arrays):
    vmem = pl.BlockSpec(memory_space=pltpu.VMEM)
    anywhere = pl.BlockSpec(memory_space=pl.ANY)
    return pl.pallas_call(
        hand_over_kernel,
        out_shape=tuple(jax.ShapeDtypeStruct(a.shape, a.dtype) for a in arrays),
        in_specs=[vmem] * len(arrays),
        out_specs=(anywhere,) * len(arrays),
        scratch_shapes=[pltpu.SemaphoreType.DMA((len(arrays),))],
        compiler_params=pltpu.CompilerParams(vmem_limit_bytes=1024 * 1024),
        name="hand_over",
    )(*arrays)


COPIES = 130


def local(tokens, norm_gain, fc1, fc2t, block_slot, out_grad):
    sz = Sizes(tokens.shape, fc1.shape, out_grad.shape)
    width, units = sz.width, sz.units
    vmem = pl.BlockSpec(memory_space=pltpu.VMEM)
    anywhere = pl.BlockSpec(memory_space=pl.ANY)
    slices = (RING, sz.rows, sz.group_pad)
    slices_t = (RING, sz.group_pad, sz.rows)
    pieces = (2, 2, 3, sz.owned_pad, sz.part_max)
    arrays = pl.pallas_call(
        functools.partial(kernel, sz, COPIES),
        out_shape=(
            pltpu.VMEM((sz.own, width), BF16),
            pltpu.VMEM(tokens.shape, BF16),
            pltpu.VMEM((sz.owned, units), F32),
            pltpu.VMEM((sz.owned, units), F32),
            pltpu.VMEM((width,), F32),
        ),
        in_specs=[
            pl.BlockSpec(memory_space=pltpu.SMEM),
            vmem,
            anywhere,
            anywhere,
            anywhere,
            anywhere,
        ],
        out_specs=(vmem,) * 5,
        scratch_shapes=[
            pltpu.VMEM((units, width), BF16),
            pltpu.VMEM((units, width), BF16),
            pltpu.VMEM(tokens.shape, BF16),
            pltpu.VMEM((RING - 1, sz.block_rows, sz.cuts[1][1]), BF16),
            pltpu.VMEM((RING - 1, sz.block_rows, sz.cuts[1][1]), BF16),
            pltpu.VMEM((sz.rows, width), BF16),
            pltpu.VMEM((sz.own, 128), F32),
            pltpu.VMEM((sz.rows, width), BF16),
            pltpu.VMEM((sz.rows, width), BF16),
            pltpu.VMEM((RING, sz.own, sz.group_pad), BF16),
            pltpu.VMEM(slices, BF16),
            pltpu.VMEM(slices, BF16),
            pltpu.VMEM(slices_t, BF16),
            pltpu.VMEM(slices_t, BF16),
            pltpu.VMEM((RING, units, sz.rows), BF16),
            pltpu.VMEM((RING, units, sz.rows), BF16),
            pltpu.VMEM((sz.rows, units), BF16),
            pltpu.VMEM((sz.rows, units), BF16),
            pltpu.VMEM((units, sz.rows), F32),
            pltpu.VMEM((units, sz.rows), F32),
            pltpu.VMEM((2, RING, sz.own, width), F32),
            pltpu.VMEM((2, RING, sz.own, width), BF16),
            pltpu.VMEM((2, RING, sz.own, width), BF16),
            pltpu.VMEM((2, 3, sz.own, width), BF16),
            pltpu.VMEM((2, 3, sz.own, width), BF16),
            pltpu.VMEM((2, 2, sz.sum_rows, sz.part_max), F32),
            pltpu.VMEM(pieces, BF16),
            pltpu.VMEM(pieces, BF16),
            pltpu.VMEM((sz.homes - 1, sz.block_rows, width), BF16),
            pltpu.VMEM((sz.own, width), F32),
            pltpu.VMEM((2, 1, width), F32),
            pltpu.VMEM((RING, 1, width), F32),
            pltpu.VMEM((RING, 1, width), F32),
            pltpu.VMEM((RING, 1, width), F32),
            pltpu.SemaphoreType.DMA((4,)),
            pltpu.SemaphoreType.DMA((COPIES,)),
            pltpu.SemaphoreType.DMA((COPIES,)),
        ],
        compiler_params=pltpu.CompilerParams(
            collective_id=0, has_side_effects=True, vmem_limit_bytes=60 * 1024 * 1024
        ),
        cost_estimate=pl.CostEstimate(
            flops=12 * sz.rows * width * units,
            bytes_accessed=4 * width * units,
            transcendentals=2 * sz.rows * units,
        ),
        name="mlp_block",
    )(
        block_slot,
        norm_gain,
        tokens,
        fc1.T,
        fc2t.T,
        out_grad.reshape(sz.own, width),
    )
    mixed, tgrad, fc1_grad, fc2_grad, gain_grad = hand_over(*arrays)
    return mixed.reshape(out_grad.shape), tgrad, fc1_grad, fc2_grad, gain_grad


def solution(mesh):
    placed = (
        P("dp", "tensor", None),
        P(),
        P(None, "tensor"),
        P(None, "tensor"),
        P(),
        P("dp", "tensor", None),
    )
    return jax.shard_map(
        local,
        mesh=mesh,
        in_specs=placed,
        out_specs=(
            P("dp", "tensor", None),
            P("dp", "tensor", None),
            P("dp", "tensor"),
            P("dp", "tensor"),
            P(),
        ),
        check_vma=False,
    )
```

```python
import functools

import jax
import jax.numpy as jnp
from jax import lax
from jax.experimental import pallas as pl
from jax.experimental.pallas import tpu as pltpu
from jax.sharding import PartitionSpec as P

MESH = pl.DeviceIdType.MESH
ROW_DIMS = (((1,), (1,)), ((), ()))
RING = 4
RANKS = RING * RING
F32 = jnp.float32
BF16 = jnp.bfloat16

STEP = (0, -1, 1, 2)


def round_up(value, unit):
    return (value + unit - 1) // unit * unit


def chunk_of(width, limit):
    tiles = width // 128
    best = 1
    for count in range(1, tiles + 1):
        if tiles % count == 0 and count * 128 <= limit:
            best = count
    return best * 128


FOLD = 4


def fold_rows(rows):
    return round_up((rows + FOLD - 1) // FOLD, 16)


def fold_lanes(value):
    rows, units = value.shape
    step = fold_rows(rows)
    total = -(-rows // step)
    if total * step > rows:
        value = jnp.concatenate(
            [value, jnp.zeros((total * step - rows, units), value.dtype)], axis=0
        )
    cuts = [value[step * k : step * (k + 1)] for k in range(total)]
    if total * units < 128:
        cuts.append(jnp.zeros((step, 128 - total * units), value.dtype))
    return jnp.concatenate(cuts, axis=1)


def unfold_lanes(value, rows, units):
    step = value.shape[0]
    total = -(-rows // step)
    cuts = [value[:, units * k : units * (k + 1)] for k in range(total)]
    return jnp.concatenate(cuts, axis=0)[:rows]


class Sizes:
    def __init__(self, tokens, fc1, out_grad):
        self.homes, self.block_rows, self.width = tokens
        self.units = fc1[1]
        self.slots = out_grad[0]
        self.own = self.slots * self.block_rows
        self.pair = 2 * self.own
        self.rows = RING * self.pair
        self.owned = self.width // RANKS
        self.owned_pad = round_up(self.owned, 16)
        self.group = RING * self.owned
        self.group_step = self.group // 128 * 128
        self.group_pad = round_up(self.group + (RING - 1) * (self.group - self.group_step), 128)
        self.sum_rows = self.group_pad + 8
        self.chunk = chunk_of(self.width, 640)
        first = round_up(self.units // 2, 128) - 128
        self.parts = ((0, first), (first, self.units - first))
        mid = round_up(self.width // 2, 128)
        self.cuts = ((0, mid), (mid, self.width - mid))
        self.part_max = max(count for _, count in self.parts)


def kernel(
    sz,
    copies,
    slot_ref,
    gain_ref,
    tokens_hbm,
    fc1_hbm,
    fc2_hbm,
    grad_hbm,
    mixed,
    tgrad,
    fc1_out,
    fc2_out,
    gain_out,
    fc1_ref,
    fc2_ref,
    arrived,
    midway,
    midway_back,
    row_all,
    inv_ref,
    grad_all,
    norm_all,
    norm_cut,
    grad_sl,
    norm_sl,
    grad_t,
    norm_t,
    hid_g,
    pre_g,
    hid_n,
    pre_n,
    pre_act,
    hid_grad,
    row_sum,
    sib_out,
    sib_in,
    rs_out,
    rs_in,
    wg_sum,
    wg_out,
    wg_in,
    fold_out,
    fold_in,
    back_out,
    input_grad,
    gain_sib,
    gain_x,
    gain_y,
    gain_z,
    local_sems,
    send_sems,
    recv_sems,
):
    dp = lax.axis_index("dp")
    t = lax.axis_index("tensor")
    y, z = dp // RING, dp % RING
    x, c = t // 2, t % 2
    own, width = sz.own, sz.width
    half = own // 2
    gain = gain_ref[...].reshape(1, width)

    def on_dp(k):
        return ((dp + k + RANKS) % RANKS, t)

    def on_x(k):
        return (dp, ((x + k + RING) % RING) * 2 + c)

    def on_y(k):
        return (((y + k + RING) % RING) * RING + z, t)

    def on_z(k):
        return (y * RING + (z + k + RING) % RING, t)

    sibling = (dp, t + 1 - 2 * c)

    started = []

    class Guarded:
        def __init__(self, made, when, arrives):
            self.made, self.when, self.arrives = made, when, arrives

        def wait_recv(self):
            pl.when(self.arrives)(self.made.wait_recv)

        def wait_send(self):
            pl.when(self.when)(self.made.wait_send)

    def send(src, dst, device, when=None, arrives=None):
        index = len(started)
        made = pltpu.make_async_remote_copy(
            src_ref=src,
            dst_ref=dst,
            send_sem=send_sems.at[index],
            recv_sem=recv_sems.at[index],
            device_id=device,
            device_id_type=MESH,
        )
        if when is None:
            made.start()
        else:
            pl.when(when)(made.start)
            made = Guarded(made, when, when if arrives is None else arrives)
        started.append(made)
        return made

    my_rows = pl.ds(pl.multiple_of(c * own, own), own)
    load_grad = pltpu.make_async_copy(grad_hbm, grad_all.at[my_rows], local_sems.at[0])
    load_token = pltpu.make_async_copy(tokens_hbm.at[0], arrived.at[0], local_sems.at[1])
    load_fc2 = pltpu.make_async_copy(fc2_hbm, fc2_ref, local_sems.at[2])
    load_fc1 = pltpu.make_async_copy(fc1_hbm, fc1_ref, local_sems.at[3])
    load_grad.start()
    load_token.start()

    partners = [on_dp(k) for k in range(1, sz.homes)]
    partners += [on_dp(-k) for k in range(1, sz.homes)]
    partners += [on_y(k) for k in (1, -1, 2)]
    partners += [on_z(k) for k in (1, -1, 2)]
    partners += [on_x(k) for k in (1, -1, 2)]
    partners += [sibling]
    barrier = pltpu.get_barrier_semaphore()
    for device in partners:
        pl.semaphore_signal(barrier, inc=1, device_id=device, device_id_type=MESH)
    pl.semaphore_wait(barrier, len(partners))

    class RowGather:
        def __init__(self, view):
            self.view = view

        def part(self, slot, lo, count):
            place = sz.pair * slot + c * own + lo
            return self.view(pl.ds(pl.multiple_of(place, 16), count))

        def start(self):
            mine = self.part(0, 0, own)
            self.right = send(mine, self.part(1, 0, own), on_x(1))
            self.left = send(mine, self.part(2, 0, own), on_x(-1))
            self.shared = [send(mine, mine, sibling)]

        def forward(self):
            self.right.wait_recv()
            self.right2 = send(self.part(1, 0, half), self.part(3, 0, half), on_x(1))
            whole = self.part(1, 0, own)
            self.shared.append(send(whole, whole, sibling))
            self.left.wait_recv()
            rest = own - half
            self.left2 = send(self.part(2, half, rest), self.part(3, half, rest), on_x(-1))
            whole = self.part(2, 0, own)
            self.shared.append(send(whole, whole, sibling))

        def last(self):
            self.right2.wait_recv()
            low = self.part(3, 0, half)
            self.shared.append(send(low, low, sibling))
            self.left2.wait_recv()
            high = self.part(3, half, own - half)
            self.shared.append(send(high, high, sibling))

        def wait(self, first, stop):
            for made in self.shared[first:stop]:
                made.wait_recv()

    class RingGather:
        def __init__(self, buf, lo, count, on_axis, low):
            self.buf, self.on_axis = buf, on_axis
            self.whole = pl.ds(lo, count)
            self.low = pl.ds(lo, low)
            self.high = pl.ds(lo + low, count - low)

        def start(self):
            buf, on_axis = self.buf, self.on_axis
            mine = buf.at[0, self.whole]
            self.right = send(mine, buf.at[1, self.whole], on_axis(1))
            self.left = send(mine, buf.at[2, self.whole], on_axis(-1))

        def forward(self):
            buf, on_axis = self.buf, self.on_axis
            self.right.wait_recv()
            self.right2 = send(buf.at[1, self.low], buf.at[3, self.low], on_axis(1))
            self.left.wait_recv()
            self.left2 = send(buf.at[2, self.high], buf.at[3, self.high], on_axis(-1))

        def finish(self):
            self.right2.wait_recv()
            self.left2.wait_recv()

    class RingReduce:
        def __init__(self, part, out, into, on_axis, mid, count, folds=None):
            self.part, self.out, self.into = part, out, into
            self.on_axis, self.folds = on_axis, folds
            self.ranges = ((0, mid), (mid, count - mid))

        def put(self, slot, h, value):
            first, count = self.ranges[h]
            if self.folds is not None:
                main, fold_out, _ = self.folds
                folded = fold_lanes(value[:, main:])
                fold_out[slot, h, 0 : folded.shape[0]] = folded.astype(BF16)
                value = value[:, :main]
            self.out[slot, pl.ds(first, count)] = value.astype(BF16)

        def ship(self, slot, h, device):
            first, count = self.ranges[h]
            rows = pl.ds(first, count)
            made = [send(self.out.at[slot, rows], self.into.at[slot, rows], device)]
            if self.folds is not None:
                main, fold_out, fold_in = self.folds
                rows = pl.ds(0, fold_rows(count))
                made.append(send(fold_out.at[slot, h, rows], fold_in.at[slot, h, rows], device))
            return made

        def get(self, slot, h):
            first, count = self.ranges[h]
            value = self.into[slot, pl.ds(first, count)].astype(F32)
            if self.folds is not None:
                main, _, fold_in = self.folds
                folded = fold_in[slot, h, 0 : fold_rows(count)].astype(F32)
                units = self.units - main
                value = jnp.concatenate([value, unfold_lanes(folded, count, units)], axis=1)
            return value

        def own_part(self, k, h):
            value = self.part(k, *self.ranges[h])
            self.units = value.shape[1]
            return value

        def start(self):
            self.put(0, 0, self.own_part(3, 0))
            self.far_right = self.ship(0, 0, self.on_axis(1))
            self.put(0, 1, self.own_part(3, 1))
            self.far_left = self.ship(0, 1, self.on_axis(-1))
            self.put(1, 1, self.own_part(2, 1))
            self.rest = self.ship(1, 1, self.on_axis(1))
            self.put(2, 0, self.own_part(1, 0))
            self.rest += self.ship(2, 0, self.on_axis(-1))

        def forward(self):
            for made in self.far_right:
                made.wait_recv()
            self.put(1, 0, self.own_part(2, 0) + self.get(0, 0))
            self.rest += self.ship(1, 0, self.on_axis(1))
            for made in self.far_left:
                made.wait_recv()
            self.put(2, 1, self.own_part(1, 1) + self.get(0, 1))
            self.rest += self.ship(2, 1, self.on_axis(-1))

        def finish(self):
            for made in self.rest:
                made.wait_recv()

        def total(self, h):
            return self.own_part(0, h) + self.get(1, h) + self.get(2, h)

    class RowReduce:
        def __init__(self, index):
            self.index = index

        def multiply(self, lhs, weight, also=None):
            index = self.index

            @pl.loop(0, width // sz.chunk)
            def _(n):
                cols = pl.ds(pl.multiple_of(n * sz.chunk, sz.chunk), sz.chunk)
                full = jnp.dot(lhs[...], weight[:, cols], preferred_element_type=F32)
                for k in range(RING):
                    even = full[sz.pair * k : sz.pair * k + own]
                    odd = full[sz.pair * k + own : sz.pair * (k + 1)]
                    row_sum[index, k, :, cols] = jnp.where(c == 0, even, odd)
                    sib_out[index, k, :, cols] = jnp.where(c == 0, odd, even).astype(BF16)
                if also is not None:
                    also(cols, full)

            self.copy = send(sib_out.at[index], sib_in.at[index], sibling)

        def start(self):
            index = self.index
            self.copy.wait_recv()
            row_sum[index] = row_sum[index] + sib_in[index].astype(F32)

            def part(k, lo, count):
                return row_sum[index, k, lo : lo + count]

            self.ring = RingReduce(part, rs_out.at[index], rs_in.at[index], on_x, half, own)
            self.ring.start()

    class WeightGrad:
        def __init__(self, index, p, slices, blocks, on_axis, owner_row, out, mid):
            self.index, self.p, self.out, self.mid = index, p, out, mid
            self.slices, self.blocks = slices, blocks
            self.lo, self.units = sz.parts[p]
            self.on_axis, self.owner_row = on_axis, owner_row

        def multiply(self):
            index, p, lo, units = self.index, self.p, self.lo, self.units
            step = sz.group_pad // 2

            @pl.loop(0, 2)
            def _(m):
                rows = pl.ds(pl.multiple_of(m * step, step), step)
                total = None
                for k in range(RING):
                    one = lax.dot_general(
                        self.slices[k, rows, :],
                        self.blocks[k, lo : lo + units, :],
                        ROW_DIMS,
                        preferred_element_type=F32,
                    )
                    total = one if total is None else total + one
                wg_sum[index, p, rows, 0:units] = total

            wg_sum[index, p, sz.group_pad : sz.sum_rows, 0:units] = jnp.zeros((8, units), F32)

            def part(k, first, count):
                place = pl.multiple_of(self.owner_row(k) + first, 8)
                return wg_sum[index, p, pl.ds(place, count), 0:units]

            main = units // 128 * 128
            folds = None
            if main < units:
                folds = (main, fold_out.at[index], fold_in.at[index])
            self.ring = RingReduce(
                part,
                wg_out.at[index, p, :, :, pl.ds(0, main)],
                wg_in.at[index, p, :, :, pl.ds(0, main)],
                self.on_axis,
                self.mid,
                sz.owned_pad,
                folds,
            )
            self.ring.start()

        def finish(self):
            self.ring.finish()
            for h, (first, count) in enumerate(self.ring.ranges):
                count = min(count, sz.owned - first)
                cols = slice(self.lo, self.lo + self.units)
                self.out[first : first + count, cols] = self.ring.total(h)[:count]

    grad_rows = RowGather(lambda rows: grad_all.at[rows])
    cut_rows = RowGather(lambda rows: norm_sl.at[pl.ds(1, RING - 1), rows])
    (lo0, count0), (lo1, count1) = sz.cuts
    cols0, cols1 = pl.ds(lo0, count0), pl.ds(lo1, count1)
    via = []
    for j in range(1, RING):
        via.append(send(tokens_hbm.at[j, :, cols1], midway.at[j - 1], on_z(j)))
    direct = []
    for j in range(1, sz.homes):
        direct.append(send(tokens_hbm.at[j, :, cols0], arrived.at[j, :, cols0], on_dp(j)))
    last = []
    for j in range(RING, sz.homes):
        last.append(send(tokens_hbm.at[j, :, cols1], arrived.at[j, :, cols1], on_dp(j)))
    load_grad.wait()
    grad_rows.start()
    load_fc2.start()
    load_fc1.start()

    def pick(s, j):
        home = (dp - j + RANKS) % RANKS
        named = slot_ref[home * sz.homes + j]
        return jnp.where(named == dp * sz.slots + s, 1.0, 0.0).astype(F32)

    def group_columns(rows, q):
        cuts = []
        for k in range(RING):
            first = sz.owned * (RING * k + q)
            cuts.append(rows[:, first : first + sz.owned])
        cuts.append(jnp.zeros((rows.shape[0], sz.group_pad - sz.group), rows.dtype))
        return jnp.concatenate(cuts, axis=1)

    for j in range(1, RING):
        via[j - 1].wait_recv()
        last.append(
            send(midway.at[j - 1], arrived.at[j, :, cols1], on_y(1), when=z < j)
        )

        @pl.when(z >= j)
        def _():
            arrived[j, :, lo1:] = midway[j - 1]

    routed = (direct, last)
    load_token.wait()
    grad_rows.forward()
    row_parts = []
    for n, (lo, count) in enumerate(sz.cuts):
        cols = slice(lo, lo + count)
        for made in routed[n]:
            made.wait_recv()
        for s in range(sz.slots):
            total = pick(s, 0) * arrived[0, :, cols].astype(F32)
            for j in range(1, sz.homes):
                total += pick(s, j) * arrived[j, :, cols].astype(F32)
            place = c * own + s * sz.block_rows
            rows = pl.ds(pl.multiple_of(place, sz.block_rows), sz.block_rows)
            row_all[rows, cols] = total.astype(BF16)
        one = RowGather(lambda rows, lo=lo, count=count: row_all.at[rows, pl.ds(lo, count)])
        one.start()
        row_parts.append(one)
    row_parts[0].forward()
    grad_rows.last()

    def normed_rows(rows):
        value = row_all[rows, :].astype(F32)
        inv = lax.rsqrt(jnp.mean(value * value, axis=-1, keepdims=True) + 1e-06)
        return value * inv, inv

    def norm_shard(slot, core):
        @pl.loop(0, own // 16)
        def _(n):
            place = sz.pair * slot + core * own + n * 16
            rows = pl.ds(pl.multiple_of(place, 16), 16)
            unit, _ = normed_rows(rows)
            norm_all[rows, :] = (unit * gain).astype(BF16)

    unit_own, inv = normed_rows(my_rows)
    inv_ref[...] = jnp.broadcast_to(inv, inv_ref.shape)
    norm_own = (unit_own * gain).astype(BF16)
    norm_all[my_rows, :] = norm_own
    for q in range(RING):
        norm_cut[q] = group_columns(norm_own, q)
    cut_sent = []
    for k, slot in ((1, 1), (-1, 2), (2, 3)):
        cut_sent.append(
            send(norm_cut.at[(z + k + RING) % RING], norm_sl.at[slot, my_rows], on_z(k))
        )
    row_parts[1].forward()
    grad_rows.wait(0, 5)
    side = sz.rows // 2
    side_rows = pl.ds(pl.multiple_of(c * side, side), side)
    slice_sent = []
    for k, slot in ((1, 1), (-1, 2), (2, 3)):
        first = pl.multiple_of(((y + k + RING) % RING) * sz.group_step, 128)
        slice_sent.append(
            send(
                grad_all.at[side_rows, pl.ds(first, sz.group_pad)],
                grad_sl.at[slot, side_rows],
                on_y(k),
            )
        )
    row_parts[0].last()

    load_fc2.wait()

    def multiply_in(lhs, lo, count, rows, out):
        @pl.loop(0, width // sz.chunk)
        def _(n):
            cols = pl.ds(pl.multiple_of(n * sz.chunk, sz.chunk), sz.chunk)
            part = lax.dot_general(
                lhs[lo : lo + count, cols], rows[:, cols], ROW_DIMS, preferred_element_type=F32
            )

            @pl.when(n == 0)
            def _():
                out[lo : lo + count, :] = part

            @pl.when(n > 0)
            def _():
                out[lo : lo + count, :] += part

    multiply_in(fc2_ref, *sz.parts[0], grad_all, hid_grad)
    for slot in (1, 2):
        norm_shard(slot, c)
    row_parts[1].last()
    for slot in range(3):
        for one in row_parts:
            one.wait(slot, slot + 1)
        norm_shard(slot, 1 - c)
    norm_shard(3, c)
    for made in cut_sent:
        made.wait_recv()
    for one in row_parts:
        one.wait(3, 5)
    norm_shard(3, 1 - c)
    cut_rows.start()
    load_fc1.wait()

    hid_ring, pre_ring = [], []
    for lo, count in sz.parts:
        if lo > 0:
            multiply_in(fc2_ref, lo, count, grad_all, hid_grad)
        multiply_in(fc1_ref, lo, count, norm_all, pre_act)

        @pl.loop(0, count // 32)
        def _(n):
            rows = pl.ds(pl.multiple_of(lo + n * 32, 32), 32)
            value = pre_act[rows, :]
            cdf = 0.5 * (1.0 + lax.erf(value * 0.7071067811865476))
            slope = cdf + value * jnp.exp(-0.5 * value * value) * 0.3989422804014327
            hid_g[0, rows, :] = (value * cdf).astype(BF16)
            pre_g[0, rows, :] = (hid_grad[rows, :] * slope).astype(BF16)

        hid_ring.append(RingGather(hid_g, lo, count, on_y, count * 2 // 3 // 16 * 16))
        pre_ring.append(RingGather(pre_g, lo, count, on_z, count // 2 // 16 * 16))
        hid_ring[-1].start()
        pre_ring[-1].start()

    back = RowReduce(1)
    branch = RowReduce(0)

    def gain_part(cols, full):
        product = full * norm_all[:, cols].astype(F32)
        gain_sib[0, :, cols] = jnp.sum(product, axis=0, keepdims=True)

    pre_n[...] = pre_g[0].T
    back.multiply(pre_n, fc1_ref, gain_part)
    gain_pair = send(gain_sib.at[0], gain_sib.at[1], sibling)
    hid_ring[0].forward()
    pre_ring[0].forward()
    cut_rows.forward()
    slice_shared = []
    for slot, made in zip((1, 2, 3), slice_sent):
        made.wait_recv()
        place = grad_sl.at[slot, side_rows]
        slice_shared.append(send(place, place, sibling))
    hid_n[...] = hid_g[0].T
    branch.multiply(hid_n, fc2_ref)
    back.start()
    hid_ring[1].forward()
    pre_ring[1].forward()
    cut_rows.last()
    own_first = pl.multiple_of(y * sz.group_step, 128)
    grad_t[0] = grad_all[:, pl.ds(own_first, sz.group_pad)].T
    for made in slice_shared:
        made.wait_recv()
    for k in range(1, RING):
        grad_t[k] = grad_sl[k].T

    def add_start(buf, me, on_axis, total):
        buf[me] = total
        return [send(buf.at[me], buf.at[me], on_axis(k)) for k in (1, -1, 2)]

    def add_finish(buf, made):
        for one in made:
            one.wait_recv()
        return buf[0] + buf[1] + buf[2] + buf[3]

    def fc2_row(k):
        return y * (sz.group - sz.group_step) + ((z + STEP[k] + RING) % RING) * sz.owned

    def fc1_row(k):
        return ((y + STEP[k] + RING) % RING) * sz.owned

    even = round_up(sz.owned_pad // 2, 16)
    more = round_up(sz.owned_pad * 2 // 3, 16)
    fc2_grad = [
        WeightGrad(0, p, grad_t, hid_g, on_z, fc2_row, fc2_out, even) for p in range(2)
    ]
    fc1_grad = [
        WeightGrad(1, p, norm_t, pre_g, on_y, fc1_row, fc1_out, more) for p in range(2)
    ]
    hid_ring[0].finish()
    fc2_grad[0].multiply()
    back.ring.forward()
    branch.start()
    gain_pair.wait_recv()
    adding = add_start(gain_x, x, on_x, gain_sib[0] + gain_sib[1])
    cut_rows.wait(0, 5)
    for q in range(RING):

        @pl.when(z == q)
        def _():
            norm_t[0] = group_columns(norm_all[...], q).T

    for k in range(1, RING):
        norm_t[k] = norm_sl[k].T
    pre_ring[0].finish()
    fc1_grad[0].multiply()
    hid_ring[1].finish()
    fc2_grad[1].multiply()
    pre_ring[1].finish()
    fc1_grad[1].multiply()
    fc2_grad[0].ring.forward()
    fc1_grad[0].ring.forward()
    total = add_finish(gain_x, adding)
    adding = add_start(gain_y, y, on_y, total)
    back.ring.finish()

    normed_grad = jnp.concatenate([back.ring.total(0), back.ring.total(1)], axis=0)
    unit = row_all[my_rows, :].astype(F32) * inv_ref[:, :1]
    scaled = normed_grad * gain
    inner = scaled - unit * jnp.mean(scaled * unit, axis=-1, keepdims=True)
    input_grad[...] = (
        (grad_all[my_rows, :].astype(F32) + inv_ref[:, :1] * inner).astype(BF16).astype(F32)
    )
    returned, via = [], []
    for j in range(sz.homes):
        total = pick(0, j) * input_grad[0 : sz.block_rows, :]
        for s in range(1, sz.slots):
            total += pick(s, j) * input_grad[s * sz.block_rows : (s + 1) * sz.block_rows, :]
        total = total.astype(BF16)
        if j == 0:
            tgrad[0] = total
            continue
        back_out[j - 1] = total
        source, place = back_out.at[j - 1], tgrad.at[j]
        if j < RING:
            via.append(send(source.at[:, cols1], midway_back.at[j - 1], on_z(-j)))
            returned.append(send(source.at[:, cols0], place.at[:, cols0], on_dp(-j)))
        else:
            returned.append(send(source, place, on_dp(-j)))
    branch.ring.forward()
    fc2_grad[1].ring.forward()
    fc1_grad[1].ring.forward()
    total = add_finish(gain_y, adding)
    adding = add_start(gain_z, z, on_z, total)
    for j in range(1, RING):
        via[j - 1].wait_recv()
        returned.append(
            send(midway_back.at[j - 1], tgrad.at[j, :, cols1], on_y(-1), when=z + j >= RING)
        )

        @pl.when(z + j < RING)
        def _():
            tgrad[j, :, lo1:] = midway_back[j - 1]

    branch.ring.finish()
    branch_sum = jnp.concatenate([branch.ring.total(0), branch.ring.total(1)], axis=0)
    mixed[...] = (row_all[my_rows, :].astype(F32) + branch_sum).astype(BF16)
    fc2_grad[0].finish()
    fc1_grad[0].finish()
    total = add_finish(gain_z, adding)
    gain_out[...] = (total / gain).reshape(width)
    for made in returned:
        made.wait_recv()
    fc2_grad[-1].finish()
    fc1_grad[-1].finish()
    for made in started:
        made.wait_send()
    if len(started) != copies:
        raise ValueError(len(started))


def hand_over_kernel(*refs):
    count = len(refs) // 2
    sems = refs[-1]
    made = [
        pltpu.make_async_copy(refs[i], refs[count + i], sems.at[i]) for i in range(count)
    ]
    for one in made:
        one.start()
    for one in made:
        one.wait()


def hand_over(*arrays):
    vmem = pl.BlockSpec(memory_space=pltpu.VMEM)
    anywhere = pl.BlockSpec(memory_space=pl.ANY)
    return pl.pallas_call(
        hand_over_kernel,
        out_shape=tuple(jax.ShapeDtypeStruct(a.shape, a.dtype) for a in arrays),
        in_specs=[vmem] * len(arrays),
        out_specs=(anywhere,) * len(arrays),
        scratch_shapes=[pltpu.SemaphoreType.DMA((len(arrays),))],
        compiler_params=pltpu.CompilerParams(vmem_limit_bytes=1024 * 1024),
        name="hand_over",
    )(*arrays)


COPIES = 142


def local(tokens, norm_gain, fc1, fc2t, block_slot, out_grad):
    sz = Sizes(tokens.shape, fc1.shape, out_grad.shape)
    width, units = sz.width, sz.units
    vmem = pl.BlockSpec(memory_space=pltpu.VMEM)
    anywhere = pl.BlockSpec(memory_space=pl.ANY)
    slices = (RING, sz.rows, sz.group_pad)
    slices_t = (RING, sz.group_pad, sz.rows)
    pieces = (2, 2, 3, sz.owned_pad, sz.part_max // 128 * 128)
    folds = (2, 3, 2, fold_rows(sz.owned_pad), 128)
    arrays = pl.pallas_call(
        functools.partial(kernel, sz, COPIES),
        out_shape=(
            pltpu.VMEM((sz.own, width), BF16),
            pltpu.VMEM(tokens.shape, BF16),
            pltpu.VMEM((sz.owned, units), F32),
            pltpu.VMEM((sz.owned, units), F32),
            pltpu.VMEM((width,), F32),
        ),
        in_specs=[
            pl.BlockSpec(memory_space=pltpu.SMEM),
            vmem,
            anywhere,
            anywhere,
            anywhere,
            anywhere,
        ],
        out_specs=(vmem,) * 5,
        scratch_shapes=[
            pltpu.VMEM((units, width), BF16),
            pltpu.VMEM((units, width), BF16),
            pltpu.VMEM(tokens.shape, BF16),
            pltpu.VMEM((RING - 1, sz.block_rows, sz.cuts[1][1]), BF16),
            pltpu.VMEM((RING - 1, sz.block_rows, sz.cuts[1][1]), BF16),
            pltpu.VMEM((sz.rows, width), BF16),
            pltpu.VMEM((sz.own, 128), F32),
            pltpu.VMEM((sz.rows, width), BF16),
            pltpu.VMEM((sz.rows, width), BF16),
            pltpu.VMEM((RING, sz.own, sz.group_pad), BF16),
            pltpu.VMEM(slices, BF16),
            pltpu.VMEM(slices, BF16),
            pltpu.VMEM(slices_t, BF16),
            pltpu.VMEM(slices_t, BF16),
            pltpu.VMEM((RING, units, sz.rows), BF16),
            pltpu.VMEM((RING, units, sz.rows), BF16),
            pltpu.VMEM((sz.rows, units), BF16),
            pltpu.VMEM((sz.rows, units), BF16),
            pltpu.VMEM((units, sz.rows), F32),
            pltpu.VMEM((units, sz.rows), F32),
            pltpu.VMEM((2, RING, sz.own, width), F32),
            pltpu.VMEM((2, RING, sz.own, width), BF16),
            pltpu.VMEM((2, RING, sz.own, width), BF16),
            pltpu.VMEM((2, 3, sz.own, width), BF16),
            pltpu.VMEM((2, 3, sz.own, width), BF16),
            pltpu.VMEM((2, 2, sz.sum_rows, sz.part_max), F32),
            pltpu.VMEM(pieces, BF16),
            pltpu.VMEM(pieces, BF16),
            pltpu.VMEM(folds, BF16),
            pltpu.VMEM(folds, BF16),
            pltpu.VMEM((sz.homes - 1, sz.block_rows, width), BF16),
            pltpu.VMEM((sz.own, width), F32),
            pltpu.VMEM((2, 1, width), F32),
            pltpu.VMEM((RING, 1, width), F32),
            pltpu.VMEM((RING, 1, width), F32),
            pltpu.VMEM((RING, 1, width), F32),
            pltpu.SemaphoreType.DMA((4,)),
            pltpu.SemaphoreType.DMA((COPIES,)),
            pltpu.SemaphoreType.DMA((COPIES,)),
        ],
        compiler_params=pltpu.CompilerParams(
            collective_id=0, has_side_effects=True, vmem_limit_bytes=60 * 1024 * 1024
        ),
        cost_estimate=pl.CostEstimate(
            flops=12 * sz.rows * width * units,
            bytes_accessed=4 * width * units,
            transcendentals=2 * sz.rows * units,
        ),
        name="mlp_block",
    )(
        block_slot,
        norm_gain,
        tokens,
        fc1.T,
        fc2t.T,
        out_grad.reshape(sz.own, width),
    )
    mixed, tgrad, fc1_grad, fc2_grad, gain_grad = hand_over(*arrays)
    return mixed.reshape(out_grad.shape), tgrad, fc1_grad, fc2_grad, gain_grad


def solution(mesh):
    placed = (
        P("dp", "tensor", None),
        P(),
        P(None, "tensor"),
        P(None, "tensor"),
        P(),
        P("dp", "tensor", None),
    )
    return jax.shard_map(
        local,
        mesh=mesh,
        in_specs=placed,
        out_specs=(
            P("dp", "tensor", None),
            P("dp", "tensor", None),
            P("dp", "tensor"),
            P("dp", "tensor"),
            P(),
        ),
        check_vma=False,
    )
```

```python
import functools

import jax
import jax.numpy as jnp
from jax import lax
from jax.experimental import pallas as pl
from jax.experimental.pallas import tpu as pltpu
from jax.sharding import PartitionSpec as P

MESH = pl.DeviceIdType.MESH
ROW_DIMS = (((1,), (1,)), ((), ()))
RING = 4
RANKS = RING * RING
F32 = jnp.float32
BF16 = jnp.bfloat16

STEP = (0, -1, 1, 2)


def round_up(value, unit):
    return (value + unit - 1) // unit * unit


def chunk_of(width, limit):
    tiles = width // 128
    best = 1
    for count in range(1, tiles + 1):
        if tiles % count == 0 and count * 128 <= limit:
            best = count
    return best * 128


FOLD = 4


def fold_rows(rows):
    return round_up((rows + FOLD - 1) // FOLD, 16)


def fold_lanes(value):
    rows, units = value.shape
    step = fold_rows(rows)
    total = -(-rows // step)
    if total * step > rows:
        value = jnp.concatenate(
            [value, jnp.zeros((total * step - rows, units), value.dtype)], axis=0
        )
    cuts = [value[step * k : step * (k + 1)] for k in range(total)]
    if total * units < 128:
        cuts.append(jnp.zeros((step, 128 - total * units), value.dtype))
    return jnp.concatenate(cuts, axis=1)


def unfold_lanes(value, rows, units):
    step = value.shape[0]
    total = -(-rows // step)
    cuts = [value[:, units * k : units * (k + 1)] for k in range(total)]
    return jnp.concatenate(cuts, axis=0)[:rows]


class Sizes:
    def __init__(self, tokens, fc1, out_grad):
        self.homes, self.block_rows, self.width = tokens
        self.units = fc1[1]
        self.slots = out_grad[0]
        self.own = self.slots * self.block_rows
        self.pair = 2 * self.own
        self.rows = RING * self.pair
        self.owned = self.width // RANKS
        self.owned_pad = round_up(self.owned, 16)
        self.group = RING * self.owned
        self.group_step = self.group // 128 * 128
        self.group_pad = round_up(self.group + (RING - 1) * (self.group - self.group_step), 128)
        self.sum_rows = self.group_pad + 8
        self.chunk = chunk_of(self.width, 640)
        first = round_up(self.units // 2, 128) - 128
        self.parts = ((0, first), (first, self.units - first))
        mid = round_up(self.width // 2, 128)
        self.cuts = ((0, mid), (mid, self.width - mid))
        self.part_max = max(count for _, count in self.parts)


def kernel(
    sz,
    copies,
    slot_ref,
    gain_ref,
    tokens_hbm,
    fc1_hbm,
    fc2_hbm,
    grad_hbm,
    mixed,
    tgrad,
    fc1_out,
    fc2_out,
    gain_out,
    fc1_ref,
    fc2_ref,
    arrived,
    midway,
    midway_back,
    row_all,
    inv_ref,
    grad_all,
    norm_all,
    norm_cut,
    grad_sl,
    norm_sl,
    grad_t,
    norm_t,
    hid_g,
    pre_g,
    hid_n,
    pre_n,
    pre_act,
    hid_grad,
    row_sum,
    sib_out,
    sib_in,
    rs_out,
    rs_in,
    wg_sum,
    wg_out,
    wg_in,
    fold_out,
    fold_in,
    back_out,
    input_grad,
    gain_sib,
    gain_x,
    gain_y,
    gain_z,
    local_sems,
    send_sems,
    recv_sems,
):
    dp = lax.axis_index("dp")
    t = lax.axis_index("tensor")
    y, z = dp // RING, dp % RING
    x, c = t // 2, t % 2
    own, width = sz.own, sz.width
    half = own // 2
    gain = gain_ref[...].reshape(1, width)

    def on_dp(k):
        return ((dp + k + RANKS) % RANKS, t)

    def on_x(k):
        return (dp, ((x + k + RING) % RING) * 2 + c)

    def on_y(k):
        return (((y + k + RING) % RING) * RING + z, t)

    def on_z(k):
        return (y * RING + (z + k + RING) % RING, t)

    sibling = (dp, t + 1 - 2 * c)

    started = []

    class Guarded:
        def __init__(self, made, when, arrives):
            self.made, self.when, self.arrives = made, when, arrives

        def wait_recv(self):
            pl.when(self.arrives)(self.made.wait_recv)

        def wait_send(self):
            pl.when(self.when)(self.made.wait_send)

    def send(src, dst, device, when=None, arrives=None):
        index = len(started)
        made = pltpu.make_async_remote_copy(
            src_ref=src,
            dst_ref=dst,
            send_sem=send_sems.at[index],
            recv_sem=recv_sems.at[index],
            device_id=device,
            device_id_type=MESH,
        )
        if when is None:
            made.start()
        else:
            pl.when(when)(made.start)
            made = Guarded(made, when, when if arrives is None else arrives)
        started.append(made)
        return made

    my_rows = pl.ds(pl.multiple_of(c * own, own), own)
    load_grad = pltpu.make_async_copy(grad_hbm, grad_all.at[my_rows], local_sems.at[0])
    load_token = pltpu.make_async_copy(tokens_hbm.at[0], arrived.at[0], local_sems.at[1])
    load_fc2 = pltpu.make_async_copy(fc2_hbm, fc2_ref, local_sems.at[2])
    load_fc1 = pltpu.make_async_copy(fc1_hbm, fc1_ref, local_sems.at[3])
    load_grad.start()
    load_token.start()

    partners = [on_dp(k) for k in range(1, sz.homes)]
    partners += [on_dp(-k) for k in range(1, sz.homes)]
    partners += [on_y(k) for k in (1, -1, 2)]
    partners += [on_z(k) for k in (1, -1, 2)]
    partners += [on_x(k) for k in (1, -1, 2)]
    partners += [sibling]
    barrier = pltpu.get_barrier_semaphore()
    for device in partners:
        pl.semaphore_signal(barrier, inc=1, device_id=device, device_id_type=MESH)
    pl.semaphore_wait(barrier, len(partners))

    class RowGather:
        def __init__(self, view):
            self.view = view

        def part(self, slot, lo, count):
            place = sz.pair * slot + c * own + lo
            return self.view(pl.ds(pl.multiple_of(place, 16), count))

        def start(self):
            mine = self.part(0, 0, own)
            self.right = send(mine, self.part(1, 0, own), on_x(1))
            self.left = send(mine, self.part(2, 0, own), on_x(-1))
            self.shared = [send(mine, mine, sibling)]

        def forward(self):
            self.right.wait_recv()
            self.right2 = send(self.part(1, 0, half), self.part(3, 0, half), on_x(1))
            whole = self.part(1, 0, own)
            self.shared.append(send(whole, whole, sibling))
            self.left.wait_recv()
            rest = own - half
            self.left2 = send(self.part(2, half, rest), self.part(3, half, rest), on_x(-1))
            whole = self.part(2, 0, own)
            self.shared.append(send(whole, whole, sibling))

        def last(self):
            self.right2.wait_recv()
            low = self.part(3, 0, half)
            self.shared.append(send(low, low, sibling))
            self.left2.wait_recv()
            high = self.part(3, half, own - half)
            self.shared.append(send(high, high, sibling))

        def wait(self, first, stop):
            for made in self.shared[first:stop]:
                made.wait_recv()

    class RingGather:
        def __init__(self, buf, lo, count, on_axis, low):
            self.buf, self.on_axis = buf, on_axis
            self.whole = pl.ds(lo, count)
            self.low = pl.ds(lo, low)
            self.high = pl.ds(lo + low, count - low)

        def start(self):
            buf, on_axis = self.buf, self.on_axis
            mine = buf.at[0, self.whole]
            self.right = send(mine, buf.at[1, self.whole], on_axis(1))
            self.left = send(mine, buf.at[2, self.whole], on_axis(-1))

        def forward(self):
            buf, on_axis = self.buf, self.on_axis
            self.right.wait_recv()
            self.right2 = send(buf.at[1, self.low], buf.at[3, self.low], on_axis(1))
            self.left.wait_recv()
            self.left2 = send(buf.at[2, self.high], buf.at[3, self.high], on_axis(-1))

        def finish(self):
            self.right2.wait_recv()
            self.left2.wait_recv()

    class RingReduce:
        def __init__(self, part, out, into, on_axis, mid, count, folds=None):
            self.part, self.out, self.into = part, out, into
            self.on_axis, self.folds = on_axis, folds
            self.ranges = ((0, mid), (mid, count - mid))

        def put(self, slot, h, value):
            first, count = self.ranges[h]
            if self.folds is not None:
                main, fold_out, _ = self.folds
                folded = fold_lanes(value[:, main:])
                fold_out[slot, h, 0 : folded.shape[0]] = folded.astype(BF16)
                value = value[:, :main]
            self.out[slot, pl.ds(first, count)] = value.astype(BF16)

        def ship(self, slot, h, device):
            first, count = self.ranges[h]
            rows = pl.ds(first, count)
            made = [send(self.out.at[slot, rows], self.into.at[slot, rows], device)]
            if self.folds is not None:
                main, fold_out, fold_in = self.folds
                rows = pl.ds(0, fold_rows(count))
                made.append(send(fold_out.at[slot, h, rows], fold_in.at[slot, h, rows], device))
            return made

        def get(self, slot, h):
            first, count = self.ranges[h]
            value = self.into[slot, pl.ds(first, count)].astype(F32)
            if self.folds is not None:
                main, _, fold_in = self.folds
                folded = fold_in[slot, h, 0 : fold_rows(count)].astype(F32)
                units = self.units - main
                value = jnp.concatenate([value, unfold_lanes(folded, count, units)], axis=1)
            return value

        def own_part(self, k, h):
            value = self.part(k, *self.ranges[h])
            self.units = value.shape[1]
            return value

        def start(self):
            self.put(0, 0, self.own_part(3, 0))
            self.far_right = self.ship(0, 0, self.on_axis(1))
            self.put(0, 1, self.own_part(3, 1))
            self.far_left = self.ship(0, 1, self.on_axis(-1))
            self.put(1, 1, self.own_part(2, 1))
            self.rest = self.ship(1, 1, self.on_axis(1))
            self.put(2, 0, self.own_part(1, 0))
            self.rest += self.ship(2, 0, self.on_axis(-1))

        def forward(self):
            for made in self.far_right:
                made.wait_recv()
            self.put(1, 0, self.own_part(2, 0) + self.get(0, 0))
            self.rest += self.ship(1, 0, self.on_axis(1))
            for made in self.far_left:
                made.wait_recv()
            self.put(2, 1, self.own_part(1, 1) + self.get(0, 1))
            self.rest += self.ship(2, 1, self.on_axis(-1))

        def finish(self):
            for made in self.rest:
                made.wait_recv()

        def total(self, h):
            return self.own_part(0, h) + self.get(1, h) + self.get(2, h)

    class RowReduce:
        def __init__(self, index):
            self.index = index

        def multiply(self, lhs, weight, also=None):
            index = self.index

            @pl.loop(0, width // sz.chunk)
            def _(n):
                cols = pl.ds(pl.multiple_of(n * sz.chunk, sz.chunk), sz.chunk)
                full = jnp.dot(lhs[...], weight[:, cols], preferred_element_type=F32)
                for k in range(RING):
                    even = full[sz.pair * k : sz.pair * k + own]
                    odd = full[sz.pair * k + own : sz.pair * (k + 1)]
                    row_sum[index, k, :, cols] = jnp.where(c == 0, even, odd)
                    sib_out[index, k, :, cols] = jnp.where(c == 0, odd, even).astype(BF16)
                if also is not None:
                    also(cols, full)

            self.copy = send(sib_out.at[index], sib_in.at[index], sibling)

        def start(self):
            index = self.index
            self.copy.wait_recv()
            row_sum[index] = row_sum[index] + sib_in[index].astype(F32)

            def part(k, lo, count):
                return row_sum[index, k, lo : lo + count]

            self.ring = RingReduce(part, rs_out.at[index], rs_in.at[index], on_x, half, own)
            self.ring.start()

    class WeightGrad:
        def __init__(self, index, p, slices, blocks, on_axis, owner_row, out, mid):
            self.index, self.p, self.out, self.mid = index, p, out, mid
            self.slices, self.blocks = slices, blocks
            self.lo, self.units = sz.parts[p]
            self.on_axis, self.owner_row = on_axis, owner_row

        def multiply(self):
            index, p, lo, units = self.index, self.p, self.lo, self.units
            step = sz.group_pad // 2

            @pl.loop(0, 2)
            def _(m):
                rows = pl.ds(pl.multiple_of(m * step, step), step)
                total = None
                for k in range(RING):
                    one = lax.dot_general(
                        self.slices[k, rows, :],
                        self.blocks[k, lo : lo + units, :],
                        ROW_DIMS,
                        preferred_element_type=F32,
                    )
                    total = one if total is None else total + one
                wg_sum[index, p, rows, 0:units] = total

            wg_sum[index, p, sz.group_pad : sz.sum_rows, 0:units] = jnp.zeros((8, units), F32)

            def part(k, first, count):
                place = pl.multiple_of(self.owner_row(k) + first, 8)
                return wg_sum[index, p, pl.ds(place, count), 0:units]

            main = units // 128 * 128
            folds = None
            if main < units:
                folds = (main, fold_out.at[index], fold_in.at[index])
            self.ring = RingReduce(
                part,
                wg_out.at[index, p, :, :, pl.ds(0, main)],
                wg_in.at[index, p, :, :, pl.ds(0, main)],
                self.on_axis,
                self.mid,
                sz.owned_pad,
                folds,
            )
            self.ring.start()

        def finish(self):
            self.ring.finish()
            for h, (first, count) in enumerate(self.ring.ranges):
                count = min(count, sz.owned - first)
                cols = slice(self.lo, self.lo + self.units)
                self.out[first : first + count, cols] = self.ring.total(h)[:count]

    grad_rows = RowGather(lambda rows: grad_all.at[rows])
    cut_rows = RowGather(lambda rows: norm_sl.at[pl.ds(1, RING - 1), rows])
    (lo0, count0), (lo1, count1) = sz.cuts
    cols0, cols1 = pl.ds(lo0, count0), pl.ds(lo1, count1)
    via = []
    for j in range(1, RING):
        via.append(send(tokens_hbm.at[j, :, cols1], midway.at[j - 1], on_z(j)))
    direct = []
    for j in range(1, sz.homes):
        direct.append(send(tokens_hbm.at[j, :, cols0], arrived.at[j, :, cols0], on_dp(j)))
    last = []
    for j in range(RING, sz.homes):
        last.append(send(tokens_hbm.at[j, :, cols1], arrived.at[j, :, cols1], on_dp(j)))
    load_grad.wait()
    grad_rows.start()
    load_fc2.start()
    load_fc1.start()

    def pick(s, j):
        home = (dp - j + RANKS) % RANKS
        named = slot_ref[home * sz.homes + j]
        return jnp.where(named == dp * sz.slots + s, 1.0, 0.0).astype(F32)

    def group_columns(rows, q):
        cuts = []
        for k in range(RING):
            first = sz.owned * (RING * k + q)
            cuts.append(rows[:, first : first + sz.owned])
        cuts.append(jnp.zeros((rows.shape[0], sz.group_pad - sz.group), rows.dtype))
        return jnp.concatenate(cuts, axis=1)

    for j in range(1, RING):
        via[j - 1].wait_recv()
        last.append(
            send(midway.at[j - 1], arrived.at[j, :, cols1], on_y(1), when=z < j)
        )

        @pl.when(z >= j)
        def _():
            arrived[j, :, lo1:] = midway[j - 1]

    routed = (direct, last)
    load_token.wait()
    grad_rows.forward()
    row_parts = []
    for n, (lo, count) in enumerate(sz.cuts):
        cols = slice(lo, lo + count)
        for made in routed[n]:
            made.wait_recv()
        for s in range(sz.slots):
            total = pick(s, 0) * arrived[0, :, cols].astype(F32)
            for j in range(1, sz.homes):
                total += pick(s, j) * arrived[j, :, cols].astype(F32)
            place = c * own + s * sz.block_rows
            rows = pl.ds(pl.multiple_of(place, sz.block_rows), sz.block_rows)
            row_all[rows, cols] = total.astype(BF16)
        one = RowGather(lambda rows, lo=lo, count=count: row_all.at[rows, pl.ds(lo, count)])
        one.start()
        row_parts.append(one)
    row_parts[0].forward()
    grad_rows.last()

    def normed_rows(rows):
        value = row_all[rows, :].astype(F32)
        inv = lax.rsqrt(jnp.mean(value * value, axis=-1, keepdims=True) + 1e-06)
        return value * inv, inv

    def norm_shard(slot, core):
        @pl.loop(0, own // 16)
        def _(n):
            place = sz.pair * slot + core * own + n * 16
            rows = pl.ds(pl.multiple_of(place, 16), 16)
            unit, _ = normed_rows(rows)
            norm_all[rows, :] = (unit * gain).astype(BF16)

    unit_own, inv = normed_rows(my_rows)
    inv_ref[...] = jnp.broadcast_to(inv, inv_ref.shape)
    norm_own = (unit_own * gain).astype(BF16)
    norm_all[my_rows, :] = norm_own
    for q in range(RING):
        norm_cut[q] = group_columns(norm_own, q)
    cut_sent = []
    for k, slot in ((1, 1), (-1, 2), (2, 3)):
        cut_sent.append(
            send(norm_cut.at[(z + k + RING) % RING], norm_sl.at[slot, my_rows], on_z(k))
        )
    row_parts[1].forward()
    grad_rows.wait(0, 5)
    side = sz.rows // 2
    side_rows = pl.ds(pl.multiple_of(c * side, side), side)
    slice_sent = []
    for k, slot in ((1, 1), (-1, 2), (2, 3)):
        first = pl.multiple_of(((y + k + RING) % RING) * sz.group_step, 128)
        slice_sent.append(
            send(
                grad_all.at[side_rows, pl.ds(first, sz.group_pad)],
                grad_sl.at[slot, side_rows],
                on_y(k),
            )
        )
    row_parts[0].last()

    load_fc2.wait()

    def multiply_in(lhs, lo, count, rows, out):
        out[lo : lo + count, :] = lax.dot_general(
            lhs[lo : lo + count, :], rows[...], ROW_DIMS, preferred_element_type=F32
        )

    multiply_in(fc2_ref, *sz.parts[0], grad_all, hid_grad)
    for slot in (1, 2):
        norm_shard(slot, c)
    row_parts[1].last()
    for slot in range(3):
        for one in row_parts:
            one.wait(slot, slot + 1)
        norm_shard(slot, 1 - c)
    norm_shard(3, c)
    for made in cut_sent:
        made.wait_recv()
    for one in row_parts:
        one.wait(3, 5)
    norm_shard(3, 1 - c)
    cut_rows.start()
    load_fc1.wait()

    hid_ring, pre_ring = [], []
    for lo, count in sz.parts:
        if lo > 0:
            multiply_in(fc2_ref, lo, count, grad_all, hid_grad)
        multiply_in(fc1_ref, lo, count, norm_all, pre_act)

        @pl.loop(0, count // 32)
        def _(n):
            rows = pl.ds(pl.multiple_of(lo + n * 32, 32), 32)
            value = pre_act[rows, :]
            cdf = 0.5 * (1.0 + lax.erf(value * 0.7071067811865476))
            slope = cdf + value * jnp.exp(-0.5 * value * value) * 0.3989422804014327
            hid_g[0, rows, :] = (value * cdf).astype(BF16)
            pre_g[0, rows, :] = (hid_grad[rows, :] * slope).astype(BF16)

        hid_ring.append(RingGather(hid_g, lo, count, on_y, count * 2 // 3 // 16 * 16))
        pre_ring.append(RingGather(pre_g, lo, count, on_z, count // 2 // 16 * 16))
        hid_ring[-1].start()
        pre_ring[-1].start()

    back = RowReduce(1)
    branch = RowReduce(0)

    def gain_part(cols, full):
        product = full * norm_all[:, cols].astype(F32)
        gain_sib[0, :, cols] = jnp.sum(product, axis=0, keepdims=True)

    pre_n[...] = pre_g[0].T
    back.multiply(pre_n, fc1_ref, gain_part)
    gain_pair = send(gain_sib.at[0], gain_sib.at[1], sibling)
    hid_ring[0].forward()
    pre_ring[0].forward()
    cut_rows.forward()
    slice_shared = []
    for slot, made in zip((1, 2, 3), slice_sent):
        made.wait_recv()
        place = grad_sl.at[slot, side_rows]
        slice_shared.append(send(place, place, sibling))
    hid_n[...] = hid_g[0].T
    branch.multiply(hid_n, fc2_ref)
    back.start()
    hid_ring[1].forward()
    pre_ring[1].forward()
    cut_rows.last()
    own_first = pl.multiple_of(y * sz.group_step, 128)
    grad_t[0] = grad_all[:, pl.ds(own_first, sz.group_pad)].T
    for made in slice_shared:
        made.wait_recv()
    for k in range(1, RING):
        grad_t[k] = grad_sl[k].T

    def add_start(buf, me, on_axis, total):
        buf[me] = total
        return [send(buf.at[me], buf.at[me], on_axis(k)) for k in (1, -1, 2)]

    def add_finish(buf, made):
        for one in made:
            one.wait_recv()
        return buf[0] + buf[1] + buf[2] + buf[3]

    def fc2_row(k):
        return y * (sz.group - sz.group_step) + ((z + STEP[k] + RING) % RING) * sz.owned

    def fc1_row(k):
        return ((y + STEP[k] + RING) % RING) * sz.owned

    even = round_up(sz.owned_pad // 2, 16)
    more = round_up(sz.owned_pad * 2 // 3, 16)
    fc2_grad = [
        WeightGrad(0, p, grad_t, hid_g, on_z, fc2_row, fc2_out, even) for p in range(2)
    ]
    fc1_grad = [
        WeightGrad(1, p, norm_t, pre_g, on_y, fc1_row, fc1_out, more) for p in range(2)
    ]
    hid_ring[0].finish()
    fc2_grad[0].multiply()
    back.ring.forward()
    gain_pair.wait_recv()
    adding = add_start(gain_x, x, on_x, gain_sib[0] + gain_sib[1])
    cut_rows.wait(0, 5)
    for q in range(RING):

        @pl.when(z == q)
        def _():
            norm_t[0] = group_columns(norm_all[...], q).T

    for k in range(1, RING):
        norm_t[k] = norm_sl[k].T
    pre_ring[0].finish()
    fc1_grad[0].multiply()
    hid_ring[1].finish()
    fc2_grad[1].multiply()
    pre_ring[1].finish()
    fc1_grad[1].multiply()
    fc2_grad[0].ring.forward()
    fc1_grad[0].ring.forward()
    branch.start()
    total = add_finish(gain_x, adding)
    adding = add_start(gain_y, y, on_y, total)
    back.ring.finish()

    normed_grad = jnp.concatenate([back.ring.total(0), back.ring.total(1)], axis=0)
    unit = row_all[my_rows, :].astype(F32) * inv_ref[:, :1]
    scaled = normed_grad * gain
    inner = scaled - unit * jnp.mean(scaled * unit, axis=-1, keepdims=True)
    input_grad[...] = (
        (grad_all[my_rows, :].astype(F32) + inv_ref[:, :1] * inner).astype(BF16).astype(F32)
    )
    returned, via = [], []
    for j in range(sz.homes):
        total = pick(0, j) * input_grad[0 : sz.block_rows, :]
        for s in range(1, sz.slots):
            total += pick(s, j) * input_grad[s * sz.block_rows : (s + 1) * sz.block_rows, :]
        total = total.astype(BF16)
        if j == 0:
            tgrad[0] = total
            continue
        back_out[j - 1] = total
        if j < RING:
            source = back_out.at[j - 1, :, cols1]
            via.append(send(source, midway_back.at[j - 1], on_z(-j)))
    for j in range(1, sz.homes):
        source, place = back_out.at[j - 1], tgrad.at[j]
        if j < RING:
            source, place = source.at[:, cols0], place.at[:, cols0]
        returned.append(send(source, place, on_dp(-j)))
    fc2_grad[1].ring.forward()
    fc1_grad[1].ring.forward()
    total = add_finish(gain_y, adding)
    adding = add_start(gain_z, z, on_z, total)
    for j in range(1, RING):
        via[j - 1].wait_recv()
        returned.append(
            send(midway_back.at[j - 1], tgrad.at[j, :, cols1], on_y(-1), when=z + j >= RING)
        )

        @pl.when(z + j < RING)
        def _():
            tgrad[j, :, lo1:] = midway_back[j - 1]

    branch.ring.forward()
    branch.ring.finish()
    branch_sum = jnp.concatenate([branch.ring.total(0), branch.ring.total(1)], axis=0)
    mixed[...] = (row_all[my_rows, :].astype(F32) + branch_sum).astype(BF16)
    fc2_grad[0].finish()
    fc1_grad[0].finish()
    total = add_finish(gain_z, adding)
    gain_out[...] = (total / gain).reshape(width)
    for made in returned:
        made.wait_recv()
    fc2_grad[-1].finish()
    fc1_grad[-1].finish()
    for made in started:
        made.wait_send()
    if len(started) != copies:
        raise ValueError(len(started))


def hand_over_kernel(*refs):
    count = len(refs) // 2
    sems = refs[-1]
    made = [
        pltpu.make_async_copy(refs[i], refs[count + i], sems.at[i]) for i in range(count)
    ]
    for one in made:
        one.start()
    for one in made:
        one.wait()


def hand_over(*arrays):
    vmem = pl.BlockSpec(memory_space=pltpu.VMEM)
    anywhere = pl.BlockSpec(memory_space=pl.ANY)
    return pl.pallas_call(
        hand_over_kernel,
        out_shape=tuple(jax.ShapeDtypeStruct(a.shape, a.dtype) for a in arrays),
        in_specs=[vmem] * len(arrays),
        out_specs=(anywhere,) * len(arrays),
        scratch_shapes=[pltpu.SemaphoreType.DMA((len(arrays),))],
        compiler_params=pltpu.CompilerParams(vmem_limit_bytes=1024 * 1024),
        name="hand_over",
    )(*arrays)


COPIES = 142


def local(tokens, norm_gain, fc1, fc2t, block_slot, out_grad):
    sz = Sizes(tokens.shape, fc1.shape, out_grad.shape)
    width, units = sz.width, sz.units
    vmem = pl.BlockSpec(memory_space=pltpu.VMEM)
    anywhere = pl.BlockSpec(memory_space=pl.ANY)
    slices = (RING, sz.rows, sz.group_pad)
    slices_t = (RING, sz.group_pad, sz.rows)
    pieces = (2, 2, 3, sz.owned_pad, sz.part_max // 128 * 128)
    folds = (2, 3, 2, fold_rows(sz.owned_pad), 128)
    arrays = pl.pallas_call(
        functools.partial(kernel, sz, COPIES),
        out_shape=(
            pltpu.VMEM((sz.own, width), BF16),
            pltpu.VMEM(tokens.shape, BF16),
            pltpu.VMEM((sz.owned, units), F32),
            pltpu.VMEM((sz.owned, units), F32),
            pltpu.VMEM((width,), F32),
        ),
        in_specs=[
            pl.BlockSpec(memory_space=pltpu.SMEM),
            vmem,
            anywhere,
            anywhere,
            anywhere,
            anywhere,
        ],
        out_specs=(vmem,) * 5,
        scratch_shapes=[
            pltpu.VMEM((units, width), BF16),
            pltpu.VMEM((units, width), BF16),
            pltpu.VMEM(tokens.shape, BF16),
            pltpu.VMEM((RING - 1, sz.block_rows, sz.cuts[1][1]), BF16),
            pltpu.VMEM((RING - 1, sz.block_rows, sz.cuts[1][1]), BF16),
            pltpu.VMEM((sz.rows, width), BF16),
            pltpu.VMEM((sz.own, 128), F32),
            pltpu.VMEM((sz.rows, width), BF16),
            pltpu.VMEM((sz.rows, width), BF16),
            pltpu.VMEM((RING, sz.own, sz.group_pad), BF16),
            pltpu.VMEM(slices, BF16),
            pltpu.VMEM(slices, BF16),
            pltpu.VMEM(slices_t, BF16),
            pltpu.VMEM(slices_t, BF16),
            pltpu.VMEM((RING, units, sz.rows), BF16),
            pltpu.VMEM((RING, units, sz.rows), BF16),
            pltpu.VMEM((sz.rows, units), BF16),
            pltpu.VMEM((sz.rows, units), BF16),
            pltpu.VMEM((units, sz.rows), F32),
            pltpu.VMEM((units, sz.rows), F32),
            pltpu.VMEM((2, RING, sz.own, width), F32),
            pltpu.VMEM((2, RING, sz.own, width), BF16),
            pltpu.VMEM((2, RING, sz.own, width), BF16),
            pltpu.VMEM((2, 3, sz.own, width), BF16),
            pltpu.VMEM((2, 3, sz.own, width), BF16),
            pltpu.VMEM((2, 2, sz.sum_rows, sz.part_max), F32),
            pltpu.VMEM(pieces, BF16),
            pltpu.VMEM(pieces, BF16),
            pltpu.VMEM(folds, BF16),
            pltpu.VMEM(folds, BF16),
            pltpu.VMEM((sz.homes - 1, sz.block_rows, width), BF16),
            pltpu.VMEM((sz.own, width), F32),
            pltpu.VMEM((2, 1, width), F32),
            pltpu.VMEM((RING, 1, width), F32),
            pltpu.VMEM((RING, 1, width), F32),
            pltpu.VMEM((RING, 1, width), F32),
            pltpu.SemaphoreType.DMA((4,)),
            pltpu.SemaphoreType.DMA((COPIES,)),
            pltpu.SemaphoreType.DMA((COPIES,)),
        ],
        compiler_params=pltpu.CompilerParams(
            collective_id=0, has_side_effects=True, vmem_limit_bytes=60 * 1024 * 1024
        ),
        cost_estimate=pl.CostEstimate(
            flops=12 * sz.rows * width * units,
            bytes_accessed=4 * width * units,
            transcendentals=2 * sz.rows * units,
        ),
        name="mlp_block",
    )(
        block_slot,
        norm_gain,
        tokens,
        fc1.T,
        fc2t.T,
        out_grad.reshape(sz.own, width),
    )
    mixed, tgrad, fc1_grad, fc2_grad, gain_grad = hand_over(*arrays)
    return mixed.reshape(out_grad.shape), tgrad, fc1_grad, fc2_grad, gain_grad


def solution(mesh):
    placed = (
        P("dp", "tensor", None),
        P(),
        P(None, "tensor"),
        P(None, "tensor"),
        P(),
        P("dp", "tensor", None),
    )
    return jax.shard_map(
        local,
        mesh=mesh,
        in_specs=placed,
        out_specs=(
            P("dp", "tensor", None),
            P("dp", "tensor", None),
            P("dp", "tensor"),
            P("dp", "tensor"),
            P(),
        ),
        check_vma=False,
    )
```
